1024 devices in a mesh: grid: 64 (over y_lo, z, core), band: 16 (over x, y_hi).
Axes of the slice: x: 8, y: 8 (y_hi: 2, y_lo: 4; y = y_hi * 4 + y_lo), z: 8, core: 2. Of those that a mesh axis runs over, the one named last changes fastest.
Arguments:
- orbitals: float32 [64, 256, 6400], P('band', 'grid'), may hold values from -6 to 6
- potential: float32 [256, 6400], P('grid'), may hold values from -6 to 6
- projectors: float32 [3, 2, 8, 256, 6400], P(None, None, None, 'grid'), may hold values from -0.18 to 0.18
- kb_energy: float32 [64, 2, 8], P('grid'), may hold values from 0.3 to 3
- proj_count: int32 [64, 2], P('grid'), may hold values from 0 to 8, as said below
Outputs:
- hpsi: float32 [64, 256, 6400], P('band', 'grid')
- correlation: float32 [64, 64], P('band')
- projected: float32 [64, 64], P('band')
The draws below stay inside these ranges and needn't reach their ends.
Inputs may be any that keep to these rules, and one draw needn't show every extreme that they name: `proj_count`: in each domain the live atom slots come first, 1 of them or more; live slots have 1 to 8 active projectors; some domain has all 2 slots live and some atom has all 8 projectors.
All inputs are finite; a program needn't handle non-finite values.
Results may differ from the reference program's by a relative error of at most 0.00005.
Values sent between devices are 32-bit elements; how exact they have to be, the bound alone decides.
A program may use at most 64 MiB of HBM per device.

```python
import math
import jax
import jax.numpy as jnp
from jax import lax

BAND_DEV = 4
CZ = 4
NY = 80
ATOMS = 2
PROJ = 8
NXY = 6400
NZ = 256
BANDS = 64
N_GRID = 64
N_BAND = 16


def draw_proj_count(key, part):
    key = jax.random.fold_in(key, 11)
    key_count, key_full, key_kinds, key_atom = jax.random.split(key, 4)
    domain_ids = jnp.arange(N_GRID, dtype=jnp.int32)
    slot_ids = jnp.arange(ATOMS, dtype=jnp.int32)
    live_counts = jax.random.randint(key_count, (N_GRID,), ATOMS // 2, ATOMS + 1)
    full_domain = jax.random.randint(key_full, (), 0, N_GRID)
    live_counts = jnp.where(domain_ids == full_domain, ATOMS, live_counts)
    kinds_drawn = jax.random.randint(key_kinds, (N_GRID, ATOMS), 1, PROJ + 1)
    kinds_drawn = jnp.where(slot_ids[None, :] < live_counts[:, None], kinds_drawn, 0)
    rich_domain = jax.random.randint(key_atom, (), 0, N_GRID)
    kinds_drawn = jnp.where((domain_ids[:, None] == rich_domain) & (slot_ids[None, :] == 0), PROJ, kinds_drawn)
    return kinds_drawn.astype(jnp.int32)


def levels(key, shape, cuts, smallest, high):
    factor_of = 1.0
    for dim, parts in cuts:
        heights = jax.random.uniform(jax.random.fold_in(jax.random.fold_in(key, 6), dim), (parts,), jnp.float32, smallest / len(cuts), high / len(cuts))
        factor_of = factor_of * jnp.repeat(jnp.exp(heights), shape[dim] // parts).reshape((-1,) + (1,) * (len(shape) - 1 - dim))
    return factor_of


def noise(stream_key, shape, width, bound, shards=(), kind=jnp.bfloat16):
    array = width * jax.random.normal(stream_key, shape, jnp.float32)
    if shards:
        array = array * levels(stream_key, shape, shards, -0.22, 0.18)
    return jnp.clip(array, -bound, bound).astype(kind)


def setup_inputs(seed: int = 0) -> dict:
    keys = jax.random.split(jax.random.key(seed), 6)
    return {
        "orbitals": noise(keys[0], (BANDS, NZ, NXY), 1.0, 6.0, ((0, 16), (1, 64)), jnp.float32),
        "potential": noise(keys[1], (NZ, NXY), 1.0, 6.0, ((0, 64),), jnp.float32),
        "projectors": noise(keys[2], (3, ATOMS, PROJ, NZ, NXY), 0.03, 0.18, ((3, 64),), jnp.float32),
        "kb_energy": jnp.clip(jnp.exp(math.log(3.0) - 2.3025851 * jax.random.uniform(keys[3], (N_GRID, ATOMS, PROJ), jnp.float32) ** levels(keys[3], (N_GRID, ATOMS, PROJ), ((0, 64),), -0.2, 0.2)), 0.3, 3.0),
        "proj_count": draw_proj_count(jax.random.fold_in(keys[5], 71), 0),
    }


STENCIL = (-205.0 / 72.0, 8.0 / 5.0, -1.0 / 5.0, 8.0 / 315.0, -1.0 / 560.0)


def laplace(orbital_field, padded, row_width):
    layers = orbital_field.shape[1]
    cell_count = orbital_field.shape[2]
    column = lax.broadcasted_iota(jnp.int32, (cell_count,), 0) % row_width
    far_pad = jnp.pad(orbital_field, ((0, 0), (0, 0), (4 * row_width, 4 * row_width)))
    near_pad = jnp.pad(orbital_field, ((0, 0), (0, 0), (4, 4)))
    result = 3.0 * STENCIL[0] * orbital_field
    for offset in range(1, 5):
        above_z = padded[:, 4 + offset:4 + offset + layers]
        below_z = padded[:, 4 - offset:4 - offset + layers]
        upper_x = far_pad[:, :, (4 + offset) * row_width:(4 + offset) * row_width + cell_count]
        lower_x = far_pad[:, :, (4 - offset) * row_width:(4 - offset) * row_width + cell_count]
        right_y = jnp.where(column + offset < row_width, near_pad[:, :, 4 + offset:4 + offset + cell_count], 0.0)
        left_y = jnp.where(column >= offset, near_pad[:, :, 4 - offset:4 - offset + cell_count], 0.0)
        result = result + STENCIL[offset] * (above_z + below_z + upper_x + lower_x + right_y + left_y)
    return result


def reference(orbitals, potential, projectors, kb_energy, proj_count):
    domain_cells = CZ * NXY
    proj_table = projectors.reshape(3, ATOMS * PROJ, N_GRID, domain_cells)
    active = (lax.broadcasted_iota(jnp.int32, (N_GRID, ATOMS, PROJ), 2) < proj_count[:, :, None]).astype(jnp.float32)
    weight = (kb_energy * active).reshape(N_GRID, ATOMS * PROJ)

    def apply_group(band_group):
        padded = jnp.concatenate([band_group[:, -4:], band_group, band_group[:, :4]], axis=1)
        kinetic = -0.5 * laplace(band_group, padded, NY)
        local_term = potential[None] * band_group
        flat_group = band_group.reshape(BAND_DEV, N_GRID, domain_cells)
        partial_value = jnp.einsum('kpdc,bdc->kdpb', proj_table, flat_group, precision=lax.Precision.HIGHEST)
        owner_total = partial_value[1] + jnp.roll(partial_value[0], -1, axis=0) + jnp.roll(partial_value[2], 1, axis=0)
        coef = owner_total * weight[:, :, None]
        neighbours = jnp.stack([jnp.roll(coef, 1, axis=0), coef, jnp.roll(coef, -1, axis=0)])
        nonlocal_term = jnp.einsum('kpdc,kdpb->bdc', proj_table, neighbours, precision=lax.Precision.HIGHEST)
        return kinetic + local_term + nonlocal_term.reshape(BAND_DEV, NZ, NXY)

    grouped = orbitals.reshape(N_BAND, BAND_DEV, NZ, NXY)
    hpsi = lax.map(apply_group, grouped).reshape(BANDS, NZ, NXY)
    flat_all = orbitals.reshape(BANDS, NZ * NXY)
    hflat = hpsi.reshape(BANDS, NZ * NXY)
    volume = 1.0 / (NZ * NXY)
    correlation = jnp.dot(flat_all, flat_all.T, preferred_element_type=jnp.float32, precision=lax.Precision.HIGHEST) * volume
    projected = jnp.dot(hflat, flat_all.T, preferred_element_type=jnp.float32, precision=lax.Precision.HIGHEST) * volume
    return hpsi, correlation, projected
```

```python
import functools

import jax
import jax.numpy as jnp
from jax import lax
from jax.experimental import pallas as pl
from jax.experimental.pallas import tpu as pltpu
from jax.sharding import PartitionSpec as P

NY = 80
STENCIL = (-205.0 / 72.0, 8.0 / 5.0, -1.0 / 5.0, 8.0 / 315.0, -1.0 / 560.0)
MESH = pl.DeviceIdType.MESH
LANES = 128
PAD = 384
CHUNK = 640
WIDE = 1280


def iota(rows, cols):
    return (
        lax.broadcasted_iota(jnp.int32, (rows, cols), 0),
        lax.broadcasted_iota(jnp.int32, (rows, cols), 1),
    )


def ones_where(condition):
    return jnp.where(condition, 1.0, 0.0).astype(jnp.float32)


def dot(a, b, dims):
    return lax.dot_general(
        a,
        b,
        (dims, ((), ())),
        precision=lax.Precision.HIGHEST,
        preferred_element_type=jnp.float32,
    )


NN = ((1,), (0,))
NT = ((1,), (1,))
TN = ((0,), (0,))


def z_matrix():
    row, col = iota(16, 48)
    same = ((row >> 2) & 3) == ((col >> 2) & 3)
    diff = (col >> 4) * 4 + (col & 3) - 4 - (row & 3)
    dist = jnp.abs(diff)
    value = jnp.zeros((16, 48), jnp.float32)
    for k in range(1, 5):
        value = jnp.where(dist == k, -0.5 * STENCIL[k], value)
    return jnp.where(same, value, 0.0)


def kernel(
    dims,
    psi_in,
    pot_in,
    table_in,
    weight_in,
    h_out,
    corr_out,
    gram_out,
    psi,
    before,
    after,
    pot,
    table,
    h,
    got_psi,
    got_h,
    ycoef,
    part,
    low1,
    high1,
    low2,
    high2,
    terms,
    band_terms,
    own_sum,
    pair_terms,
    pair_sum,
    line_terms,
    in_sem,
    table_sem,
    halo_send,
    halo_recv,
    part_send,
    part_recv,
    psi_send,
    psi_recv,
    h_send,
    h_recv,
    extra_send,
    extra_recv,
    out_sem,
    a_send,
    a_recv,
    b_send,
    b_recv,
    c_send,
    c_recv,
):
    nx, ny, nz = dims
    nb, ng = nx * 2, ny * nz * 2
    cells = pot_in.shape[1]
    per = (cells // LANES) // nb
    share = per * LANES
    me_g = lax.axis_index("grid")
    me_b = lax.axis_index("band")
    my_x, my_h = me_b // 2, me_b % 2
    my_c, my_z, my_y = me_g % 2, (me_g // 2) % nz, me_g // (2 * nz)

    extras = [(per * nb + i, (0, nx + 1)[i]) for i in range(cells // LANES - per * nb)]
    band_offsets = [(dx, dh) for dh in (1, 0) for dx in range(nx) if (dx, dh) != (0, 0)]
    pair_offsets = [(dy, dc) for dy in range(ny) for dc in range(2) if (dy, dc) != (0, 0)]

    def band_peer(dx, dh):
        return ((my_x + dx) % nx) * 2 + (my_h + dh) % 2

    def pair_peer(dy, dc):
        return (((my_y + dy) % ny) * nz + my_z) * 2 + (my_c + dc) % 2

    def line_peer(dz):
        return (my_y * nz + (my_z + dz) % nz) * 2 + my_c

    def grid_peer(step):
        return (me_g + step + ng) % ng

    loads = [
        pltpu.make_async_copy(
            psi_in.at[b], psi.at[pl.ds(4 * b, 4), pl.ds(PAD, cells)], in_sem.at[b]
        )
        for b in range(4)
    ]
    pot_loads = [
        pltpu.make_async_copy(pot_in, pot.at[pl.ds(4 * b, 4), :], in_sem.at[4 + b])
        for b in range(2)
    ]
    for copy in loads:
        copy.start()
    for copy in pot_loads:
        copy.start()

    def table_copy(i):
        return pltpu.make_async_copy(
            table_in.at[i], table.at[pl.ds(pl.multiple_of(4 * i, 4), 4), :], table_sem.at[i]
        )

    @pl.loop(0, 48)
    def _(i):
        table_copy(i).start()

    psi[:, 0:PAD] = jnp.zeros((16, PAD), jnp.float32)
    psi[:, PAD + cells : PAD + cells + PAD] = jnp.zeros((16, PAD), jnp.float32)
    got_psi[:, share : share + LANES] = jnp.zeros((16 * nb, LANES), jnp.float32)
    got_h[:, share : share + LANES] = jnp.zeros((16 * nb, LANES), jnp.float32)

    barrier = pltpu.get_barrier_semaphore()
    peers = 0
    for dx, dh in band_offsets:
        pl.semaphore_signal(
            barrier, inc=1, device_id=(me_g, band_peer(dx, dh)), device_id_type=MESH
        )
        peers += 1
    for step in (1, -1, 2, -2):
        pl.semaphore_signal(
            barrier, inc=1, device_id=(grid_peer(step), me_b), device_id_type=MESH
        )
        peers += 1
    for dy, dc in pair_offsets:
        pl.semaphore_signal(
            barrier, inc=1, device_id=(pair_peer(dy, dc), me_b), device_id_type=MESH
        )
        peers += 1
    for dz in range(1, nz):
        pl.semaphore_signal(
            barrier, inc=1, device_id=(line_peer(dz), me_b), device_id_type=MESH
        )
        peers += 1

    _, lane = iota(8, CHUNK)
    turn = jnp.zeros((8, CHUNK), jnp.int32)
    for m in range(1, CHUNK // NY):
        turn = turn + jnp.where(lane >= m * NY, 1, 0)
    column = lane - turn * NY
    for k in range(1, 5):
        ycoef[k - 1] = jnp.where(column + k < NY, -0.5 * STENCIL[k], 0.0)
        ycoef[3 + k] = jnp.where(column >= k, -0.5 * STENCIL[k], 0.0)

    for copy in loads:
        copy.wait()
    pl.semaphore_wait(barrier, peers)

    halo = []
    for i, (step, target) in enumerate(((1, before), (-1, after))):
        copy = pltpu.make_async_remote_copy(
            src_ref=psi.at[:, pl.ds(PAD, cells)],
            dst_ref=target,
            send_sem=halo_send.at[i],
            recv_sem=halo_recv.at[i],
            device_id=(grid_peer(step), me_b),
            device_id_type=MESH,
        )
        copy.start()
        halo.append(copy)

    my_rows = pl.ds(pl.multiple_of(me_b * 16, 16), 16)

    def spread(source, base, target, send, recv, which):
        copies = []
        for i, (dx, dh) in enumerate(band_offsets):
            peer = band_peer(dx, dh)
            start = pl.multiple_of(base + peer * share, LANES)
            copy = pltpu.make_async_remote_copy(
                src_ref=source.at[:, pl.ds(start, share)],
                dst_ref=target.at[my_rows, pl.ds(0, share)],
                send_sem=send.at[i],
                recv_sem=recv.at[i],
                device_id=(me_g, peer),
                device_id_type=MESH,
            )
            copy.start()
            copies.append(copy)
        for i, (tile, owner) in enumerate(extras):

            @pl.when(me_b != owner)
            def _(i=i, tile=tile, owner=owner):
                extra_copy(source, base, target, which, i, tile, owner, me_b).start()

        return copies

    def extra_copy(source, base, target, which, i, tile, owner, sem):
        return pltpu.make_async_remote_copy(
            src_ref=source.at[:, pl.ds(base + tile * LANES, LANES)],
            dst_ref=target.at[my_rows, pl.ds(share, LANES)],
            send_sem=extra_send.at[which * 2 + i],
            recv_sem=extra_recv.at[which * 16 + sem],
            device_id=(me_g, owner),
            device_id_type=MESH,
        )

    def keep_own(source, base, target):
        start = pl.multiple_of(base + me_b * share, LANES)
        target[my_rows, 0:share] = source[:, pl.ds(start, share)]
        for tile, owner in extras:

            @pl.when(me_b == owner)
            def _(tile=tile):
                target[my_rows, share : share + LANES] = source[
                    :, base + tile * LANES : base + (tile + 1) * LANES
                ]

    def await_spread(copies, source, base, target, which):
        for copy in copies:
            copy.wait_recv()
        for i, (tile, owner) in enumerate(extras):

            @pl.when(me_b == owner)
            def _(i=i, tile=tile, owner=owner):
                for other in range(nb):
                    if other != owner:
                        extra_copy(
                            source, base, target, which, i, tile, owner, other
                        ).wait_recv()

    def await_sent(copies, source, base, target, which):
        for copy in copies:
            copy.wait_send()
        for i, (tile, owner) in enumerate(extras):

            @pl.when(me_b != owner)
            def _(i=i, tile=tile, owner=owner):
                extra_copy(source, base, target, which, i, tile, owner, me_b).wait_send()

    psi_copies = spread(psi, PAD, got_psi, psi_send, psi_recv, 0)

    @pl.loop(0, 48)
    def _(i):
        table_copy(i).wait()

    def partial_step(i, total):
        start = pl.multiple_of(i * WIDE, LANES)
        return total + dot(
            table[:, pl.ds(start, WIDE)], psi[:, pl.ds(start + PAD, WIDE)], NT
        )

    raw = lax.fori_loop(0, cells // WIDE, partial_step, jnp.zeros((192, 16), jnp.float32))
    row, col = iota(192, 16)
    raw = jnp.where((row & 3) == (col & 3), raw, 0.0)
    row, col = iota(64, 192)
    source_row = jnp.where(row < 32, row, jnp.where(row < 48, -1, row - 16))
    gather = ones_where(source_row == (col >> 2))
    row, col = iota(16, LANES)
    widen = ones_where((row >> 2) == (col >> 2))
    sums = dot(dot(gather, raw, NN), widen, NN)
    part[...] = sums
    part[32:48, :] = weight_in[...]

    part_copies = []
    for i, (step, first, count, target) in enumerate(
        ((1, 16, 48, low1), (-1, 0, 48, high1), (2, 48, 16, low2), (-2, 0, 16, high2))
    ):
        copy = pltpu.make_async_remote_copy(
            src_ref=part.at[pl.ds(first, count), :],
            dst_ref=target,
            send_sem=part_send.at[i],
            recv_sem=part_recv.at[i],
            device_id=(grid_peer(step), me_b),
            device_id_type=MESH,
        )
        copy.start()
        part_copies.append(copy)

    for copy in pot_loads:
        copy.wait()

    @pl.loop(0, cells // CHUNK)
    def _(i):
        start = pl.multiple_of(i * CHUNK, LANES)
        wide = psi[:, pl.ds(start, CHUNK + 2 * PAD)]

        def shifted(offset):
            return wide[:, PAD + offset : PAD + offset + CHUNK]

        here = pot[:, pl.ds(start, CHUNK)] + (-1.5 * STENCIL[0])
        total = jnp.concatenate([here, here], axis=0) * shifted(0)
        for k in range(1, 5):
            total = total + (-0.5 * STENCIL[k]) * (shifted(NY * k) + shifted(-NY * k))
            up, down = ycoef[k - 1], ycoef[3 + k]
            total = total + jnp.concatenate([up, up], axis=0) * shifted(k)
            total = total + jnp.concatenate([down, down], axis=0) * shifted(-k)
        h[:, pl.ds(start, CHUNK)] = total

    keep_own(psi, PAD, got_psi)

    for copy in halo:
        copy.wait_recv()
    across = z_matrix()

    @pl.loop(0, cells // WIDE)
    def _(i):
        start = pl.multiple_of(i * WIDE, LANES)
        here = pl.ds(start, WIDE)
        planes = jnp.concatenate(
            [before[:, here], psi[:, pl.ds(start + PAD, WIDE)], after[:, here]], axis=0
        )
        h[:, here] = h[:, here] + dot(across, planes, NN)

    for copy in part_copies:
        copy.wait_recv()
    coef = jnp.concatenate(
        [
            low1[16:32, :] * (low1[0:16, :] + part[0:16, :] + low2[...]),
            part[32:48, :] * (part[16:32, :] + high1[0:16, :] + low1[32:48, :]),
            high1[32:48, :] * (high1[16:32, :] + high2[...] + part[48:64, :]),
        ],
        axis=0,
    )
    row, col = iota(48, 192)
    repeat = ones_where(row == (col >> 2))
    spread_coef = dot(coef, repeat, TN)[0:16, :]
    row, col = iota(16, 192)
    spread_coef = jnp.where((row & 3) == (col & 3), spread_coef, 0.0)

    @pl.loop(0, cells // WIDE)
    def _(i):
        start = pl.multiple_of(i * WIDE, LANES)
        here = pl.ds(start, WIDE)
        h[:, here] = h[:, here] + dot(spread_coef, table[:, here], NN)

    h_copies = spread(h, 0, got_h, h_send, h_recv, 1)
    stores = [
        pltpu.make_async_copy(h.at[pl.ds(4 * b, 4), :], h_out.at[b], out_sem.at[b])
        for b in range(4)
    ]
    for copy in stores:
        copy.start()
    keep_own(h, 0, got_h)

    rows = 16 * nb
    await_spread(psi_copies, psi, PAD, got_psi, 0)
    bands = got_psi[...]
    row, col = iota(rows, rows)
    same_plane = (row & 3) == (col & 3)
    corr = jnp.where(same_plane, dot(bands, bands, NT), 0.0)
    await_spread(h_copies, h, 0, got_h, 1)
    gram = jnp.where(same_plane, dot(got_h[...], bands, NT), 0.0)
    row, col = iota(8 * nb, rows)
    band_of = (row >> 3) * 4 + (row & 3)
    pick_corr = ones_where(((row & 4) == 0) & (band_of == (col >> 2)))
    pick_gram = ones_where(((row & 4) == 4) & (band_of == (col >> 2)))
    row, col = iota(rows, LANES)
    narrow = ones_where((row >> 2) == col)
    blocks = dot(dot(pick_corr, corr, NN) + dot(pick_gram, gram, NN), narrow, NN)
    terms[...] = blocks.reshape(nb, 8, LANES)

    def exchange(source_of, target, slot, peers_, send, recv):
        copies = []
        for i, peer in enumerate(peers_):
            copy = pltpu.make_async_remote_copy(
                src_ref=source_of(i),
                dst_ref=target.at[slot],
                send_sem=send.at[i],
                recv_sem=recv.at[i],
                device_id=peer,
                device_id_type=MESH,
            )
            copy.start()
            copies.append(copy)
        return copies

    band_peers = [band_peer(dx, dh) for dx, dh in band_offsets]
    a_copies = exchange(
        lambda i: terms.at[band_peers[i]],
        band_terms,
        me_b,
        [(me_g, peer) for peer in band_peers],
        a_send,
        a_recv,
    )
    band_terms[me_b] = terms[me_b]
    for copy in a_copies:
        copy.wait_recv()
    own_sum[...] = jnp.sum(band_terms[...], axis=0)

    my_pair = my_y * 2 + my_c
    b_copies = exchange(
        lambda i: own_sum,
        pair_terms,
        my_pair,
        [(pair_peer(dy, dc), me_b) for dy, dc in pair_offsets],
        b_send,
        b_recv,
    )
    pair_terms[my_pair] = own_sum[...]
    for copy in b_copies:
        copy.wait_recv()
    pair_sum[...] = jnp.sum(pair_terms[...], axis=0)

    c_copies = exchange(
        lambda i: pair_sum,
        line_terms,
        my_z,
        [(line_peer(dz), me_b) for dz in range(1, nz)],
        c_send,
        c_recv,
    )
    line_terms[my_z] = pair_sum[...]
    for copy in c_copies:
        copy.wait_recv()
    volume = 1.0 / (4 * cells * ng)
    final = jnp.sum(line_terms[...], axis=0) * volume
    corr_out[...] = final[0:4, 0 : 4 * nb]
    gram_out[...] = final[4:8, 0 : 4 * nb]

    for copy in halo + part_copies + a_copies + b_copies + c_copies:
        copy.wait_send()
    await_sent(psi_copies, psi, PAD, got_psi, 0)
    await_sent(h_copies, h, 0, got_h, 1)
    for copy in stores:
        copy.wait()


def shards(dims, orbitals, potential, projectors, kb_energy, proj_count):
    groups, layers, cells = orbitals.shape
    nx, ny, nz = dims
    nb = nx * 2
    kinds = projectors.shape[2]
    active = lax.broadcasted_iota(jnp.int32, kb_energy.shape, 2) < proj_count[:, :, None]
    weight = jnp.where(active, kb_energy, 0.0).reshape(16, 1)
    weight = jnp.broadcast_to(weight, (16, LANES))
    width = ((cells // LANES) // nb + 1) * LANES
    f32 = jnp.float32
    any_space = pl.BlockSpec(memory_space=pl.ANY)
    vmem = pl.BlockSpec(memory_space=pltpu.VMEM)
    dma = pltpu.SemaphoreType.DMA
    return pl.pallas_call(
        functools.partial(kernel, dims),
        out_shape=(
            jax.ShapeDtypeStruct(orbitals.shape, f32),
            jax.ShapeDtypeStruct((groups, groups * nb), f32),
            jax.ShapeDtypeStruct((groups, groups * nb), f32),
        ),
        in_specs=[any_space, any_space, any_space, vmem],
        out_specs=(any_space, vmem, vmem),
        scratch_shapes=[
            pltpu.VMEM((16, cells + 2 * PAD), f32),
            pltpu.VMEM((16, cells), f32),
            pltpu.VMEM((16, cells), f32),
            pltpu.VMEM((8, cells), f32),
            pltpu.VMEM((192, cells), f32),
            pltpu.VMEM((16, cells), f32),
            pltpu.VMEM((16 * nb, width), f32),
            pltpu.VMEM((16 * nb, width), f32),
            pltpu.VMEM((8, 8, CHUNK), f32),
            pltpu.VMEM((64, LANES), f32),
            pltpu.VMEM((48, LANES), f32),
            pltpu.VMEM((48, LANES), f32),
            pltpu.VMEM((16, LANES), f32),
            pltpu.VMEM((16, LANES), f32),
            pltpu.VMEM((nb, 8, LANES), f32),
            pltpu.VMEM((nb, 8, LANES), f32),
            pltpu.VMEM((8, LANES), f32),
            pltpu.VMEM((ny * 2, 8, LANES), f32),
            pltpu.VMEM((8, LANES), f32),
            pltpu.VMEM((nz, 8, LANES), f32),
            dma((6,)),
            dma((48,)),
            dma((2,)),
            dma((2,)),
            dma((4,)),
            dma((4,)),
            dma((nb,)),
            dma((nb,)),
            dma((nb,)),
            dma((nb,)),
            dma((4,)),
            dma((32,)),
            dma((4,)),
            dma((nb,)),
            dma((nb,)),
            dma((ny * 2,)),
            dma((ny * 2,)),
            dma((nz,)),
            dma((nz,)),
        ],
        compiler_params=pltpu.CompilerParams(
            collective_id=0, has_side_effects=True, vmem_limit_bytes=60 * 2**20
        ),
        cost_estimate=pl.CostEstimate(
            flops=80_000_000, bytes_accessed=6_000_000, transcendentals=0
        ),
    )(
        orbitals,
        potential,
        projectors.reshape(3 * 2 * kinds, layers, cells),
        weight,
    )


def solution(mesh):
    ny = 4 if mesh.shape["grid"] == 64 else 1
    dims = (mesh.shape["band"] // 2, ny, mesh.shape["grid"] // (2 * ny))
    in_specs = (
        P("band", "grid", None),
        P("grid", None),
        P(None, None, None, "grid", None),
        P("grid", None, None),
        P("grid", None),
    )
    out_specs = (P("band", "grid", None), P("band", None), P("band", None))
    return jax.shard_map(
        functools.partial(shards, dims),
        mesh=mesh,
        in_specs=in_specs,
        out_specs=out_specs,
        check_vma=False,
    )
```

```python
import functools

import jax
import jax.numpy as jnp
from jax import lax
from jax.experimental import pallas as pl
from jax.experimental.pallas import tpu as pltpu
from jax.sharding import PartitionSpec as P

NY = 80
STENCIL = (-205.0 / 72.0, 8.0 / 5.0, -1.0 / 5.0, 8.0 / 315.0, -1.0 / 560.0)
MESH = pl.DeviceIdType.MESH
LANES = 128
PAD = 384
CHUNK = 640
WIDE = 1280


def iota(rows, cols):
    return (
        lax.broadcasted_iota(jnp.int32, (rows, cols), 0),
        lax.broadcasted_iota(jnp.int32, (rows, cols), 1),
    )


def ones_where(condition):
    return jnp.where(condition, 1.0, 0.0).astype(jnp.float32)


def dot(a, b, dims):
    return lax.dot_general(
        a,
        b,
        (dims, ((), ())),
        precision=lax.Precision.HIGHEST,
        preferred_element_type=jnp.float32,
    )


NN = ((1,), (0,))
NT = ((1,), (1,))
TN = ((0,), (0,))


def z_matrix():
    row, col = iota(16, 48)
    same = ((row >> 2) & 3) == ((col >> 2) & 3)
    diff = (col >> 4) * 4 + (col & 3) - 4 - (row & 3)
    dist = jnp.abs(diff)
    value = jnp.zeros((16, 48), jnp.float32)
    for k in range(1, 5):
        value = jnp.where(dist == k, -0.5 * STENCIL[k], value)
    return jnp.where(same, value, 0.0)


def kernel(
    dims,
    psi_in,
    pot_in,
    table_in,
    energy_in,
    count_in,
    h_out,
    sums_out,
    psi,
    before,
    after,
    pot,
    table,
    energy,
    count,
    h,
    full,
    got_psi,
    got_h,
    ycoef,
    part,
    low1,
    high1,
    low2,
    high2,
    owner,
    owners,
    terms,
    x_terms,
    x_sum,
    y_terms,
    y_sum,
    z_terms,
    in_sem,
    table_sem,
    halo_send,
    halo_recv,
    part_send,
    part_recv,
    psi_send,
    psi_recv,
    h_send,
    h_recv,
    extra_send,
    extra_recv,
    owner_send,
    owner_recv,
    out_sem,
    x_send,
    x_recv,
    y_send,
    y_recv,
    z_send,
    z_recv,
):
    nx, ny, nz = dims
    nb, ng = nx * 2, ny * nz * 2
    cells = pot_in.shape[1]
    per = (cells // LANES) // nb
    share = per * LANES
    me_g = lax.axis_index("grid")
    me_b = lax.axis_index("band")
    my_x, my_h = me_b // 2, me_b % 2
    my_c, my_z, my_y = me_g % 2, (me_g // 2) % nz, me_g // (2 * nz)

    extras = [(per * nb + i, (0, nx + 1)[i]) for i in range(cells // LANES - per * nb)]
    band_offsets = [(dx, dh) for dh in (1, 0) for dx in range(nx) if (dx, dh) != (0, 0)]
    x_offsets = range(1, nx)
    y_offsets = [(dh, dy) for dh in (1, 0) for dy in range(ny) if (dh, dy) != (0, 0)]
    z_offsets = [(dz, dc) for dz in range(nz) for dc in range(2) if (dz, dc) != (0, 0)]
    root = me_g % nb

    def band_peer(dx, dh):
        return ((my_x + dx) % nx) * 2 + (my_h + dh) % 2

    def y_peer(dh, dy):
        peer_g = (((my_y + dy) % ny) * nz + my_z) * 2 + my_c
        return peer_g, my_x * 2 + (my_h + dh) % 2

    def z_peer(dz, dc):
        return (my_y * nz + (my_z + dz) % nz) * 2 + (my_c + dc) % 2, me_b

    def grid_peer(step):
        return (me_g + step + ng) % ng

    loads = [
        pltpu.make_async_copy(
            psi_in.at[b], psi.at[pl.ds(4 * b, 4), pl.ds(PAD, cells)], in_sem.at[b]
        )
        for b in range(4)
    ]
    pot_loads = [
        pltpu.make_async_copy(pot_in, pot.at[pl.ds(4 * b, 4), :], in_sem.at[4 + b])
        for b in range(2)
    ]
    for copy in loads:
        copy.start()
    small_loads = pot_loads + [
        pltpu.make_async_copy(energy_in, energy, in_sem.at[6]),
        pltpu.make_async_copy(count_in, count, in_sem.at[7]),
    ]
    for copy in small_loads:
        copy.start()

    def table_copy(i):
        return pltpu.make_async_copy(
            table_in.at[i], table.at[pl.ds(pl.multiple_of(4 * i, 4), 4), :], table_sem.at[i]
        )

    @pl.loop(0, 48)
    def _(i):
        table_copy(i).start()

    psi[:, 0:PAD] = jnp.zeros((16, PAD), jnp.float32)
    psi[:, PAD + cells : PAD + cells + PAD] = jnp.zeros((16, PAD), jnp.float32)
    got_psi[:, share : share + LANES] = jnp.zeros((16 * nb, LANES), jnp.float32)
    got_h[:, share : share + LANES] = jnp.zeros((16 * nb, LANES), jnp.float32)
    owners[...] = jnp.zeros(owners.shape, jnp.float32)

    barrier = pltpu.get_barrier_semaphore()
    peers = 0
    for dx, dh in band_offsets:
        pl.semaphore_signal(
            barrier, inc=1, device_id=(me_g, band_peer(dx, dh)), device_id_type=MESH
        )
        peers += 1
    for step in (1, -1, 2, -2):
        pl.semaphore_signal(
            barrier, inc=1, device_id=(grid_peer(step), me_b), device_id_type=MESH
        )
        peers += 1
    for peer in [y_peer(dh, dy) for dh, dy in y_offsets] + [
        z_peer(dz, dc) for dz, dc in z_offsets
    ]:
        pl.semaphore_signal(barrier, inc=1, device_id=peer, device_id_type=MESH)
        peers += 1

    _, lane = iota(8, CHUNK)
    turn = jnp.zeros((8, CHUNK), jnp.int32)
    for m in range(1, CHUNK // NY):
        turn = turn + jnp.where(lane >= m * NY, 1, 0)
    column = lane - turn * NY
    for k in range(1, 5):
        ycoef[k - 1] = jnp.where(column + k < NY, -0.5 * STENCIL[k], 0.0)
        ycoef[3 + k] = jnp.where(column >= k, -0.5 * STENCIL[k], 0.0)

    for copy in loads:
        copy.wait()
    pl.semaphore_wait(barrier, peers)

    halo = []
    for i, (step, target) in enumerate(((1, before), (-1, after))):
        copy = pltpu.make_async_remote_copy(
            src_ref=psi.at[:, pl.ds(PAD, cells)],
            dst_ref=target,
            send_sem=halo_send.at[i],
            recv_sem=halo_recv.at[i],
            device_id=(grid_peer(step), me_b),
            device_id_type=MESH,
        )
        copy.start()
        halo.append(copy)

    my_rows = pl.ds(pl.multiple_of(me_b * 16, 16), 16)

    def spread(source, base, target, send, recv, which):
        copies = []
        for i, (dx, dh) in enumerate(band_offsets):
            peer = band_peer(dx, dh)
            start = pl.multiple_of(base + peer * share, LANES)
            copy = pltpu.make_async_remote_copy(
                src_ref=source.at[:, pl.ds(start, share)],
                dst_ref=target.at[my_rows, pl.ds(0, share)],
                send_sem=send.at[i],
                recv_sem=recv.at[i],
                device_id=(me_g, peer),
                device_id_type=MESH,
            )
            copy.start()
            copies.append(copy)
        for i, (tile, owner) in enumerate(extras):

            @pl.when(me_b != owner)
            def _(i=i, tile=tile, owner=owner):
                extra_copy(source, base, target, which, i, tile, owner, me_b).start()

        return copies

    def extra_copy(source, base, target, which, i, tile, owner, sem):
        return pltpu.make_async_remote_copy(
            src_ref=source.at[:, pl.ds(base + tile * LANES, LANES)],
            dst_ref=target.at[my_rows, pl.ds(share, LANES)],
            send_sem=extra_send.at[which * 2 + i],
            recv_sem=extra_recv.at[which * 16 + sem],
            device_id=(me_g, owner),
            device_id_type=MESH,
        )

    def keep_own(source, base, target):
        start = pl.multiple_of(base + me_b * share, LANES)
        target[my_rows, 0:share] = source[:, pl.ds(start, share)]
        for tile, owner in extras:

            @pl.when(me_b == owner)
            def _(tile=tile):
                target[my_rows, share : share + LANES] = source[
                    :, base + tile * LANES : base + (tile + 1) * LANES
                ]

    def await_spread(copies, source, base, target, which):
        for copy in copies:
            copy.wait_recv()
        for i, (tile, owner) in enumerate(extras):

            @pl.when(me_b == owner)
            def _(i=i, tile=tile, owner=owner):
                for other in range(nb):
                    if other != owner:
                        extra_copy(
                            source, base, target, which, i, tile, owner, other
                        ).wait_recv()

    def await_sent(copies, source, base, target, which):
        for copy in copies:
            copy.wait_send()
        for i, (tile, owner) in enumerate(extras):

            @pl.when(me_b != owner)
            def _(i=i, tile=tile, owner=owner):
                extra_copy(source, base, target, which, i, tile, owner, me_b).wait_send()

    psi_copies = spread(psi, PAD, got_psi, psi_send, psi_recv, 0)

    @pl.loop(0, 48)
    def _(i):
        table_copy(i).wait()

    def partial_step(i, total):
        start = pl.multiple_of(i * WIDE, LANES)
        return total + dot(
            table[:, pl.ds(start, WIDE)], psi[:, pl.ds(start + PAD, WIDE)], NT
        )

    raw = lax.fori_loop(0, cells // WIDE, partial_step, jnp.zeros((192, 16), jnp.float32))
    row, col = iota(192, 16)
    raw = jnp.where((row & 3) == (col & 3), raw, 0.0)
    row, col = iota(64, 192)
    source_row = jnp.where(row < 32, row, jnp.where(row < 48, -1, row - 16))
    gather = ones_where(source_row == (col >> 2))
    row, col = iota(16, LANES)
    widen = ones_where((row >> 2) == (col >> 2))
    sums = dot(dot(gather, raw, NN), widen, NN)
    part[...] = sums
    for copy in small_loads:
        copy.wait()
    row, col = iota(16, 8)
    kinds = jnp.concatenate(
        [jnp.broadcast_to(energy[0, a : a + 1, :], (8, 8)) for a in range(2)], axis=0
    )
    active = jnp.concatenate(
        [jnp.broadcast_to(count[0:1, a : a + 1], (8, 8)) for a in range(2)], axis=0
    )
    chosen = jnp.where((col == (row & 7)) & (col < active), kinds, 0.0)
    weight = jnp.broadcast_to(jnp.sum(chosen, axis=1, keepdims=True), (16, LANES))
    part[32:48, :] = weight

    part_copies = []
    for i, (step, first, count, target) in enumerate(
        ((1, 16, 48, low1), (-1, 0, 48, high1), (2, 48, 16, low2), (-2, 0, 16, high2))
    ):
        copy = pltpu.make_async_remote_copy(
            src_ref=part.at[pl.ds(first, count), :],
            dst_ref=target,
            send_sem=part_send.at[i],
            recv_sem=part_recv.at[i],
            device_id=(grid_peer(step), me_b),
            device_id_type=MESH,
        )
        copy.start()
        part_copies.append(copy)

    @pl.loop(0, cells // CHUNK)
    def _(i):
        start = pl.multiple_of(i * CHUNK, LANES)
        wide = psi[:, pl.ds(start, CHUNK + 2 * PAD)]

        def shifted(offset):
            return wide[:, PAD + offset : PAD + offset + CHUNK]

        here = pot[:, pl.ds(start, CHUNK)] + (-1.5 * STENCIL[0])
        total = jnp.concatenate([here, here], axis=0) * shifted(0)
        for k in range(1, 5):
            total = total + (-0.5 * STENCIL[k]) * (shifted(NY * k) + shifted(-NY * k))
            up, down = ycoef[k - 1], ycoef[3 + k]
            total = total + jnp.concatenate([up, up], axis=0) * shifted(k)
            total = total + jnp.concatenate([down, down], axis=0) * shifted(-k)
        h[:, pl.ds(start, CHUNK)] = total

    keep_own(psi, PAD, got_psi)

    for copy in halo:
        copy.wait_recv()
    across = z_matrix()

    @pl.loop(0, cells // WIDE)
    def _(i):
        start = pl.multiple_of(i * WIDE, LANES)
        here = pl.ds(start, WIDE)
        planes = jnp.concatenate(
            [before[:, here], psi[:, pl.ds(start + PAD, WIDE)], after[:, here]], axis=0
        )
        h[:, here] = h[:, here] + dot(across, planes, NN)

    h_copies = spread(h, 0, got_h, h_send, h_recv, 1)
    keep_own(h, 0, got_h)

    for copy in part_copies:
        copy.wait_recv()
    total = part[16:32, :] + high1[0:16, :] + low1[32:48, :]
    coef = jnp.concatenate(
        [
            low1[16:32, :] * (low1[0:16, :] + part[0:16, :] + low2[...]),
            weight * total,
            high1[32:48, :] * (high1[16:32, :] + high2[...] + part[48:64, :]),
        ],
        axis=0,
    )

    row, col = iota(LANES, LANES)
    place = ones_where((row < 16) & ((row & 3) == 0) & (col == me_b * 4 + (row >> 2)))
    owner[...] = dot(total, place, NN)

    def owner_copy(sem):
        return pltpu.make_async_remote_copy(
            src_ref=owner,
            dst_ref=owners.at[me_b],
            send_sem=owner_send,
            recv_sem=owner_recv.at[sem],
            device_id=(me_g, root),
            device_id_type=MESH,
        )

    @pl.when(me_b != root)
    def _():
        owner_copy(me_b).start()

    @pl.when(me_b == root)
    def _():
        owners[me_b] = owner[...]

    row, col = iota(48, 192)
    repeat = ones_where(row == (col >> 2))
    spread_coef = dot(coef, repeat, TN)[0:16, :]
    row, col = iota(16, 192)
    spread_coef = jnp.where((row & 3) == (col & 3), spread_coef, 0.0)

    @pl.loop(0, cells // WIDE)
    def _(i):
        start = pl.multiple_of(i * WIDE, LANES)
        here = pl.ds(start, WIDE)
        full[:, here] = h[:, here] + dot(spread_coef, table[:, here], NN)

    stores = [
        pltpu.make_async_copy(full.at[pl.ds(4 * b, 4), :], h_out.at[b], out_sem.at[b])
        for b in range(4)
    ]
    for copy in stores:
        copy.start()

    @pl.when(me_b == root)
    def _():
        for other in range(nb):

            @pl.when(other != me_b)
            def _(other=other):
                owner_copy(other).wait_recv()

    projections = jnp.sum(owners[...], axis=0)
    nonlocal_gram = dot(projections * weight, projections, TN)

    rows = 16 * nb
    row, col = iota(8 * nb, rows)
    band_of = (row >> 3) * 4 + (row & 3)
    pick_corr = ones_where(((row & 4) == 0) & (band_of == (col >> 2)))
    pick_gram = ones_where(((row & 4) == 4) & (band_of == (col >> 2)))
    row, col = iota(8 * nb, LANES)
    band_of = (row >> 3) * 4 + (row & 3)
    pick_nonlocal = ones_where(((row & 4) == 4) & (band_of == col))
    row, col = iota(rows, LANES)
    narrow = ones_where((row >> 2) == col)
    row, col = iota(rows, rows)
    same_plane = (row & 3) == (col & 3)
    await_spread(psi_copies, psi, PAD, got_psi, 0)
    bands = got_psi[...]
    corr = jnp.where(same_plane, dot(bands, bands, NT), 0.0)
    early = dot(pick_nonlocal, nonlocal_gram, NN) + dot(dot(pick_corr, corr, NN), narrow, NN)
    await_spread(h_copies, h, 0, got_h, 1)
    gram = jnp.where(same_plane, dot(got_h[...], bands, NT), 0.0)
    blocks = early + dot(dot(pick_gram, gram, NN), narrow, NN)
    terms[...] = blocks.reshape(nb, 8, LANES)

    def exchange(source_of, target, slot, peers_, send, recv):
        copies = []
        for i, peer in enumerate(peers_):
            copy = pltpu.make_async_remote_copy(
                src_ref=source_of(i),
                dst_ref=target.at[slot],
                send_sem=send.at[i],
                recv_sem=recv.at[i],
                device_id=peer,
                device_id_type=MESH,
            )
            copy.start()
            copies.append(copy)
        return copies

    x_copies = exchange(
        lambda i: terms.at[pl.ds(((my_x + x_offsets[i]) % nx) * 2, 2)],
        x_terms,
        my_x,
        [(me_g, band_peer(dx, 0)) for dx in x_offsets],
        x_send,
        x_recv,
    )
    x_terms[my_x] = terms[pl.ds(my_x * 2, 2)]
    for copy in x_copies:
        copy.wait_recv()
    x_sum[...] = jnp.sum(x_terms[...], axis=0)

    slot = my_h * ny + my_y
    y_copies = exchange(
        lambda i: x_sum.at[(my_h + y_offsets[i][0]) % 2],
        y_terms,
        slot,
        [y_peer(dh, dy) for dh, dy in y_offsets],
        y_send,
        y_recv,
    )
    y_terms[slot] = x_sum[my_h]
    for copy in y_copies:
        copy.wait_recv()
    y_sum[...] = jnp.sum(y_terms[...], axis=0)

    slot = my_z * 2 + my_c
    z_copies = exchange(
        lambda i: y_sum,
        z_terms,
        slot,
        [z_peer(dz, dc) for dz, dc in z_offsets],
        z_send,
        z_recv,
    )
    z_terms[slot] = y_sum[...]
    for copy in z_copies:
        copy.wait_recv()
    sums_out[...] = jnp.sum(z_terms[...], axis=0) * (1.0 / (4 * cells * ng))

    for copy in halo + part_copies + x_copies + y_copies + z_copies:
        copy.wait_send()
    await_sent(psi_copies, psi, PAD, got_psi, 0)
    await_sent(h_copies, h, 0, got_h, 1)

    @pl.when(me_b != root)
    def _():
        owner_copy(me_b).wait_send()

    for copy in stores:
        copy.wait()


def finish(h_in, sums_in, h_out, corr_out, gram_out, sem):
    copies = [pltpu.make_async_copy(h_in.at[b], h_out.at[b], sem.at[b]) for b in range(4)]
    for copy in copies:
        copy.start()
    width = corr_out.shape[1]
    corr_out[...] = sums_in[0:4, 0:width]
    gram_out[...] = sums_in[4:8, 0:width]
    for copy in copies:
        copy.wait()


def shards(dims, orbitals, potential, projectors, kb_energy, proj_count):
    groups, layers, cells = orbitals.shape
    nx, ny, nz = dims
    nb = nx * 2
    kinds = projectors.shape[2]
    width = ((cells // LANES) // nb + 1) * LANES
    f32 = jnp.float32
    any_space = pl.BlockSpec(memory_space=pl.ANY)
    vmem = pl.BlockSpec(memory_space=pltpu.VMEM)
    dma = pltpu.SemaphoreType.DMA
    full, sums = pl.pallas_call(
        functools.partial(kernel, dims),
        out_shape=(
            jax.ShapeDtypeStruct(orbitals.shape, f32),
            jax.ShapeDtypeStruct((8, LANES), f32),
        ),
        in_specs=[any_space] * 5,
        out_specs=(any_space, vmem),
        scratch_shapes=[
            pltpu.VMEM((16, cells + 2 * PAD), f32),
            pltpu.VMEM((16, cells), f32),
            pltpu.VMEM((16, cells), f32),
            pltpu.VMEM((8, cells), f32),
            pltpu.VMEM((192, cells), f32),
            pltpu.VMEM(kb_energy.shape, f32),
            pltpu.VMEM(proj_count.shape, jnp.int32),
            pltpu.VMEM((16, cells), f32),
            pltpu.VMEM((16, cells), f32),
            pltpu.VMEM((16 * nb, width), f32),
            pltpu.VMEM((16 * nb, width), f32),
            pltpu.VMEM((8, 8, CHUNK), f32),
            pltpu.VMEM((64, LANES), f32),
            pltpu.VMEM((48, LANES), f32),
            pltpu.VMEM((48, LANES), f32),
            pltpu.VMEM((16, LANES), f32),
            pltpu.VMEM((16, LANES), f32),
            pltpu.VMEM((16, LANES), f32),
            pltpu.VMEM((nb, 16, LANES), f32),
            pltpu.VMEM((nb, 8, LANES), f32),
            pltpu.VMEM((nx, 2, 8, LANES), f32),
            pltpu.VMEM((2, 8, LANES), f32),
            pltpu.VMEM((ny * 2, 8, LANES), f32),
            pltpu.VMEM((8, LANES), f32),
            pltpu.VMEM((nz * 2, 8, LANES), f32),
            dma((8,)),
            dma((48,)),
            dma((2,)),
            dma((2,)),
            dma((4,)),
            dma((4,)),
            dma((nb,)),
            dma((nb,)),
            dma((nb,)),
            dma((nb,)),
            dma((4,)),
            dma((32,)),
            dma,
            dma((nb,)),
            dma((4,)),
            dma((nx,)),
            dma((nx,)),
            dma((ny * 2,)),
            dma((ny * 2,)),
            dma((nz * 2,)),
            dma((nz * 2,)),
        ],
        compiler_params=pltpu.CompilerParams(
            collective_id=0, has_side_effects=True, vmem_limit_bytes=60 * 2**20
        ),
        cost_estimate=pl.CostEstimate(
            flops=80_000_000, bytes_accessed=6_000_000, transcendentals=0
        ),
    )(
        orbitals,
        potential,
        projectors.reshape(3 * 2 * kinds, layers, cells),
        kb_energy,
        proj_count,
    )
    return pl.pallas_call(
        finish,
        out_shape=(
            jax.ShapeDtypeStruct(orbitals.shape, f32),
            jax.ShapeDtypeStruct((groups, groups * nb), f32),
            jax.ShapeDtypeStruct((groups, groups * nb), f32),
        ),
        in_specs=[any_space, vmem],
        out_specs=(any_space, vmem, vmem),
        scratch_shapes=[dma((4,))],
        compiler_params=pltpu.CompilerParams(vmem_limit_bytes=60 * 2**20),
        cost_estimate=pl.CostEstimate(flops=0, bytes_accessed=900_000, transcendentals=0),
    )(full, sums)


def solution(mesh):
    ny = 4 if mesh.shape["grid"] == 64 else 1
    dims = (mesh.shape["band"] // 2, ny, mesh.shape["grid"] // (2 * ny))
    in_specs = (
        P("band", "grid", None),
        P("grid", None),
        P(None, None, None, "grid", None),
        P("grid", None, None),
        P("grid", None),
    )
    out_specs = (P("band", "grid", None), P("band", None), P("band", None))
    return jax.shard_map(
        functools.partial(shards, dims),
        mesh=mesh,
        in_specs=in_specs,
        out_specs=out_specs,
        check_vma=False,
    )
```

```python
import functools

import jax
import jax.numpy as jnp
from jax import lax
from jax.experimental import pallas as pl
from jax.experimental.pallas import tpu as pltpu
from jax.sharding import PartitionSpec as P

NY = 80
STENCIL = (-205.0 / 72.0, 8.0 / 5.0, -1.0 / 5.0, 8.0 / 315.0, -1.0 / 560.0)
MESH = pl.DeviceIdType.MESH
LANES = 128
PAD = 384
CHUNK = 640
WIDE = 1280


def iota(rows, cols):
    return (
        lax.broadcasted_iota(jnp.int32, (rows, cols), 0),
        lax.broadcasted_iota(jnp.int32, (rows, cols), 1),
    )


def ones_where(condition):
    return jnp.where(condition, 1.0, 0.0).astype(jnp.float32)


def dot(a, b, dims):
    return lax.dot_general(
        a,
        b,
        (dims, ((), ())),
        precision=lax.Precision.HIGHEST,
        preferred_element_type=jnp.float32,
    )


NN = ((1,), (0,))
NT = ((1,), (1,))
TN = ((0,), (0,))


def z_matrix():
    row, col = iota(16, 48)
    same = ((row >> 2) & 3) == ((col >> 2) & 3)
    diff = (col >> 4) * 4 + (col & 3) - 4 - (row & 3)
    dist = jnp.abs(diff)
    value = jnp.zeros((16, 48), jnp.float32)
    for k in range(1, 5):
        value = jnp.where(dist == k, -0.5 * STENCIL[k], value)
    return jnp.where(same, value, 0.0)


def kernel(
    dims,
    psi_in,
    pot_in,
    table_in,
    energy_in,
    count_in,
    h_out,
    sums_out,
    psi,
    before,
    after,
    pot,
    table,
    energy,
    count,
    h,
    full,
    got_psi,
    got_h,
    ycoef,
    part,
    low1,
    high1,
    low2,
    high2,
    owner,
    owners,
    terms,
    x_terms,
    x_sum,
    y_terms,
    y_sum,
    z_terms,
    in_sem,
    table_sem,
    halo_send,
    halo_recv,
    part_send,
    part_recv,
    psi_send,
    psi_recv,
    h_send,
    h_recv,
    extra_send,
    extra_recv,
    owner_send,
    owner_recv,
    out_sem,
    x_send,
    x_recv,
    y_send,
    y_recv,
    z_send,
    z_recv,
):
    nx, ny, nz = dims
    nb, ng = nx * 2, ny * nz * 2
    cells = pot_in.shape[1]
    per = (cells // LANES) // nb
    share = per * LANES
    me_g = lax.axis_index("grid")
    me_b = lax.axis_index("band")
    my_x, my_h = me_b // 2, me_b % 2
    my_c, my_z, my_y = me_g % 2, (me_g // 2) % nz, me_g // (2 * nz)

    extras = [(per * nb + i, (0, nx + 1)[i]) for i in range(cells // LANES - per * nb)]
    band_offsets = [(dx, dh) for dh in (1, 0) for dx in range(nx) if (dx, dh) != (0, 0)]
    x_offsets = range(1, nx)
    y_offsets = [(dh, dy) for dh in (1, 0) for dy in range(ny) if (dh, dy) != (0, 0)]
    z_offsets = [(dz, dc) for dz in range(nz) for dc in range(2) if (dz, dc) != (0, 0)]
    root = me_g % nb

    def band_peer(dx, dh):
        return ((my_x + dx) % nx) * 2 + (my_h + dh) % 2

    def y_peer(dh, dy):
        peer_g = (((my_y + dy) % ny) * nz + my_z) * 2 + my_c
        return peer_g, my_x * 2 + (my_h + dh) % 2

    def z_peer(dz, dc):
        return (my_y * nz + (my_z + dz) % nz) * 2 + (my_c + dc) % 2, me_b

    def grid_peer(step):
        return (me_g + step + ng) % ng

    barrier = pltpu.get_barrier_semaphore()
    peers = 0
    for dx, dh in band_offsets:
        pl.semaphore_signal(
            barrier, inc=1, device_id=(me_g, band_peer(dx, dh)), device_id_type=MESH
        )
        peers += 1
    for step in (1, -1, 2, -2):
        pl.semaphore_signal(
            barrier, inc=1, device_id=(grid_peer(step), me_b), device_id_type=MESH
        )
        peers += 1
    for peer in [y_peer(dh, dy) for dh, dy in y_offsets] + [
        z_peer(dz, dc) for dz, dc in z_offsets
    ]:
        pl.semaphore_signal(barrier, inc=1, device_id=peer, device_id_type=MESH)
        peers += 1

    loads = [
        pltpu.make_async_copy(
            psi_in.at[b], psi.at[pl.ds(4 * b, 4), pl.ds(PAD, cells)], in_sem.at[b]
        )
        for b in range(4)
    ]
    pot_loads = [
        pltpu.make_async_copy(pot_in, pot.at[pl.ds(4 * b, 4), :], in_sem.at[4 + b])
        for b in range(2)
    ]
    for copy in loads:
        copy.start()
    small_loads = pot_loads + [
        pltpu.make_async_copy(energy_in, energy, in_sem.at[6]),
        pltpu.make_async_copy(count_in, count, in_sem.at[7]),
    ]
    for copy in small_loads:
        copy.start()

    def table_copy(i):
        return pltpu.make_async_copy(
            table_in.at[i], table.at[pl.ds(pl.multiple_of(4 * i, 4), 4), :], table_sem.at[i]
        )

    @pl.loop(0, 48)
    def _(i):
        table_copy(i).start()

    psi[:, 0:PAD] = jnp.zeros((16, PAD), jnp.float32)
    psi[:, PAD + cells : PAD + cells + PAD] = jnp.zeros((16, PAD), jnp.float32)

    @pl.when((me_b != extras[0][1]) & (me_b != extras[1][1]))
    def _():
        got_psi[:, share : share + LANES] = jnp.zeros((16 * nb, LANES), jnp.float32)
        got_h[:, share : share + LANES] = jnp.zeros((16 * nb, LANES), jnp.float32)

    @pl.when(me_b != root)
    def _():
        owners[...] = jnp.zeros(owners.shape, jnp.float32)


    _, lane = iota(8, CHUNK)
    turn = jnp.zeros((8, CHUNK), jnp.int32)
    for m in range(1, CHUNK // NY):
        turn = turn + jnp.where(lane >= m * NY, 1, 0)
    column = lane - turn * NY
    for k in range(1, 5):
        ycoef[k - 1] = jnp.where(column + k < NY, -0.5 * STENCIL[k], 0.0)
        ycoef[3 + k] = jnp.where(column >= k, -0.5 * STENCIL[k], 0.0)

    for copy in loads:
        copy.wait()
    pl.semaphore_wait(barrier, peers)

    halo = []
    for i, (step, target) in enumerate(((1, before), (-1, after))):
        copy = pltpu.make_async_remote_copy(
            src_ref=psi.at[:, pl.ds(PAD, cells)],
            dst_ref=target,
            send_sem=halo_send.at[i],
            recv_sem=halo_recv.at[i],
            device_id=(grid_peer(step), me_b),
            device_id_type=MESH,
        )
        copy.start()
        halo.append(copy)

    my_rows = pl.ds(pl.multiple_of(me_b * 16, 16), 16)

    def spread(source, base, target, send, recv, which):
        copies = []
        for i, (dx, dh) in enumerate(band_offsets):
            peer = band_peer(dx, dh)
            start = pl.multiple_of(base + peer * share, LANES)
            copy = pltpu.make_async_remote_copy(
                src_ref=source.at[:, pl.ds(start, share)],
                dst_ref=target.at[my_rows, pl.ds(0, share)],
                send_sem=send.at[i],
                recv_sem=recv.at[i],
                device_id=(me_g, peer),
                device_id_type=MESH,
            )
            copy.start()
            copies.append(copy)
        for i, (tile, owner) in enumerate(extras):

            @pl.when(me_b != owner)
            def _(i=i, tile=tile, owner=owner):
                extra_copy(source, base, target, which, i, tile, owner, me_b).start()

        return copies

    def extra_copy(source, base, target, which, i, tile, owner, sem):
        return pltpu.make_async_remote_copy(
            src_ref=source.at[:, pl.ds(base + tile * LANES, LANES)],
            dst_ref=target.at[my_rows, pl.ds(share, LANES)],
            send_sem=extra_send.at[which * 2 + i],
            recv_sem=extra_recv.at[which * 16 + sem],
            device_id=(me_g, owner),
            device_id_type=MESH,
        )

    def keep_own(source, base, target):
        start = pl.multiple_of(base + me_b * share, LANES)
        target[my_rows, 0:share] = source[:, pl.ds(start, share)]
        for tile, owner in extras:

            @pl.when(me_b == owner)
            def _(tile=tile):
                target[my_rows, share : share + LANES] = source[
                    :, base + tile * LANES : base + (tile + 1) * LANES
                ]

    def await_spread(copies, source, base, target, which):
        for copy in copies:
            copy.wait_recv()
        for i, (tile, owner) in enumerate(extras):

            @pl.when(me_b == owner)
            def _(i=i, tile=tile, owner=owner):
                for other in range(nb):
                    if other != owner:
                        extra_copy(
                            source, base, target, which, i, tile, owner, other
                        ).wait_recv()

    def await_sent(copies, source, base, target, which):
        for copy in copies:
            copy.wait_send()
        for i, (tile, owner) in enumerate(extras):

            @pl.when(me_b != owner)
            def _(i=i, tile=tile, owner=owner):
                extra_copy(source, base, target, which, i, tile, owner, me_b).wait_send()

    psi_copies = spread(psi, PAD, got_psi, psi_send, psi_recv, 0)

    @pl.loop(0, 48)
    def _(i):
        table_copy(i).wait()

    def partial_step(i, total):
        start = pl.multiple_of(i * WIDE, LANES)
        return total + dot(
            table[:, pl.ds(start, WIDE)], psi[:, pl.ds(start + PAD, WIDE)], NT
        )

    raw = lax.fori_loop(0, cells // WIDE, partial_step, jnp.zeros((192, 16), jnp.float32))
    row, col = iota(192, 16)
    raw = jnp.where((row & 3) == (col & 3), raw, 0.0)
    row, col = iota(64, 192)
    source_row = jnp.where(row < 32, row, jnp.where(row < 48, -1, row - 16))
    gather = ones_where(source_row == (col >> 2))
    row, col = iota(16, LANES)
    widen = ones_where((row >> 2) == (col >> 2))
    sums = dot(dot(gather, raw, NN), widen, NN)
    part[...] = sums
    for copy in small_loads:
        copy.wait()
    row, col = iota(16, 8)
    kinds = jnp.concatenate(
        [jnp.broadcast_to(energy[0, a : a + 1, :], (8, 8)) for a in range(2)], axis=0
    )
    active = jnp.concatenate(
        [jnp.broadcast_to(count[0:1, a : a + 1], (8, 8)) for a in range(2)], axis=0
    )
    chosen = jnp.where((col == (row & 7)) & (col < active), kinds, 0.0)
    weight = jnp.broadcast_to(jnp.sum(chosen, axis=1, keepdims=True), (16, LANES))
    part[32:48, :] = weight

    part_copies = []
    for i, (step, first, count, target) in enumerate(
        ((1, 16, 48, low1), (-1, 0, 48, high1), (2, 48, 16, low2), (-2, 0, 16, high2))
    ):
        copy = pltpu.make_async_remote_copy(
            src_ref=part.at[pl.ds(first, count), :],
            dst_ref=target,
            send_sem=part_send.at[i],
            recv_sem=part_recv.at[i],
            device_id=(grid_peer(step), me_b),
            device_id_type=MESH,
        )
        copy.start()
        part_copies.append(copy)

    @pl.loop(0, cells // CHUNK)
    def _(i):
        start = pl.multiple_of(i * CHUNK, LANES)
        wide = psi[:, pl.ds(start, CHUNK + 2 * PAD)]

        def shifted(offset):
            return wide[:, PAD + offset : PAD + offset + CHUNK]

        here = pot[:, pl.ds(start, CHUNK)] + (-1.5 * STENCIL[0])
        total = jnp.concatenate([here, here], axis=0) * shifted(0)
        for k in range(1, 5):
            total = total + (-0.5 * STENCIL[k]) * (shifted(NY * k) + shifted(-NY * k))
            up, down = ycoef[k - 1], ycoef[3 + k]
            total = total + jnp.concatenate([up, up], axis=0) * shifted(k)
            total = total + jnp.concatenate([down, down], axis=0) * shifted(-k)
        h[:, pl.ds(start, CHUNK)] = total

    keep_own(psi, PAD, got_psi)

    for copy in halo:
        copy.wait_recv()
    across = z_matrix()

    @pl.loop(0, cells // WIDE)
    def _(i):
        start = pl.multiple_of(i * WIDE, LANES)
        here = pl.ds(start, WIDE)
        planes = jnp.concatenate(
            [before[:, here], psi[:, pl.ds(start + PAD, WIDE)], after[:, here]], axis=0
        )
        h[:, here] = h[:, here] + dot(across, planes, NN)

    h_copies = spread(h, 0, got_h, h_send, h_recv, 1)
    keep_own(h, 0, got_h)

    for copy in part_copies:
        copy.wait_recv()
    total = part[16:32, :] + high1[0:16, :] + low1[32:48, :]
    coef = jnp.concatenate(
        [
            low1[16:32, :] * (low1[0:16, :] + part[0:16, :] + low2[...]),
            weight * total,
            high1[32:48, :] * (high1[16:32, :] + high2[...] + part[48:64, :]),
        ],
        axis=0,
    )

    row, col = iota(LANES, LANES)
    place = ones_where((row < 16) & ((row & 3) == 0) & (col == me_b * 4 + (row >> 2)))
    owner[...] = dot(total, place, NN)

    def owner_copy(sem):
        return pltpu.make_async_remote_copy(
            src_ref=owner,
            dst_ref=owners.at[me_b],
            send_sem=owner_send,
            recv_sem=owner_recv.at[sem],
            device_id=(me_g, root),
            device_id_type=MESH,
        )

    @pl.when(me_b != root)
    def _():
        owner_copy(me_b).start()

    @pl.when(me_b == root)
    def _():
        owners[me_b] = owner[...]

    row, col = iota(48, 192)
    repeat = ones_where(row == (col >> 2))
    spread_coef = dot(coef, repeat, TN)[0:16, :]
    row, col = iota(16, 192)
    spread_coef = jnp.where((row & 3) == (col & 3), spread_coef, 0.0)

    @pl.loop(0, cells // WIDE)
    def _(i):
        start = pl.multiple_of(i * WIDE, LANES)
        here = pl.ds(start, WIDE)
        full[:, here] = h[:, here] + dot(spread_coef, table[:, here], NN)

    stores = [
        pltpu.make_async_copy(full.at[pl.ds(4 * b, 4), :], h_out.at[b], out_sem.at[b])
        for b in range(4)
    ]
    for copy in stores:
        copy.start()

    @pl.when(me_b == root)
    def _():
        for other in range(nb):

            @pl.when(other != me_b)
            def _(other=other):
                owner_copy(other).wait_recv()

    projections = jnp.sum(owners[...], axis=0)
    nonlocal_gram = dot(projections * weight, projections, TN)

    rows = 16 * nb
    row, col = iota(8 * nb, rows)
    band_of = (row >> 3) * 4 + (row & 3)
    pick_corr = ones_where(((row & 4) == 0) & (band_of == (col >> 2)))
    pick_gram = ones_where(((row & 4) == 4) & (band_of == (col >> 2)))
    row, col = iota(8 * nb, LANES)
    band_of = (row >> 3) * 4 + (row & 3)
    pick_nonlocal = ones_where(((row & 4) == 4) & (band_of == col))
    row, col = iota(rows, LANES)
    narrow = ones_where((row >> 2) == col)
    row, col = iota(rows, rows)
    same_plane = (row & 3) == (col & 3)
    await_spread(psi_copies, psi, PAD, got_psi, 0)
    bands = got_psi[...]
    corr = jnp.where(same_plane, dot(bands, bands, NT), 0.0)
    early = dot(pick_nonlocal, nonlocal_gram, NN) + dot(dot(pick_corr, corr, NN), narrow, NN)
    await_spread(h_copies, h, 0, got_h, 1)
    gram = jnp.where(same_plane, dot(got_h[...], bands, NT), 0.0)
    blocks = early + dot(dot(pick_gram, gram, NN), narrow, NN)
    terms[...] = blocks.reshape(nb, 8, LANES)

    def exchange(source_of, target, slot, peers_, send, recv):
        copies = []
        for i, peer in enumerate(peers_):
            copy = pltpu.make_async_remote_copy(
                src_ref=source_of(i),
                dst_ref=target.at[slot],
                send_sem=send.at[i],
                recv_sem=recv.at[i],
                device_id=peer,
                device_id_type=MESH,
            )
            copy.start()
            copies.append(copy)
        return copies

    x_copies = exchange(
        lambda i: terms.at[pl.ds(((my_x + x_offsets[i]) % nx) * 2, 2)],
        x_terms,
        my_x,
        [(me_g, band_peer(dx, 0)) for dx in x_offsets],
        x_send,
        x_recv,
    )
    x_terms[my_x] = terms[pl.ds(my_x * 2, 2)]
    for copy in x_copies:
        copy.wait_recv()
    x_sum[...] = jnp.sum(x_terms[...], axis=0)

    slot = my_h * ny + my_y
    y_copies = exchange(
        lambda i: x_sum.at[(my_h + y_offsets[i][0]) % 2],
        y_terms,
        slot,
        [y_peer(dh, dy) for dh, dy in y_offsets],
        y_send,
        y_recv,
    )
    y_terms[slot] = x_sum[my_h]
    for copy in y_copies:
        copy.wait_recv()
    y_sum[...] = jnp.sum(y_terms[...], axis=0)

    slot = my_z * 2 + my_c
    z_copies = exchange(
        lambda i: y_sum,
        z_terms,
        slot,
        [z_peer(dz, dc) for dz, dc in z_offsets],
        z_send,
        z_recv,
    )
    z_terms[slot] = y_sum[...]
    for copy in z_copies:
        copy.wait_recv()
    sums_out[...] = jnp.sum(z_terms[...], axis=0) * (1.0 / (4 * cells * ng))

    for copy in halo + part_copies + x_copies + y_copies + z_copies:
        copy.wait_send()
    await_sent(psi_copies, psi, PAD, got_psi, 0)
    await_sent(h_copies, h, 0, got_h, 1)

    @pl.when(me_b != root)
    def _():
        owner_copy(me_b).wait_send()

    for copy in stores:
        copy.wait()


def finish(h_in, sums_in, h_out, corr_out, gram_out, held, sem):
    ins = [pltpu.make_async_copy(h_in.at[b], held.at[b], sem.at[b]) for b in range(4)]
    outs = [pltpu.make_async_copy(held.at[b], h_out.at[b], sem.at[4 + b]) for b in range(4)]
    for copy in ins:
        copy.start()
    width = corr_out.shape[1]
    corr_out[...] = sums_in[0:4, 0:width]
    gram_out[...] = sums_in[4:8, 0:width]
    for copy, onward in zip(ins, outs):
        copy.wait()
        onward.start()
    for copy in outs:
        copy.wait()


def shards(dims, orbitals, potential, projectors, kb_energy, proj_count):
    groups, layers, cells = orbitals.shape
    nx, ny, nz = dims
    nb = nx * 2
    kinds = projectors.shape[2]
    width = ((cells // LANES) // nb + 1) * LANES
    f32 = jnp.float32
    any_space = pl.BlockSpec(memory_space=pl.ANY)
    vmem = pl.BlockSpec(memory_space=pltpu.VMEM)
    dma = pltpu.SemaphoreType.DMA
    full, sums = pl.pallas_call(
        functools.partial(kernel, dims),
        out_shape=(
            jax.ShapeDtypeStruct(orbitals.shape, f32),
            jax.ShapeDtypeStruct((8, LANES), f32),
        ),
        in_specs=[any_space] * 5,
        out_specs=(any_space, vmem),
        scratch_shapes=[
            pltpu.VMEM((16, cells + 2 * PAD), f32),
            pltpu.VMEM((16, cells), f32),
            pltpu.VMEM((16, cells), f32),
            pltpu.VMEM((8, cells), f32),
            pltpu.VMEM((192, cells), f32),
            pltpu.VMEM(kb_energy.shape, f32),
            pltpu.VMEM(proj_count.shape, jnp.int32),
            pltpu.VMEM((16, cells), f32),
            pltpu.VMEM((16, cells), f32),
            pltpu.VMEM((16 * nb, width), f32),
            pltpu.VMEM((16 * nb, width), f32),
            pltpu.VMEM((8, 8, CHUNK), f32),
            pltpu.VMEM((64, LANES), f32),
            pltpu.VMEM((48, LANES), f32),
            pltpu.VMEM((48, LANES), f32),
            pltpu.VMEM((16, LANES), f32),
            pltpu.VMEM((16, LANES), f32),
            pltpu.VMEM((16, LANES), f32),
            pltpu.VMEM((nb, 16, LANES), f32),
            pltpu.VMEM((nb, 8, LANES), f32),
            pltpu.VMEM((nx, 2, 8, LANES), f32),
            pltpu.VMEM((2, 8, LANES), f32),
            pltpu.VMEM((ny * 2, 8, LANES), f32),
            pltpu.VMEM((8, LANES), f32),
            pltpu.VMEM((nz * 2, 8, LANES), f32),
            dma((8,)),
            dma((48,)),
            dma((2,)),
            dma((2,)),
            dma((4,)),
            dma((4,)),
            dma((nb,)),
            dma((nb,)),
            dma((nb,)),
            dma((nb,)),
            dma((4,)),
            dma((32,)),
            dma,
            dma((nb,)),
            dma((4,)),
            dma((nx,)),
            dma((nx,)),
            dma((ny * 2,)),
            dma((ny * 2,)),
            dma((nz * 2,)),
            dma((nz * 2,)),
        ],
        compiler_params=pltpu.CompilerParams(
            collective_id=0, has_side_effects=True, vmem_limit_bytes=60 * 2**20
        ),
        cost_estimate=pl.CostEstimate(
            flops=80_000_000, bytes_accessed=6_000_000, transcendentals=0
        ),
    )(
        orbitals,
        potential,
        projectors.reshape(3 * 2 * kinds, layers, cells),
        kb_energy,
        proj_count,
    )
    return pl.pallas_call(
        finish,
        out_shape=(
            jax.ShapeDtypeStruct(orbitals.shape, f32),
            jax.ShapeDtypeStruct((groups, groups * nb), f32),
            jax.ShapeDtypeStruct((groups, groups * nb), f32),
        ),
        in_specs=[any_space, vmem],
        out_specs=(any_space, vmem, vmem),
        scratch_shapes=[pltpu.VMEM(orbitals.shape, f32), dma((8,))],
        compiler_params=pltpu.CompilerParams(vmem_limit_bytes=60 * 2**20),
        cost_estimate=pl.CostEstimate(flops=0, bytes_accessed=900_000, transcendentals=0),
    )(full, sums)


def solution(mesh):
    ny = 4 if mesh.shape["grid"] == 64 else 1
    dims = (mesh.shape["band"] // 2, ny, mesh.shape["grid"] // (2 * ny))
    in_specs = (
        P("band", "grid", None),
        P("grid", None),
        P(None, None, None, "grid", None),
        P("grid", None, None),
        P("grid", None),
    )
    out_specs = (P("band", "grid", None), P("band", None), P("band", None))
    return jax.shard_map(
        functools.partial(shards, dims),
        mesh=mesh,
        in_specs=in_specs,
        out_specs=out_specs,
        check_vma=False,
    )
```

```python
import functools

import jax
import jax.numpy as jnp
from jax import lax
from jax.experimental import pallas as pl
from jax.experimental.pallas import tpu as pltpu
from jax.sharding import PartitionSpec as P

NY = 80
STENCIL = (-205.0 / 72.0, 8.0 / 5.0, -1.0 / 5.0, 8.0 / 315.0, -1.0 / 560.0)
MESH = pl.DeviceIdType.MESH
LANES = 128
PAD = 384
CHUNK = 640
WIDE = 1280


def iota(rows, cols):
    return (
        lax.broadcasted_iota(jnp.int32, (rows, cols), 0),
        lax.broadcasted_iota(jnp.int32, (rows, cols), 1),
    )


def ones_where(condition):
    return jnp.where(condition, 1.0, 0.0).astype(jnp.float32)


def dot(a, b, dims):
    return lax.dot_general(
        a,
        b,
        (dims, ((), ())),
        precision=lax.Precision.HIGHEST,
        preferred_element_type=jnp.float32,
    )


NN = ((1,), (0,))
NT = ((1,), (1,))
TN = ((0,), (0,))


def z_matrix():
    row, col = iota(16, 48)
    same = ((row >> 2) & 3) == ((col >> 2) & 3)
    diff = (col >> 4) * 4 + (col & 3) - 4 - (row & 3)
    dist = jnp.abs(diff)
    value = jnp.zeros((16, 48), jnp.float32)
    for k in range(1, 5):
        value = jnp.where(dist == k, -0.5 * STENCIL[k], value)
    return jnp.where(same, value, 0.0)


def kernel(
    dims,
    psi_in,
    pot_in,
    table_in,
    energy_in,
    count_in,
    h_out,
    sums_out,
    psi,
    before,
    after,
    pot,
    table,
    energy,
    count,
    h,
    full,
    got_psi,
    got_h,
    got_next,
    ycoef,
    part,
    low1,
    high1,
    low2,
    high2,
    owner,
    owners,
    terms,
    x_terms,
    x_sum,
    y_terms,
    y_sum,
    z_terms,
    in_sem,
    table_sem,
    halo_send,
    halo_recv,
    part_send,
    part_recv,
    psi_send,
    psi_recv,
    h_send,
    h_recv,
    extra_send,
    extra_recv,
    next_send,
    next_recv,
    owner_send,
    owner_recv,
    out_sem,
    x_send,
    x_recv,
    y_send,
    y_recv,
    z_send,
    z_recv,
):
    nx, ny, nz = dims
    nb, ng = nx * 2, ny * nz * 2
    cells = pot_in.shape[1]
    per = (cells // LANES) // nb
    share = per * LANES
    me_g = lax.axis_index("grid")
    me_b = lax.axis_index("band")
    my_x, my_h = me_b // 2, me_b % 2
    my_c, my_z, my_y = me_g % 2, (me_g // 2) % nz, me_g // (2 * nz)

    extras = [(per * nb + i, (0, nx + 1)[i]) for i in range(cells // LANES - per * nb)]
    far_x = sorted(range(nx), key=lambda dx: -min(dx, nx - dx))
    far_z = sorted(range(nz), key=lambda dz: -min(dz, nz - dz))
    band_offsets = [(dx, dh) for dh in (1, 0) for dx in far_x if (dx, dh) != (0, 0)]
    x_offsets = [dx for dx in far_x if dx]
    y_offsets = [(dh, dy) for dh in (1, 0) for dy in range(ny) if (dh, dy) != (0, 0)]
    z_offsets = [(dz, dc) for dz in far_z for dc in (1, 0) if (dz, dc) != (0, 0)]
    root = me_g % nb

    def band_peer(dx, dh):
        return ((my_x + dx) % nx) * 2 + (my_h + dh) % 2

    def y_peer(dh, dy):
        peer_g = (((my_y + dy) % ny) * nz + my_z) * 2 + my_c
        return peer_g, my_x * 2 + (my_h + dh) % 2

    def z_peer(dz, dc):
        return (my_y * nz + (my_z + dz) % nz) * 2 + (my_c + dc) % 2, me_b

    def grid_peer(step):
        return (me_g + step + ng) % ng

    barrier = pltpu.get_barrier_semaphore()
    peers = 0
    for dx, dh in band_offsets:
        pl.semaphore_signal(
            barrier, inc=1, device_id=(me_g, band_peer(dx, dh)), device_id_type=MESH
        )
        peers += 1
    for step in (1, -1, 2, -2):
        pl.semaphore_signal(
            barrier, inc=1, device_id=(grid_peer(step), me_b), device_id_type=MESH
        )
        peers += 1
    for peer in [y_peer(dh, dy) for dh, dy in y_offsets] + [
        z_peer(dz, dc) for dz, dc in z_offsets
    ]:
        pl.semaphore_signal(barrier, inc=1, device_id=peer, device_id_type=MESH)
        peers += 1

    loads = [
        pltpu.make_async_copy(
            psi_in.at[b], psi.at[pl.ds(4 * b, 4), pl.ds(PAD, cells)], in_sem.at[b]
        )
        for b in range(4)
    ]
    pot_loads = [
        pltpu.make_async_copy(pot_in, pot.at[pl.ds(4 * b, 4), :], in_sem.at[4 + b])
        for b in range(2)
    ]
    for copy in loads:
        copy.start()
    small_loads = pot_loads + [
        pltpu.make_async_copy(energy_in, energy, in_sem.at[6]),
        pltpu.make_async_copy(count_in, count, in_sem.at[7]),
    ]
    for copy in small_loads:
        copy.start()

    def table_copy(i):
        return pltpu.make_async_copy(
            table_in.at[i], table.at[pl.ds(pl.multiple_of(4 * i, 4), 4), :], table_sem.at[i]
        )

    @pl.loop(0, 48)
    def _(i):
        table_copy(i).start()

    psi[:, 0:PAD] = jnp.zeros((16, PAD), jnp.float32)
    psi[:, PAD + cells : PAD + cells + PAD] = jnp.zeros((16, PAD), jnp.float32)

    @pl.when((me_b != extras[0][1]) & (me_b != extras[1][1]))
    def _():
        got_psi[:, share : share + LANES] = jnp.zeros((16 * nb, LANES), jnp.float32)
        got_h[:, share : share + LANES] = jnp.zeros((16 * nb, LANES), jnp.float32)
        got_next[:, share : share + LANES] = jnp.zeros((16 * nb, LANES), jnp.float32)

    @pl.when(me_b != root)
    def _():
        owners[...] = jnp.zeros(owners.shape, jnp.float32)


    _, lane = iota(8, CHUNK)
    turn = jnp.zeros((8, CHUNK), jnp.int32)
    for m in range(1, CHUNK // NY):
        turn = turn + jnp.where(lane >= m * NY, 1, 0)
    column = lane - turn * NY
    for k in range(1, 5):
        ycoef[k - 1] = jnp.where(column + k < NY, -0.5 * STENCIL[k], 0.0)
        ycoef[3 + k] = jnp.where(column >= k, -0.5 * STENCIL[k], 0.0)

    for copy in loads:
        copy.wait()
    pl.semaphore_wait(barrier, peers)

    my_rows = pl.ds(pl.multiple_of(me_b * 16, 16), 16)

    def spread(source, base, target, send, recv, which):
        copies = []
        for i, (dx, dh) in enumerate(band_offsets):
            peer = band_peer(dx, dh)
            start = pl.multiple_of(base + peer * share, LANES)
            copy = pltpu.make_async_remote_copy(
                src_ref=source.at[:, pl.ds(start, share)],
                dst_ref=target.at[my_rows, pl.ds(0, share)],
                send_sem=send.at[i],
                recv_sem=recv.at[i],
                device_id=(me_g, peer),
                device_id_type=MESH,
            )
            copy.start()
            copies.append(copy)
        for i, (tile, owner) in enumerate(extras):

            @pl.when(me_b != owner)
            def _(i=i, tile=tile, owner=owner):
                extra_copy(source, base, target, which, i, tile, owner, me_b).start()

        return copies

    def extra_copy(source, base, target, which, i, tile, owner, sem):
        return pltpu.make_async_remote_copy(
            src_ref=source.at[:, pl.ds(base + tile * LANES, LANES)],
            dst_ref=target.at[my_rows, pl.ds(share, LANES)],
            send_sem=extra_send.at[which * 2 + i],
            recv_sem=extra_recv.at[which * 16 + sem],
            device_id=(me_g, owner),
            device_id_type=MESH,
        )

    def keep_own(source, base, target):
        start = pl.multiple_of(base + me_b * share, LANES)
        target[my_rows, 0:share] = source[:, pl.ds(start, share)]
        for tile, owner in extras:

            @pl.when(me_b == owner)
            def _(tile=tile):
                target[my_rows, share : share + LANES] = source[
                    :, base + tile * LANES : base + (tile + 1) * LANES
                ]

    def await_spread(copies, source, base, target, which):
        for copy in copies:
            copy.wait_recv()
        for i, (tile, owner) in enumerate(extras):

            @pl.when(me_b == owner)
            def _(i=i, tile=tile, owner=owner):
                for other in range(nb):
                    if other != owner:
                        extra_copy(
                            source, base, target, which, i, tile, owner, other
                        ).wait_recv()

    def await_sent(copies, source, base, target, which):
        for copy in copies:
            copy.wait_send()
        for i, (tile, owner) in enumerate(extras):

            @pl.when(me_b != owner)
            def _(i=i, tile=tile, owner=owner):
                extra_copy(source, base, target, which, i, tile, owner, me_b).wait_send()

    psi_copies = spread(psi, PAD, got_psi, psi_send, psi_recv, 0)

    halo = []
    for i, (step, target) in enumerate(((1, before), (-1, after))):
        copy = pltpu.make_async_remote_copy(
            src_ref=psi.at[:, pl.ds(PAD, cells)],
            dst_ref=target,
            send_sem=halo_send.at[i],
            recv_sem=halo_recv.at[i],
            device_id=(grid_peer(step), me_b),
            device_id_type=MESH,
        )
        copy.start()
        halo.append(copy)

    for copy in small_loads:
        copy.wait()

    @pl.loop(0, cells // CHUNK)
    def _(i):
        start = pl.multiple_of(i * CHUNK, LANES)
        wide = psi[:, pl.ds(start, CHUNK + 2 * PAD)]

        def shifted(offset):
            return wide[:, PAD + offset : PAD + offset + CHUNK]

        here = pot[:, pl.ds(start, CHUNK)] + (-1.5 * STENCIL[0])
        total = jnp.concatenate([here, here], axis=0) * shifted(0)
        for k in range(1, 5):
            total = total + (-0.5 * STENCIL[k]) * (shifted(NY * k) + shifted(-NY * k))
            up, down = ycoef[k - 1], ycoef[3 + k]
            total = total + jnp.concatenate([up, up], axis=0) * shifted(k)
            total = total + jnp.concatenate([down, down], axis=0) * shifted(-k)
        h[:, pl.ds(start, CHUNK)] = total

    h_copies = spread(h, 0, got_h, h_send, h_recv, 1)
    keep_own(h, 0, got_h)

    keep_own(psi, PAD, got_psi)

    @pl.loop(0, 48)
    def _(i):
        table_copy(i).wait()

    def partial_step(i, total):
        start = pl.multiple_of(i * WIDE, LANES)
        return total + dot(
            table[:, pl.ds(start, WIDE)], psi[:, pl.ds(start + PAD, WIDE)], NT
        )

    raw = lax.fori_loop(0, cells // WIDE, partial_step, jnp.zeros((192, 16), jnp.float32))
    row, col = iota(192, 16)
    raw = jnp.where((row & 3) == (col & 3), raw, 0.0)
    row, col = iota(64, 192)
    source_row = jnp.where(row < 32, row, jnp.where(row < 48, -1, row - 16))
    gather = ones_where(source_row == (col >> 2))
    row, col = iota(16, LANES)
    widen = ones_where((row >> 2) == (col >> 2))
    sums = dot(dot(gather, raw, NN), widen, NN)
    part[...] = sums
    row, col = iota(16, 8)
    kinds = jnp.concatenate(
        [jnp.broadcast_to(energy[0, a : a + 1, :], (8, 8)) for a in range(2)], axis=0
    )
    active = jnp.concatenate(
        [jnp.broadcast_to(count[0:1, a : a + 1], (8, 8)) for a in range(2)], axis=0
    )
    chosen = jnp.where((col == (row & 7)) & (col < active), kinds, 0.0)
    weight = jnp.broadcast_to(jnp.sum(chosen, axis=1, keepdims=True), (16, LANES))
    part[32:48, :] = weight

    part_copies = []
    for i, (step, first, count, target) in enumerate(
        ((1, 16, 48, low1), (-1, 0, 48, high1), (2, 48, 16, low2), (-2, 0, 16, high2))
    ):
        copy = pltpu.make_async_remote_copy(
            src_ref=part.at[pl.ds(first, count), :],
            dst_ref=target,
            send_sem=part_send.at[i],
            recv_sem=part_recv.at[i],
            device_id=(grid_peer(step), me_b),
            device_id_type=MESH,
        )
        copy.start()
        part_copies.append(copy)

    for copy in halo:
        copy.wait_recv()
    across = z_matrix()

    @pl.loop(0, cells // WIDE)
    def _(i):
        start = pl.multiple_of(i * WIDE, LANES)
        here = pl.ds(start, WIDE)
        planes = jnp.concatenate(
            [before[:, here], psi[:, pl.ds(start + PAD, WIDE)], after[:, here]], axis=0
        )
        full[:, here] = h[:, here] + dot(across, planes, NN)

    for copy in part_copies:
        copy.wait_recv()
    total = part[16:32, :] + high1[0:16, :] + low1[32:48, :]
    coef = jnp.concatenate(
        [
            low1[16:32, :] * (low1[0:16, :] + part[0:16, :] + low2[...]),
            weight * total,
            high1[32:48, :] * (high1[16:32, :] + high2[...] + part[48:64, :]),
        ],
        axis=0,
    )

    row, col = iota(LANES, LANES)
    place = ones_where((row < 16) & ((row & 3) == 0) & (col == me_b * 4 + (row >> 2)))
    owner[...] = dot(total, place, NN)

    def owner_copy(sem):
        return pltpu.make_async_remote_copy(
            src_ref=owner,
            dst_ref=owners.at[me_b],
            send_sem=owner_send,
            recv_sem=owner_recv.at[sem],
            device_id=(me_g, root),
            device_id_type=MESH,
        )

    @pl.when(me_b != root)
    def _():
        owner_copy(me_b).start()

    @pl.when(me_b == root)
    def _():
        owners[me_b] = owner[...]

    await_spread(psi_copies, psi, PAD, got_psi, 0)

    def next_copy(first, width, sem):
        return pltpu.make_async_remote_copy(
            src_ref=got_psi.at[:, pl.ds(first, width)],
            dst_ref=got_next.at[:, pl.ds(first, width)],
            send_sem=next_send.at[sem],
            recv_sem=next_recv.at[sem],
            device_id=(grid_peer(-1), me_b),
            device_id_type=MESH,
        )

    holds_extra = (me_b == extras[0][1]) | (me_b == extras[1][1])
    next_copy(0, share, 0).start()

    @pl.when(holds_extra)
    def _():
        next_copy(share, LANES, 1).start()

    row, col = iota(48, 192)
    repeat = ones_where(row == (col >> 2))
    spread_coef = dot(coef, repeat, TN)[0:16, :]
    row, col = iota(16, 192)
    spread_coef = jnp.where((row & 3) == (col & 3), spread_coef, 0.0)

    @pl.loop(0, cells // WIDE)
    def _(i):
        start = pl.multiple_of(i * WIDE, LANES)
        here = pl.ds(start, WIDE)
        full[:, here] = full[:, here] + dot(spread_coef, table[:, here], NN)

    stores = [
        pltpu.make_async_copy(full.at[pl.ds(4 * b, 4), :], h_out.at[b], out_sem.at[b])
        for b in range(4)
    ]
    for copy in stores:
        copy.start()

    @pl.when(me_b == root)
    def _():
        for other in range(nb):

            @pl.when(other != me_b)
            def _(other=other):
                owner_copy(other).wait_recv()

    projections = jnp.sum(owners[...], axis=0)
    nonlocal_gram = dot(projections * weight, projections, TN)

    rows = 16 * nb
    row, col = iota(8 * nb, rows)
    band_of = (row >> 3) * 4 + (row & 3)
    pick_corr = ones_where(((row & 4) == 0) & (band_of == (col >> 2)))
    pick_gram = ones_where(((row & 4) == 4) & (band_of == (col >> 2)))
    row, col = iota(8 * nb, LANES)
    band_of = (row >> 3) * 4 + (row & 3)
    pick_nonlocal = ones_where(((row & 4) == 4) & (band_of == col))
    row, col = iota(rows, LANES)
    narrow = ones_where((row >> 2) == col)
    row, col = iota(rows, rows)
    same_plane = (row & 3) == (col & 3)
    apart = jnp.abs((row & 3) - (col & 3))
    above = (col & 3) + 4 - (row & 3)
    below = (row & 3) + 4 - (col & 3)

    def coupled(distance):
        value = jnp.zeros((rows, rows), jnp.float32)
        for k in range(1, 5):
            value = jnp.where(distance == k, -0.5 * STENCIL[k], value)
        return value

    bands = got_psi[...]
    pairs = dot(bands, bands, NT)
    corr = jnp.where(same_plane, pairs, 0.0)
    early = dot(pick_nonlocal, nonlocal_gram, NN) + dot(dot(pick_corr, corr, NN), narrow, NN)
    across_gram = coupled(apart) * pairs
    next_copy(0, share, 0).wait_recv()

    @pl.when(holds_extra)
    def _():
        next_copy(share, LANES, 1).wait_recv()

    following = got_next[...]
    across_gram = across_gram + coupled(above) * dot(bands, following, NT)
    across_gram = across_gram + coupled(below) * dot(following, bands, NT)
    await_spread(h_copies, h, 0, got_h, 1)
    gram = jnp.where(same_plane, dot(got_h[...], bands, NT), 0.0) + across_gram
    blocks = early + dot(dot(pick_gram, gram, NN), narrow, NN)
    terms[...] = blocks.reshape(nb, 8, LANES)

    def exchange(source_of, target, slot, peers_, send, recv):
        copies = []
        for i, peer in enumerate(peers_):
            copy = pltpu.make_async_remote_copy(
                src_ref=source_of(i),
                dst_ref=target.at[slot],
                send_sem=send.at[i],
                recv_sem=recv.at[i],
                device_id=peer,
                device_id_type=MESH,
            )
            copy.start()
            copies.append(copy)
        return copies

    x_copies = exchange(
        lambda i: terms.at[pl.ds(((my_x + x_offsets[i]) % nx) * 2, 2)],
        x_terms,
        my_x,
        [(me_g, band_peer(dx, 0)) for dx in x_offsets],
        x_send,
        x_recv,
    )
    x_terms[my_x] = terms[pl.ds(my_x * 2, 2)]
    for copy in x_copies:
        copy.wait_recv()
    x_sum[...] = jnp.sum(x_terms[...], axis=0)

    slot = my_h * ny + my_y
    y_copies = exchange(
        lambda i: x_sum.at[(my_h + y_offsets[i][0]) % 2],
        y_terms,
        slot,
        [y_peer(dh, dy) for dh, dy in y_offsets],
        y_send,
        y_recv,
    )
    y_terms[slot] = x_sum[my_h]
    for copy in y_copies:
        copy.wait_recv()
    y_sum[...] = jnp.sum(y_terms[...], axis=0)

    slot = my_z * 2 + my_c
    z_copies = exchange(
        lambda i: y_sum,
        z_terms,
        slot,
        [z_peer(dz, dc) for dz, dc in z_offsets],
        z_send,
        z_recv,
    )
    z_terms[slot] = y_sum[...]
    for copy in z_copies:
        copy.wait_recv()
    sums_out[...] = jnp.sum(z_terms[...], axis=0) * (1.0 / (4 * cells * ng))

    for copy in halo + part_copies + x_copies + y_copies + z_copies:
        copy.wait_send()
    await_sent(psi_copies, psi, PAD, got_psi, 0)
    await_sent(h_copies, h, 0, got_h, 1)

    next_copy(0, share, 0).wait_send()

    @pl.when(holds_extra)
    def _():
        next_copy(share, LANES, 1).wait_send()

    @pl.when(me_b != root)
    def _():
        owner_copy(me_b).wait_send()

    for copy in stores:
        copy.wait()


def finish(h_in, sums_in, h_out, corr_out, gram_out, held, sums, corr, gram, sem):
    ins = [pltpu.make_async_copy(h_in.at[b], held.at[b], sem.at[b]) for b in range(4)]
    outs = [pltpu.make_async_copy(held.at[b], h_out.at[b], sem.at[4 + b]) for b in range(4)]
    sums_copy = pltpu.make_async_copy(sums_in, sums, sem.at[8])
    outs.append(pltpu.make_async_copy(corr, corr_out, sem.at[9]))
    outs.append(pltpu.make_async_copy(gram, gram_out, sem.at[10]))
    sums_copy.start()
    for copy in ins:
        copy.start()
    width = corr_out.shape[1]
    sums_copy.wait()
    corr[...] = sums[0:4, 0:width]
    gram[...] = sums[4:8, 0:width]
    for copy in ins:
        copy.wait()
    for copy in outs:
        copy.start()
    for copy in outs:
        copy.wait()


def shards(dims, orbitals, potential, projectors, kb_energy, proj_count):
    groups, layers, cells = orbitals.shape
    nx, ny, nz = dims
    nb = nx * 2
    kinds = projectors.shape[2]
    width = ((cells // LANES) // nb + 1) * LANES
    f32 = jnp.float32
    any_space = pl.BlockSpec(memory_space=pl.ANY)
    vmem = pl.BlockSpec(memory_space=pltpu.VMEM)
    dma = pltpu.SemaphoreType.DMA
    full, sums = pl.pallas_call(
        functools.partial(kernel, dims),
        out_shape=(
            jax.ShapeDtypeStruct(orbitals.shape, f32),
            jax.ShapeDtypeStruct((8, LANES), f32),
        ),
        in_specs=[any_space] * 5,
        out_specs=(any_space, vmem),
        scratch_shapes=[
            pltpu.VMEM((16, cells + 2 * PAD), f32),
            pltpu.VMEM((16, cells), f32),
            pltpu.VMEM((16, cells), f32),
            pltpu.VMEM((8, cells), f32),
            pltpu.VMEM((192, cells), f32),
            pltpu.VMEM(kb_energy.shape, f32),
            pltpu.VMEM(proj_count.shape, jnp.int32),
            pltpu.VMEM((16, cells), f32),
            pltpu.VMEM((16, cells), f32),
            pltpu.VMEM((16 * nb, width), f32),
            pltpu.VMEM((16 * nb, width), f32),
            pltpu.VMEM((16 * nb, width), f32),
            pltpu.VMEM((8, 8, CHUNK), f32),
            pltpu.VMEM((64, LANES), f32),
            pltpu.VMEM((48, LANES), f32),
            pltpu.VMEM((48, LANES), f32),
            pltpu.VMEM((16, LANES), f32),
            pltpu.VMEM((16, LANES), f32),
            pltpu.VMEM((16, LANES), f32),
            pltpu.VMEM((nb, 16, LANES), f32),
            pltpu.VMEM((nb, 8, LANES), f32),
            pltpu.VMEM((nx, 2, 8, LANES), f32),
            pltpu.VMEM((2, 8, LANES), f32),
            pltpu.VMEM((ny * 2, 8, LANES), f32),
            pltpu.VMEM((8, LANES), f32),
            pltpu.VMEM((nz * 2, 8, LANES), f32),
            dma((8,)),
            dma((48,)),
            dma((2,)),
            dma((2,)),
            dma((4,)),
            dma((4,)),
            dma((nb,)),
            dma((nb,)),
            dma((nb,)),
            dma((nb,)),
            dma((4,)),
            dma((32,)),
            dma((2,)),
            dma((2,)),
            dma,
            dma((nb,)),
            dma((4,)),
            dma((nx,)),
            dma((nx,)),
            dma((ny * 2,)),
            dma((ny * 2,)),
            dma((nz * 2,)),
            dma((nz * 2,)),
        ],
        compiler_params=pltpu.CompilerParams(
            collective_id=0, has_side_effects=True, vmem_limit_bytes=60 * 2**20
        ),
        cost_estimate=pl.CostEstimate(
            flops=80_000_000, bytes_accessed=6_000_000, transcendentals=0
        ),
    )(
        orbitals,
        potential,
        projectors.reshape(3 * 2 * kinds, layers, cells),
        kb_energy,
        proj_count,
    )
    return pl.pallas_call(
        finish,
        out_shape=(
            jax.ShapeDtypeStruct(orbitals.shape, f32),
            jax.ShapeDtypeStruct((groups, groups * nb), f32),
            jax.ShapeDtypeStruct((groups, groups * nb), f32),
        ),
        in_specs=[any_space, any_space],
        out_specs=(any_space, any_space, any_space),
        scratch_shapes=[
            pltpu.VMEM(orbitals.shape, f32),
            pltpu.VMEM((8, LANES), f32),
            pltpu.VMEM((groups, groups * nb), f32),
            pltpu.VMEM((groups, groups * nb), f32),
            dma((11,)),
        ],
        compiler_params=pltpu.CompilerParams(vmem_limit_bytes=60 * 2**20),
        cost_estimate=pl.CostEstimate(flops=0, bytes_accessed=900_000, transcendentals=0),
    )(full, sums)


def solution(mesh):
    ny = 4 if mesh.shape["grid"] == 64 else 1
    dims = (mesh.shape["band"] // 2, ny, mesh.shape["grid"] // (2 * ny))
    in_specs = (
        P("band", "grid", None),
        P("grid", None),
        P(None, None, None, "grid", None),
        P("grid", None, None),
        P("grid", None),
    )
    out_specs = (P("band", "grid", None), P("band", None), P("band", None))
    return jax.shard_map(
        functools.partial(shards, dims),
        mesh=mesh,
        in_specs=in_specs,
        out_specs=out_specs,
        check_vma=False,
    )
```

```python
import functools

import jax
import jax.numpy as jnp
from jax import lax
from jax.experimental import pallas as pl
from jax.experimental.pallas import tpu as pltpu
from jax.sharding import PartitionSpec as P

NY = 80
STENCIL = (-205.0 / 72.0, 8.0 / 5.0, -1.0 / 5.0, 8.0 / 315.0, -1.0 / 560.0)
MESH = pl.DeviceIdType.MESH
LANES = 128
PAD = 384
CHUNK = 640
WIDE = 1280


def iota(rows, cols):
    return (
        lax.broadcasted_iota(jnp.int32, (rows, cols), 0),
        lax.broadcasted_iota(jnp.int32, (rows, cols), 1),
    )


def ones_where(condition):
    return jnp.where(condition, 1.0, 0.0).astype(jnp.float32)


def dot(a, b, dims):
    return lax.dot_general(
        a,
        b,
        (dims, ((), ())),
        precision=lax.Precision.HIGHEST,
        preferred_element_type=jnp.float32,
    )


NN = ((1,), (0,))
NT = ((1,), (1,))
TN = ((0,), (0,))


def z_matrix():
    row, col = iota(16, 48)
    same = ((row >> 2) & 3) == ((col >> 2) & 3)
    diff = (col >> 4) * 4 + (col & 3) - 4 - (row & 3)
    dist = jnp.abs(diff)
    value = jnp.zeros((16, 48), jnp.float32)
    for k in range(1, 5):
        value = jnp.where(dist == k, -0.5 * STENCIL[k], value)
    return jnp.where(same, value, 0.0)


def kernel(
    dims,
    psi_in,
    pot_in,
    table_in,
    energy_in,
    count_in,
    h_out,
    sums_out,
    psi,
    before,
    after,
    pot,
    table,
    energy,
    count,
    h,
    full,
    got_psi,
    got_h,
    got_next,
    ycoef,
    part,
    low1,
    high1,
    low2,
    high2,
    owner,
    owners,
    terms,
    x_terms,
    x_sum,
    y_terms,
    y_sum,
    z_terms,
    in_sem,
    table_sem,
    halo_send,
    halo_recv,
    part_send,
    part_recv,
    psi_send,
    psi_recv,
    h_send,
    h_recv,
    extra_send,
    extra_recv,
    next_send,
    next_recv,
    owner_send,
    owner_recv,
    out_sem,
    x_send,
    x_recv,
    y_send,
    y_recv,
    z_send,
    z_recv,
):
    nx, ny, nz = dims
    nb, ng = nx * 2, ny * nz * 2
    cells = pot_in.shape[1]
    per = (cells // LANES) // nb
    share = per * LANES
    me_g = lax.axis_index("grid")
    me_b = lax.axis_index("band")
    my_x, my_h = me_b // 2, me_b % 2
    my_c, my_z, my_y = me_g % 2, (me_g // 2) % nz, me_g // (2 * nz)

    extras = [(per * nb + i, (0, nx + 1)[i]) for i in range(cells // LANES - per * nb)]
    far_x = sorted(range(nx), key=lambda dx: -min(dx, nx - dx))
    far_z = sorted(range(nz), key=lambda dz: -min(dz, nz - dz))
    band_offsets = [(dx, dh) for dh in (1, 0) for dx in far_x if (dx, dh) != (0, 0)]
    x_offsets = [dx for dx in far_x if dx]
    y_offsets = [(dh, dy) for dh in (1, 0) for dy in range(ny) if (dh, dy) != (0, 0)]
    z_offsets = [(dz, dc) for dz in far_z for dc in (1, 0) if (dz, dc) != (0, 0)]
    root = me_g % nb

    def band_peer(dx, dh):
        return ((my_x + dx) % nx) * 2 + (my_h + dh) % 2

    def y_peer(dh, dy):
        peer_g = (((my_y + dy) % ny) * nz + my_z) * 2 + my_c
        return peer_g, my_x * 2 + (my_h + dh) % 2

    def z_peer(dz, dc):
        return (my_y * nz + (my_z + dz) % nz) * 2 + (my_c + dc) % 2, me_b

    def grid_peer(step):
        return (me_g + step + ng) % ng

    barrier = pltpu.get_barrier_semaphore()
    peers = 0
    for dx, dh in band_offsets:
        pl.semaphore_signal(
            barrier, inc=1, device_id=(me_g, band_peer(dx, dh)), device_id_type=MESH
        )
        peers += 1
    for step in (1, -1, 2, -2):
        pl.semaphore_signal(
            barrier, inc=1, device_id=(grid_peer(step), me_b), device_id_type=MESH
        )
        peers += 1
    for peer in [y_peer(dh, dy) for dh, dy in y_offsets] + [
        z_peer(dz, dc) for dz, dc in z_offsets
    ]:
        pl.semaphore_signal(barrier, inc=1, device_id=peer, device_id_type=MESH)
        peers += 1

    loads = [
        pltpu.make_async_copy(
            psi_in.at[b], psi.at[pl.ds(4 * b, 4), pl.ds(PAD, cells)], in_sem.at[b]
        )
        for b in range(4)
    ]
    pot_loads = [
        pltpu.make_async_copy(pot_in, pot.at[pl.ds(4 * b, 4), :], in_sem.at[4 + b])
        for b in range(2)
    ]
    for copy in loads:
        copy.start()
    small_loads = pot_loads + [
        pltpu.make_async_copy(energy_in, energy, in_sem.at[6]),
        pltpu.make_async_copy(count_in, count, in_sem.at[7]),
    ]
    for copy in small_loads:
        copy.start()

    def table_copy(i):
        return pltpu.make_async_copy(
            table_in.at[i], table.at[pl.ds(pl.multiple_of(4 * i, 4), 4), :], table_sem.at[i]
        )

    @pl.loop(0, 48)
    def _(i):
        table_copy(i).start()

    psi[:, 0:PAD] = jnp.zeros((16, PAD), jnp.float32)
    psi[:, PAD + cells : PAD + cells + PAD] = jnp.zeros((16, PAD), jnp.float32)

    @pl.when((me_b != extras[0][1]) & (me_b != extras[1][1]))
    def _():
        got_psi[:, share : share + LANES] = jnp.zeros((16 * nb, LANES), jnp.float32)
        got_h[:, share : share + LANES] = jnp.zeros((16 * nb, LANES), jnp.float32)
        got_next[:, share : share + LANES] = jnp.zeros((16 * nb, LANES), jnp.float32)

    @pl.when(me_b != root)
    def _():
        owners[...] = jnp.zeros(owners.shape, jnp.float32)


    _, lane = iota(8, CHUNK)
    turn = jnp.zeros((8, CHUNK), jnp.int32)
    for m in range(1, CHUNK // NY):
        turn = turn + jnp.where(lane >= m * NY, 1, 0)
    column = lane - turn * NY
    for k in range(1, 5):
        ycoef[k - 1] = jnp.where(column + k < NY, -0.5 * STENCIL[k], 0.0)
        ycoef[3 + k] = jnp.where(column >= k, -0.5 * STENCIL[k], 0.0)

    for copy in loads:
        copy.wait()
    pl.semaphore_wait(barrier, peers)

    my_rows = pl.ds(pl.multiple_of(me_b * 16, 16), 16)

    def spread(source, base, target, send, recv, which):
        copies = []
        for i, (dx, dh) in enumerate(band_offsets):
            peer = band_peer(dx, dh)
            start = pl.multiple_of(base + peer * share, LANES)
            copy = pltpu.make_async_remote_copy(
                src_ref=source.at[:, pl.ds(start, share)],
                dst_ref=target.at[my_rows, pl.ds(0, share)],
                send_sem=send.at[i],
                recv_sem=recv.at[i],
                device_id=(me_g, peer),
                device_id_type=MESH,
            )
            copy.start()
            copies.append(copy)
        for i, (tile, owner) in enumerate(extras):

            @pl.when(me_b != owner)
            def _(i=i, tile=tile, owner=owner):
                extra_copy(source, base, target, which, i, tile, owner, me_b).start()

        return copies

    def extra_copy(source, base, target, which, i, tile, owner, sem):
        return pltpu.make_async_remote_copy(
            src_ref=source.at[:, pl.ds(base + tile * LANES, LANES)],
            dst_ref=target.at[my_rows, pl.ds(share, LANES)],
            send_sem=extra_send.at[which * 2 + i],
            recv_sem=extra_recv.at[which * 16 + sem],
            device_id=(me_g, owner),
            device_id_type=MESH,
        )

    def keep_own(source, base, target):
        start = pl.multiple_of(base + me_b * share, LANES)
        target[my_rows, 0:share] = source[:, pl.ds(start, share)]
        for tile, owner in extras:

            @pl.when(me_b == owner)
            def _(tile=tile):
                target[my_rows, share : share + LANES] = source[
                    :, base + tile * LANES : base + (tile + 1) * LANES
                ]

    def await_spread(copies, source, base, target, which):
        for copy in copies:
            copy.wait_recv()
        for i, (tile, owner) in enumerate(extras):

            @pl.when(me_b == owner)
            def _(i=i, tile=tile, owner=owner):
                for other in range(nb):
                    if other != owner:
                        extra_copy(
                            source, base, target, which, i, tile, owner, other
                        ).wait_recv()

    def await_sent(copies, source, base, target, which):
        for copy in copies:
            copy.wait_send()
        for i, (tile, owner) in enumerate(extras):

            @pl.when(me_b != owner)
            def _(i=i, tile=tile, owner=owner):
                extra_copy(source, base, target, which, i, tile, owner, me_b).wait_send()

    psi_copies = spread(psi, PAD, got_psi, psi_send, psi_recv, 0)

    for copy in small_loads:
        copy.wait()

    @pl.loop(0, cells // CHUNK)
    def _(i):
        start = pl.multiple_of(i * CHUNK, LANES)
        wide = psi[:, pl.ds(start, CHUNK + 2 * PAD)]

        def shifted(offset):
            return wide[:, PAD + offset : PAD + offset + CHUNK]

        here = pot[:, pl.ds(start, CHUNK)] + (-1.5 * STENCIL[0])
        total = jnp.concatenate([here, here], axis=0) * shifted(0)
        for k in range(1, 5):
            total = total + (-0.5 * STENCIL[k]) * (shifted(NY * k) + shifted(-NY * k))
            up, down = ycoef[k - 1], ycoef[3 + k]
            total = total + jnp.concatenate([up, up], axis=0) * shifted(k)
            total = total + jnp.concatenate([down, down], axis=0) * shifted(-k)
        h[:, pl.ds(start, CHUNK)] = total

    h_copies = spread(h, 0, got_h, h_send, h_recv, 1)
    keep_own(h, 0, got_h)

    keep_own(psi, PAD, got_psi)

    @pl.loop(0, 48)
    def _(i):
        table_copy(i).wait()

    def partial_step(i, total):
        start = pl.multiple_of(i * WIDE, LANES)
        return total + dot(
            table[:, pl.ds(start, WIDE)], psi[:, pl.ds(start + PAD, WIDE)], NT
        )

    raw = lax.fori_loop(0, cells // WIDE, partial_step, jnp.zeros((192, 16), jnp.float32))
    row, col = iota(192, 16)
    raw = jnp.where((row & 3) == (col & 3), raw, 0.0)
    row, col = iota(64, 192)
    source_row = jnp.where(row < 32, row, jnp.where(row < 48, -1, row - 16))
    gather = ones_where(source_row == (col >> 2))
    row, col = iota(16, LANES)
    widen = ones_where((row >> 2) == (col >> 2))
    sums = dot(dot(gather, raw, NN), widen, NN)
    part[...] = sums
    row, col = iota(16, 8)
    kinds = jnp.concatenate(
        [jnp.broadcast_to(energy[0, a : a + 1, :], (8, 8)) for a in range(2)], axis=0
    )
    active = jnp.concatenate(
        [jnp.broadcast_to(count[0:1, a : a + 1], (8, 8)) for a in range(2)], axis=0
    )
    chosen = jnp.where((col == (row & 7)) & (col < active), kinds, 0.0)
    weight = jnp.broadcast_to(jnp.sum(chosen, axis=1, keepdims=True), (16, LANES))
    part[32:48, :] = weight

    part_copies = []
    for i, (step, first, count, target) in enumerate(
        ((1, 16, 48, low1), (-1, 0, 48, high1), (2, 48, 16, low2), (-2, 0, 16, high2))
    ):
        copy = pltpu.make_async_remote_copy(
            src_ref=part.at[pl.ds(first, count), :],
            dst_ref=target,
            send_sem=part_send.at[i],
            recv_sem=part_recv.at[i],
            device_id=(grid_peer(step), me_b),
            device_id_type=MESH,
        )
        copy.start()
        part_copies.append(copy)

    await_spread(psi_copies, psi, PAD, got_psi, 0)

    def next_copy(first, width, sem):
        return pltpu.make_async_remote_copy(
            src_ref=got_psi.at[:, pl.ds(first, width)],
            dst_ref=got_next.at[:, pl.ds(first, width)],
            send_sem=next_send.at[sem],
            recv_sem=next_recv.at[sem],
            device_id=(grid_peer(-1), me_b),
            device_id_type=MESH,
        )

    holds_extra = (me_b == extras[0][1]) | (me_b == extras[1][1])
    next_copy(0, share, 0).start()

    @pl.when(holds_extra)
    def _():
        next_copy(share, LANES, 1).start()

    for copy in part_copies:
        copy.wait_recv()
    total = part[16:32, :] + high1[0:16, :] + low1[32:48, :]
    coef = jnp.concatenate(
        [
            low1[16:32, :] * (low1[0:16, :] + part[0:16, :] + low2[...]),
            weight * total,
            high1[32:48, :] * (high1[16:32, :] + high2[...] + part[48:64, :]),
        ],
        axis=0,
    )

    row, col = iota(LANES, LANES)
    place = ones_where((row < 16) & ((row & 3) == 0) & (col == me_b * 4 + (row >> 2)))
    owner[...] = dot(total, place, NN)

    def owner_copy(sem):
        return pltpu.make_async_remote_copy(
            src_ref=owner,
            dst_ref=owners.at[me_b],
            send_sem=owner_send,
            recv_sem=owner_recv.at[sem],
            device_id=(me_g, root),
            device_id_type=MESH,
        )

    @pl.when(me_b != root)
    def _():
        owner_copy(me_b).start()

    @pl.when(me_b == root)
    def _():
        owners[me_b] = owner[...]

    row, col = iota(48, 192)
    repeat = ones_where(row == (col >> 2))
    spread_coef = dot(coef, repeat, TN)[0:16, :]
    row, col = iota(16, 192)
    spread_coef = jnp.where((row & 3) == (col & 3), spread_coef, 0.0)

    halo = []
    for i, (step, target) in enumerate(((1, before), (-1, after))):
        copy = pltpu.make_async_remote_copy(
            src_ref=psi.at[:, pl.ds(PAD, cells)],
            dst_ref=target,
            send_sem=halo_send.at[i],
            recv_sem=halo_recv.at[i],
            device_id=(grid_peer(step), me_b),
            device_id_type=MESH,
        )
        copy.start()
        halo.append(copy)

    rows = 16 * nb
    row, col = iota(8 * nb, rows)
    band_of = (row >> 3) * 4 + (row & 3)
    pick_corr = ones_where(((row & 4) == 0) & (band_of == (col >> 2)))
    pick_gram = ones_where(((row & 4) == 4) & (band_of == (col >> 2)))
    row, col = iota(8 * nb, LANES)
    band_of = (row >> 3) * 4 + (row & 3)
    pick_nonlocal = ones_where(((row & 4) == 4) & (band_of == col))
    row, col = iota(rows, LANES)
    narrow = ones_where((row >> 2) == col)
    row, col = iota(rows, rows)
    same_plane = (row & 3) == (col & 3)
    apart = jnp.abs((row & 3) - (col & 3))
    above = (col & 3) + 4 - (row & 3)
    below = (row & 3) + 4 - (col & 3)

    def coupled(distance):
        value = jnp.zeros((rows, rows), jnp.float32)
        for k in range(1, 5):
            value = jnp.where(distance == k, -0.5 * STENCIL[k], value)
        return value

    bands = got_psi[...]
    pairs = dot(bands, bands, NT)
    corr = jnp.where(same_plane, pairs, 0.0)
    early = dot(dot(pick_corr, corr, NN), narrow, NN)
    across_gram = coupled(apart) * pairs
    await_spread(h_copies, h, 0, got_h, 1)
    gram = jnp.where(same_plane, dot(got_h[...], bands, NT), 0.0) + across_gram
    next_copy(0, share, 0).wait_recv()

    @pl.when(holds_extra)
    def _():
        next_copy(share, LANES, 1).wait_recv()

    following = got_next[...]
    gram = gram + coupled(above) * dot(bands, following, NT)
    gram = gram + coupled(below) * dot(following, bands, NT)
    @pl.when(me_b == root)
    def _():
        for other in range(nb):

            @pl.when(other != me_b)
            def _(other=other):
                owner_copy(other).wait_recv()

    projections = jnp.sum(owners[...], axis=0)
    nonlocal_gram = dot(projections * weight, projections, TN)

    blocks = early + dot(pick_nonlocal, nonlocal_gram, NN)
    blocks = blocks + dot(dot(pick_gram, gram, NN), narrow, NN)
    terms[...] = blocks.reshape(nb, 8, LANES)

    def exchange(source_of, target, slot, peers_, send, recv):
        copies = []
        for i, peer in enumerate(peers_):
            copy = pltpu.make_async_remote_copy(
                src_ref=source_of(i),
                dst_ref=target.at[slot],
                send_sem=send.at[i],
                recv_sem=recv.at[i],
                device_id=peer,
                device_id_type=MESH,
            )
            copy.start()
            copies.append(copy)
        return copies

    x_copies = exchange(
        lambda i: terms.at[pl.ds(((my_x + x_offsets[i]) % nx) * 2, 2)],
        x_terms,
        my_x,
        [(me_g, band_peer(dx, 0)) for dx in x_offsets],
        x_send,
        x_recv,
    )
    x_terms[my_x] = terms[pl.ds(my_x * 2, 2)]
    for copy in x_copies:
        copy.wait_recv()
    x_sum[...] = jnp.sum(x_terms[...], axis=0)

    slot = my_h * ny + my_y
    y_copies = exchange(
        lambda i: x_sum.at[(my_h + y_offsets[i][0]) % 2],
        y_terms,
        slot,
        [y_peer(dh, dy) for dh, dy in y_offsets],
        y_send,
        y_recv,
    )
    y_terms[slot] = x_sum[my_h]

    for copy in halo:
        copy.wait_recv()
    across = z_matrix()

    @pl.loop(0, cells // WIDE)
    def _(i):
        start = pl.multiple_of(i * WIDE, LANES)
        here = pl.ds(start, WIDE)
        planes = jnp.concatenate(
            [before[:, here], psi[:, pl.ds(start + PAD, WIDE)], after[:, here]], axis=0
        )
        full[:, here] = h[:, here] + dot(across, planes, NN)

    for copy in y_copies:
        copy.wait_recv()
    y_sum[...] = jnp.sum(y_terms[...], axis=0)

    slot = my_z * 2 + my_c
    z_copies = exchange(
        lambda i: y_sum,
        z_terms,
        slot,
        [z_peer(dz, dc) for dz, dc in z_offsets],
        z_send,
        z_recv,
    )
    z_terms[slot] = y_sum[...]

    @pl.loop(0, cells // WIDE)
    def _(i):
        start = pl.multiple_of(i * WIDE, LANES)
        here = pl.ds(start, WIDE)
        full[:, here] = full[:, here] + dot(spread_coef, table[:, here], NN)

    stores = [
        pltpu.make_async_copy(full.at[pl.ds(4 * b, 4), :], h_out.at[b], out_sem.at[b])
        for b in range(4)
    ]
    for copy in stores:
        copy.start()

    for copy in z_copies:
        copy.wait_recv()
    sums_out[...] = jnp.sum(z_terms[...], axis=0) * (1.0 / (4 * cells * ng))

    for copy in halo + part_copies + x_copies + y_copies + z_copies:
        copy.wait_send()
    await_sent(psi_copies, psi, PAD, got_psi, 0)
    await_sent(h_copies, h, 0, got_h, 1)

    next_copy(0, share, 0).wait_send()

    @pl.when(holds_extra)
    def _():
        next_copy(share, LANES, 1).wait_send()

    @pl.when(me_b != root)
    def _():
        owner_copy(me_b).wait_send()

    for copy in stores:
        copy.wait()


def finish(h_in, sums_in, h_out, corr_out, gram_out, held, sums, corr, gram, sem):
    ins = [pltpu.make_async_copy(h_in.at[b], held.at[b], sem.at[b]) for b in range(4)]
    outs = [pltpu.make_async_copy(held.at[b], h_out.at[b], sem.at[4 + b]) for b in range(4)]
    sums_copy = pltpu.make_async_copy(sums_in, sums, sem.at[8])
    outs.append(pltpu.make_async_copy(corr, corr_out, sem.at[9]))
    outs.append(pltpu.make_async_copy(gram, gram_out, sem.at[10]))
    sums_copy.start()
    for copy in ins:
        copy.start()
    width = corr_out.shape[1]
    sums_copy.wait()
    corr[...] = sums[0:4, 0:width]
    gram[...] = sums[4:8, 0:width]
    for copy in ins:
        copy.wait()
    for copy in outs:
        copy.start()
    for copy in outs:
        copy.wait()


def shards(dims, orbitals, potential, projectors, kb_energy, proj_count):
    groups, layers, cells = orbitals.shape
    nx, ny, nz = dims
    nb = nx * 2
    kinds = projectors.shape[2]
    width = ((cells // LANES) // nb + 1) * LANES
    f32 = jnp.float32
    any_space = pl.BlockSpec(memory_space=pl.ANY)
    vmem = pl.BlockSpec(memory_space=pltpu.VMEM)
    dma = pltpu.SemaphoreType.DMA
    full, sums = pl.pallas_call(
        functools.partial(kernel, dims),
        out_shape=(
            jax.ShapeDtypeStruct(orbitals.shape, f32),
            jax.ShapeDtypeStruct((8, LANES), f32),
        ),
        in_specs=[any_space] * 5,
        out_specs=(any_space, vmem),
        scratch_shapes=[
            pltpu.VMEM((16, cells + 2 * PAD), f32),
            pltpu.VMEM((16, cells), f32),
            pltpu.VMEM((16, cells), f32),
            pltpu.VMEM((8, cells), f32),
            pltpu.VMEM((192, cells), f32),
            pltpu.VMEM(kb_energy.shape, f32),
            pltpu.VMEM(proj_count.shape, jnp.int32),
            pltpu.VMEM((16, cells), f32),
            pltpu.VMEM((16, cells), f32),
            pltpu.VMEM((16 * nb, width), f32),
            pltpu.VMEM((16 * nb, width), f32),
            pltpu.VMEM((16 * nb, width), f32),
            pltpu.VMEM((8, 8, CHUNK), f32),
            pltpu.VMEM((64, LANES), f32),
            pltpu.VMEM((48, LANES), f32),
            pltpu.VMEM((48, LANES), f32),
            pltpu.VMEM((16, LANES), f32),
            pltpu.VMEM((16, LANES), f32),
            pltpu.VMEM((16, LANES), f32),
            pltpu.VMEM((nb, 16, LANES), f32),
            pltpu.VMEM((nb, 8, LANES), f32),
            pltpu.VMEM((nx, 2, 8, LANES), f32),
            pltpu.VMEM((2, 8, LANES), f32),
            pltpu.VMEM((ny * 2, 8, LANES), f32),
            pltpu.VMEM((8, LANES), f32),
            pltpu.VMEM((nz * 2, 8, LANES), f32),
            dma((8,)),
            dma((48,)),
            dma((2,)),
            dma((2,)),
            dma((4,)),
            dma((4,)),
            dma((nb,)),
            dma((nb,)),
            dma((nb,)),
            dma((nb,)),
            dma((4,)),
            dma((32,)),
            dma((2,)),
            dma((2,)),
            dma,
            dma((nb,)),
            dma((4,)),
            dma((nx,)),
            dma((nx,)),
            dma((ny * 2,)),
            dma((ny * 2,)),
            dma((nz * 2,)),
            dma((nz * 2,)),
        ],
        compiler_params=pltpu.CompilerParams(
            collective_id=0, has_side_effects=True, vmem_limit_bytes=60 * 2**20
        ),
        cost_estimate=pl.CostEstimate(
            flops=80_000_000, bytes_accessed=6_000_000, transcendentals=0
        ),
    )(
        orbitals,
        potential,
        projectors.reshape(3 * 2 * kinds, layers, cells),
        kb_energy,
        proj_count,
    )
    return pl.pallas_call(
        finish,
        out_shape=(
            jax.ShapeDtypeStruct(orbitals.shape, f32),
            jax.ShapeDtypeStruct((groups, groups * nb), f32),
            jax.ShapeDtypeStruct((groups, groups * nb), f32),
        ),
        in_specs=[any_space, any_space],
        out_specs=(any_space, any_space, any_space),
        scratch_shapes=[
            pltpu.VMEM(orbitals.shape, f32),
            pltpu.VMEM((8, LANES), f32),
            pltpu.VMEM((groups, groups * nb), f32),
            pltpu.VMEM((groups, groups * nb), f32),
            dma((11,)),
        ],
        compiler_params=pltpu.CompilerParams(vmem_limit_bytes=60 * 2**20),
        cost_estimate=pl.CostEstimate(flops=0, bytes_accessed=900_000, transcendentals=0),
    )(full, sums)


def solution(mesh):
    ny = 4 if mesh.shape["grid"] == 64 else 1
    dims = (mesh.shape["band"] // 2, ny, mesh.shape["grid"] // (2 * ny))
    in_specs = (
        P("band", "grid", None),
        P("grid", None),
        P(None, None, None, "grid", None),
        P("grid", None, None),
        P("grid", None),
    )
    out_specs = (P("band", "grid", None), P("band", None), P("band", None))
    return jax.shard_map(
        functools.partial(shards, dims),
        mesh=mesh,
        in_specs=in_specs,
        out_specs=out_specs,
        check_vma=False,
    )
```

```python
import functools

import jax
import jax.numpy as jnp
from jax import lax
from jax.experimental import pallas as pl
from jax.experimental.pallas import tpu as pltpu
from jax.sharding import PartitionSpec as P

NY = 80
STENCIL = (-205.0 / 72.0, 8.0 / 5.0, -1.0 / 5.0, 8.0 / 315.0, -1.0 / 560.0)
MESH = pl.DeviceIdType.MESH
LANES = 128
PAD = 384
CHUNK = 640
WIDE = 1280


def iota(rows, cols):
    return (
        lax.broadcasted_iota(jnp.int32, (rows, cols), 0),
        lax.broadcasted_iota(jnp.int32, (rows, cols), 1),
    )


def ones_where(condition):
    return jnp.where(condition, 1.0, 0.0).astype(jnp.float32)


def dot(a, b, dims):
    return lax.dot_general(
        a,
        b,
        (dims, ((), ())),
        precision=lax.Precision.HIGHEST,
        preferred_element_type=jnp.float32,
    )


NN = ((1,), (0,))
NT = ((1,), (1,))
TN = ((0,), (0,))


def z_matrix():
    row, col = iota(16, 48)
    same = ((row >> 2) & 3) == ((col >> 2) & 3)
    diff = (col >> 4) * 4 + (col & 3) - 4 - (row & 3)
    dist = jnp.abs(diff)
    value = jnp.zeros((16, 48), jnp.float32)
    for k in range(1, 5):
        value = jnp.where(dist == k, -0.5 * STENCIL[k], value)
    return jnp.where(same, value, 0.0)


def kernel(
    dims,
    psi_in,
    pot_in,
    table_in,
    energy_in,
    count_in,
    h_out,
    sums_out,
    psi,
    before,
    after,
    pot,
    table,
    energy,
    count,
    h,
    full,
    got_psi,
    got_h,
    got_next,
    ycoef,
    part,
    low1,
    high1,
    low2,
    high2,
    owner,
    owners,
    terms,
    x_terms,
    x_sum,
    y_terms,
    y_sum,
    z_terms,
    in_sem,
    table_sem,
    halo_send,
    halo_recv,
    part_send,
    part_recv,
    psi_send,
    psi_recv,
    h_send,
    h_recv,
    extra_send,
    extra_recv,
    next_send,
    next_recv,
    owner_send,
    owner_recv,
    out_sem,
    x_send,
    x_recv,
    y_send,
    y_recv,
    z_send,
    z_recv,
):
    nx, ny, nz = dims
    nb, ng = nx * 2, ny * nz * 2
    cells = pot_in.shape[1]
    per = (cells // LANES) // nb
    share = per * LANES
    me_g = lax.axis_index("grid")
    me_b = lax.axis_index("band")
    my_x, my_h = me_b // 2, me_b % 2
    my_c, my_z, my_y = me_g % 2, (me_g // 2) % nz, me_g // (2 * nz)

    def extra_owner(i, core):
        return ((i * (nx // 2) + core * max(nx // 4, 1)) % nx) * 2 + i

    extras = [(per * nb + i, extra_owner(i, my_c)) for i in range(cells // LANES - per * nb)]
    far_x = sorted(range(nx), key=lambda dx: -min(dx, nx - dx))
    far_z = sorted(range(nz), key=lambda dz: -min(dz, nz - dz))
    band_offsets = [(dx, dh) for dh in (1, 0) for dx in far_x if (dx, dh) != (0, 0)]
    x_offsets = [dx for dx in far_x if dx]
    y_offsets = [(dh, dy) for dh in (1, 0) for dy in range(ny) if (dh, dy) != (0, 0)]
    z_offsets = [(dz, dc) for dz in far_z for dc in (1, 0) if (dz, dc) != (0, 0)]
    root = me_g % nb

    def band_peer(dx, dh):
        return ((my_x + dx) % nx) * 2 + (my_h + dh) % 2

    def y_peer(dh, dy):
        peer_g = (((my_y + dy) % ny) * nz + my_z) * 2 + my_c
        return peer_g, my_x * 2 + (my_h + dh) % 2

    def z_peer(dz, dc):
        return (my_y * nz + (my_z + dz) % nz) * 2 + (my_c + dc) % 2, me_b

    def grid_peer(step):
        return (me_g + step + ng) % ng

    barrier = pltpu.get_barrier_semaphore()
    peers = 0
    for dx, dh in band_offsets:
        pl.semaphore_signal(
            barrier, inc=1, device_id=(me_g, band_peer(dx, dh)), device_id_type=MESH
        )
        peers += 1
    for step in (1, -1, 2, -2):
        pl.semaphore_signal(
            barrier, inc=1, device_id=(grid_peer(step), me_b), device_id_type=MESH
        )
        peers += 1
    for peer in [y_peer(dh, dy) for dh, dy in y_offsets] + [
        z_peer(dz, dc) for dz, dc in z_offsets
    ]:
        pl.semaphore_signal(barrier, inc=1, device_id=peer, device_id_type=MESH)
        peers += 1

    other_x = (my_x + max(nx // 4, 1) * (1 - 2 * my_c) + nx) % nx
    pl.semaphore_signal(
        barrier,
        inc=1,
        device_id=(grid_peer(1), other_x * 2 + my_h),
        device_id_type=MESH,
    )
    peers += 1

    loads = [
        pltpu.make_async_copy(
            psi_in.at[b], psi.at[pl.ds(4 * b, 4), pl.ds(PAD, cells)], in_sem.at[b]
        )
        for b in range(4)
    ]
    pot_loads = [
        pltpu.make_async_copy(pot_in, pot.at[pl.ds(4 * b, 4), :], in_sem.at[4 + b])
        for b in range(2)
    ]
    for copy in loads:
        copy.start()
    small_loads = pot_loads + [
        pltpu.make_async_copy(energy_in, energy, in_sem.at[6]),
        pltpu.make_async_copy(count_in, count, in_sem.at[7]),
    ]
    for copy in small_loads:
        copy.start()

    def table_copy(i):
        return pltpu.make_async_copy(
            table_in.at[i], table.at[pl.ds(pl.multiple_of(4 * i, 4), 4), :], table_sem.at[i]
        )

    @pl.loop(0, 48)
    def _(i):
        table_copy(i).start()

    psi[:, 0:PAD] = jnp.zeros((16, PAD), jnp.float32)
    psi[:, PAD + cells : PAD + cells + PAD] = jnp.zeros((16, PAD), jnp.float32)

    @pl.when((me_b != extras[0][1]) & (me_b != extras[1][1]))
    def _():
        got_psi[:, share : share + LANES] = jnp.zeros((16 * nb, LANES), jnp.float32)
        got_h[:, share : share + LANES] = jnp.zeros((16 * nb, LANES), jnp.float32)
        got_next[:, share : share + LANES] = jnp.zeros((16 * nb, LANES), jnp.float32)

    @pl.when(me_b != root)
    def _():
        owners[...] = jnp.zeros(owners.shape, jnp.float32)


    _, lane = iota(8, CHUNK)
    turn = jnp.zeros((8, CHUNK), jnp.int32)
    for m in range(1, CHUNK // NY):
        turn = turn + jnp.where(lane >= m * NY, 1, 0)
    column = lane - turn * NY
    for k in range(1, 5):
        ycoef[k - 1] = jnp.where(column + k < NY, -0.5 * STENCIL[k], 0.0)
        ycoef[3 + k] = jnp.where(column >= k, -0.5 * STENCIL[k], 0.0)

    for copy in loads:
        copy.wait()
    pl.semaphore_wait(barrier, peers)

    my_rows = pl.ds(pl.multiple_of(me_b * 16, 16), 16)

    def spread(source, base, target, send, recv, which):
        copies = []
        for i, (dx, dh) in enumerate(band_offsets):
            peer = band_peer(dx, dh)
            start = pl.multiple_of(base + peer * share, LANES)
            copy = pltpu.make_async_remote_copy(
                src_ref=source.at[:, pl.ds(start, share)],
                dst_ref=target.at[my_rows, pl.ds(0, share)],
                send_sem=send.at[i],
                recv_sem=recv.at[i],
                device_id=(me_g, peer),
                device_id_type=MESH,
            )
            copy.start()
            copies.append(copy)
        for i, (tile, owner) in enumerate(extras):

            @pl.when(me_b != owner)
            def _(i=i, tile=tile, owner=owner):
                extra_copy(source, base, target, which, i, tile, owner, me_b).start()

        return copies

    def extra_copy(source, base, target, which, i, tile, owner, sem):
        return pltpu.make_async_remote_copy(
            src_ref=source.at[:, pl.ds(base + tile * LANES, LANES)],
            dst_ref=target.at[my_rows, pl.ds(share, LANES)],
            send_sem=extra_send.at[which * 2 + i],
            recv_sem=extra_recv.at[which * 16 + sem],
            device_id=(me_g, owner),
            device_id_type=MESH,
        )

    def keep_own(source, base, target):
        start = pl.multiple_of(base + me_b * share, LANES)
        target[my_rows, 0:share] = source[:, pl.ds(start, share)]
        for tile, owner in extras:

            @pl.when(me_b == owner)
            def _(tile=tile):
                target[my_rows, share : share + LANES] = source[
                    :, base + tile * LANES : base + (tile + 1) * LANES
                ]

    def await_spread(copies, source, base, target, which):
        for copy in copies:
            copy.wait_recv()
        for i, (tile, owner) in enumerate(extras):

            @pl.when(me_b == owner)
            def _(i=i, tile=tile, owner=owner):
                for other in range(nb):

                    @pl.when(other != owner)
                    def _(other=other):
                        extra_copy(
                            source, base, target, which, i, tile, owner, other
                        ).wait_recv()

    def await_sent(copies, source, base, target, which):
        for copy in copies:
            copy.wait_send()
        for i, (tile, owner) in enumerate(extras):

            @pl.when(me_b != owner)
            def _(i=i, tile=tile, owner=owner):
                extra_copy(source, base, target, which, i, tile, owner, me_b).wait_send()

    psi_copies = spread(psi, PAD, got_psi, psi_send, psi_recv, 0)

    for copy in small_loads:
        copy.wait()

    @pl.loop(0, 48)
    def _(i):
        table_copy(i).wait()

    def partial_step(i, total):
        start = pl.multiple_of(i * WIDE, LANES)
        return total + dot(
            table[:, pl.ds(start, WIDE)], psi[:, pl.ds(start + PAD, WIDE)], NT
        )

    raw = lax.fori_loop(0, cells // WIDE, partial_step, jnp.zeros((192, 16), jnp.float32))
    row, col = iota(192, 16)
    raw = jnp.where((row & 3) == (col & 3), raw, 0.0)
    row, col = iota(64, 192)
    source_row = jnp.where(row < 32, row, jnp.where(row < 48, -1, row - 16))
    gather = ones_where(source_row == (col >> 2))
    row, col = iota(16, LANES)
    widen = ones_where((row >> 2) == (col >> 2))
    sums = dot(dot(gather, raw, NN), widen, NN)
    part[...] = sums
    row, col = iota(16, 8)
    kinds = jnp.concatenate(
        [jnp.broadcast_to(energy[0, a : a + 1, :], (8, 8)) for a in range(2)], axis=0
    )
    active = jnp.concatenate(
        [jnp.broadcast_to(count[0:1, a : a + 1], (8, 8)) for a in range(2)], axis=0
    )
    chosen = jnp.where((col == (row & 7)) & (col < active), kinds, 0.0)
    weight = jnp.broadcast_to(jnp.sum(chosen, axis=1, keepdims=True), (16, LANES))
    part[32:48, :] = weight

    part_copies = []
    for i, (step, first, count, target) in enumerate(
        ((1, 16, 48, low1), (-1, 0, 48, high1), (2, 48, 16, low2), (-2, 0, 16, high2))
    ):
        copy = pltpu.make_async_remote_copy(
            src_ref=part.at[pl.ds(first, count), :],
            dst_ref=target,
            send_sem=part_send.at[i],
            recv_sem=part_recv.at[i],
            device_id=(grid_peer(step), me_b),
            device_id_type=MESH,
        )
        copy.start()
        part_copies.append(copy)

    @pl.loop(0, cells // CHUNK)
    def _(i):
        start = pl.multiple_of(i * CHUNK, LANES)
        wide = psi[:, pl.ds(start, CHUNK + 2 * PAD)]

        def shifted(offset):
            return wide[:, PAD + offset : PAD + offset + CHUNK]

        here = pot[:, pl.ds(start, CHUNK)] + (-1.5 * STENCIL[0])
        total = jnp.concatenate([here, here], axis=0) * shifted(0)
        for k in range(1, 5):
            total = total + (-0.5 * STENCIL[k]) * (shifted(NY * k) + shifted(-NY * k))
            up, down = ycoef[k - 1], ycoef[3 + k]
            total = total + jnp.concatenate([up, up], axis=0) * shifted(k)
            total = total + jnp.concatenate([down, down], axis=0) * shifted(-k)
        h[:, pl.ds(start, CHUNK)] = total

    h_copies = spread(h, 0, got_h, h_send, h_recv, 1)
    keep_own(h, 0, got_h)

    keep_own(psi, PAD, got_psi)

    await_spread(psi_copies, psi, PAD, got_psi, 0)

    def next_copy(first, width, sem, target):
        return pltpu.make_async_remote_copy(
            src_ref=got_psi.at[:, pl.ds(first, width)],
            dst_ref=got_next.at[:, pl.ds(first, width)],
            send_sem=next_send.at[sem],
            recv_sem=next_recv.at[sem],
            device_id=(grid_peer(-1), target),
            device_id_type=MESH,
        )

    def each_extra(act):
        for _, owner in extras:

            @pl.when(me_b == owner)
            def _():
                act(next_copy(share, LANES, 1, other_x * 2 + my_h))

    next_copy(0, share, 0, me_b).start()
    each_extra(lambda copy: copy.start())

    for copy in part_copies:
        copy.wait_recv()
    total = part[16:32, :] + high1[0:16, :] + low1[32:48, :]
    coef = jnp.concatenate(
        [
            low1[16:32, :] * (low1[0:16, :] + part[0:16, :] + low2[...]),
            weight * total,
            high1[32:48, :] * (high1[16:32, :] + high2[...] + part[48:64, :]),
        ],
        axis=0,
    )

    row, col = iota(LANES, LANES)
    place = ones_where((row < 16) & ((row & 3) == 0) & (col == me_b * 4 + (row >> 2)))
    owner[...] = dot(total, place, NN)

    def owner_copy(sem):
        return pltpu.make_async_remote_copy(
            src_ref=owner,
            dst_ref=owners.at[me_b],
            send_sem=owner_send,
            recv_sem=owner_recv.at[sem],
            device_id=(me_g, root),
            device_id_type=MESH,
        )

    @pl.when(me_b != root)
    def _():
        owner_copy(me_b).start()

    @pl.when(me_b == root)
    def _():
        owners[me_b] = owner[...]

    row, col = iota(48, 192)
    repeat = ones_where(row == (col >> 2))
    spread_coef = dot(coef, repeat, TN)[0:16, :]
    row, col = iota(16, 192)
    spread_coef = jnp.where((row & 3) == (col & 3), spread_coef, 0.0)

    rows = 16 * nb
    row, col = iota(8 * nb, rows)
    band_of = (row >> 3) * 4 + (row & 3)
    pick_corr = ones_where(((row & 4) == 0) & (band_of == (col >> 2)))
    pick_gram = ones_where(((row & 4) == 4) & (band_of == (col >> 2)))
    row, col = iota(8 * nb, LANES)
    band_of = (row >> 3) * 4 + (row & 3)
    pick_nonlocal = ones_where(((row & 4) == 4) & (band_of == col))
    row, col = iota(rows, LANES)
    narrow = ones_where((row >> 2) == col)
    row, col = iota(rows, rows)
    same_plane = (row & 3) == (col & 3)
    apart = jnp.abs((row & 3) - (col & 3))
    above = (col & 3) + 4 - (row & 3)

    def coupled(distance):
        value = jnp.zeros((rows, rows), jnp.float32)
        for k in range(1, 5):
            value = jnp.where(distance == k, -0.5 * STENCIL[k], value)
        return value

    bands = got_psi[...]
    pairs = dot(bands, bands, NT)
    corr = jnp.where(same_plane, pairs, 0.0)
    early = dot(dot(pick_corr, corr, NN), narrow, NN)
    across_gram = coupled(apart) * pairs
    await_spread(h_copies, h, 0, got_h, 1)
    gram = jnp.where(same_plane, dot(got_h[...], bands, NT), 0.0) + across_gram
    halo = []
    for i, (step, target) in enumerate(((1, before), (-1, after))):
        copy = pltpu.make_async_remote_copy(
            src_ref=psi.at[:, pl.ds(PAD, cells)],
            dst_ref=target,
            send_sem=halo_send.at[i],
            recv_sem=halo_recv.at[i],
            device_id=(grid_peer(step), me_b),
            device_id_type=MESH,
        )
        copy.start()
        halo.append(copy)

    next_copy(0, share, 0, me_b).wait_recv()
    each_extra(lambda copy: copy.wait_recv())

    following = got_next[...]
    crossing = dot(coupled(above) * dot(bands, following, NT), narrow, NN)
    crossing = dot(narrow, crossing, TN)
    @pl.when(me_b == root)
    def _():
        for other in range(nb):

            @pl.when(other != me_b)
            def _(other=other):
                owner_copy(other).wait_recv()

    projections = jnp.sum(owners[...], axis=0)
    nonlocal_gram = dot(projections * weight, projections, TN)

    blocks = early + dot(pick_nonlocal, nonlocal_gram + crossing, NN)
    blocks = blocks + dot(pick_nonlocal, crossing, NT)
    blocks = blocks + dot(dot(pick_gram, gram, NN), narrow, NN)
    terms[...] = blocks.reshape(nb, 8, LANES)

    def exchange(source_of, target, slot, peers_, send, recv):
        copies = []
        for i, peer in enumerate(peers_):
            copy = pltpu.make_async_remote_copy(
                src_ref=source_of(i),
                dst_ref=target.at[slot],
                send_sem=send.at[i],
                recv_sem=recv.at[i],
                device_id=peer,
                device_id_type=MESH,
            )
            copy.start()
            copies.append(copy)
        return copies

    x_copies = exchange(
        lambda i: terms.at[pl.ds(((my_x + x_offsets[i]) % nx) * 2, 2)],
        x_terms,
        my_x,
        [(me_g, band_peer(dx, 0)) for dx in x_offsets],
        x_send,
        x_recv,
    )
    x_terms[my_x] = terms[pl.ds(my_x * 2, 2)]
    for copy in x_copies:
        copy.wait_recv()
    x_sum[...] = jnp.sum(x_terms[...], axis=0)

    slot = my_h * ny + my_y
    y_copies = exchange(
        lambda i: x_sum.at[(my_h + y_offsets[i][0]) % 2],
        y_terms,
        slot,
        [y_peer(dh, dy) for dh, dy in y_offsets],
        y_send,
        y_recv,
    )
    y_terms[slot] = x_sum[my_h]

    for copy in halo:
        copy.wait_recv()
    across = z_matrix()

    @pl.loop(0, cells // WIDE)
    def _(i):
        start = pl.multiple_of(i * WIDE, LANES)
        here = pl.ds(start, WIDE)
        planes = jnp.concatenate(
            [before[:, here], psi[:, pl.ds(start + PAD, WIDE)], after[:, here]], axis=0
        )
        full[:, here] = h[:, here] + dot(across, planes, NN)

    for copy in y_copies:
        copy.wait_recv()
    y_sum[...] = jnp.sum(y_terms[...], axis=0)

    slot = my_z * 2 + my_c
    z_copies = exchange(
        lambda i: y_sum,
        z_terms,
        slot,
        [z_peer(dz, dc) for dz, dc in z_offsets],
        z_send,
        z_recv,
    )
    z_terms[slot] = y_sum[...]

    @pl.loop(0, cells // WIDE)
    def _(i):
        start = pl.multiple_of(i * WIDE, LANES)
        here = pl.ds(start, WIDE)
        full[:, here] = full[:, here] + dot(spread_coef, table[:, here], NN)

    stores = [
        pltpu.make_async_copy(full.at[pl.ds(4 * b, 4), :], h_out.at[b], out_sem.at[b])
        for b in range(4)
    ]
    for copy in stores:
        copy.start()

    for copy in z_copies:
        copy.wait_recv()
    sums_out[...] = jnp.sum(z_terms[...], axis=0) * (1.0 / (4 * cells * ng))

    for copy in halo + part_copies + x_copies + y_copies + z_copies:
        copy.wait_send()
    await_sent(psi_copies, psi, PAD, got_psi, 0)
    await_sent(h_copies, h, 0, got_h, 1)

    next_copy(0, share, 0, me_b).wait_send()
    each_extra(lambda copy: copy.wait_send())

    @pl.when(me_b != root)
    def _():
        owner_copy(me_b).wait_send()

    for copy in stores:
        copy.wait()


def finish(h_in, sums_in, h_out, corr_out, gram_out, held, sums, corr, gram, sem):
    ins = [pltpu.make_async_copy(h_in.at[b], held.at[b], sem.at[b]) for b in range(4)]
    outs = [pltpu.make_async_copy(held.at[b], h_out.at[b], sem.at[4 + b]) for b in range(4)]
    sums_copy = pltpu.make_async_copy(sums_in, sums, sem.at[8])
    outs.append(pltpu.make_async_copy(corr, corr_out, sem.at[9]))
    outs.append(pltpu.make_async_copy(gram, gram_out, sem.at[10]))
    sums_copy.start()
    for copy in ins:
        copy.start()
    width = corr_out.shape[1]
    sums_copy.wait()
    corr[...] = sums[0:4, 0:width]
    gram[...] = sums[4:8, 0:width]
    for copy in ins:
        copy.wait()
    for copy in outs:
        copy.start()
    for copy in outs:
        copy.wait()


def shards(dims, orbitals, potential, projectors, kb_energy, proj_count):
    groups, layers, cells = orbitals.shape
    nx, ny, nz = dims
    nb = nx * 2
    kinds = projectors.shape[2]
    width = ((cells // LANES) // nb + 1) * LANES
    f32 = jnp.float32
    any_space = pl.BlockSpec(memory_space=pl.ANY)
    vmem = pl.BlockSpec(memory_space=pltpu.VMEM)
    dma = pltpu.SemaphoreType.DMA
    full, sums = pl.pallas_call(
        functools.partial(kernel, dims),
        out_shape=(
            jax.ShapeDtypeStruct(orbitals.shape, f32),
            jax.ShapeDtypeStruct((8, LANES), f32),
        ),
        in_specs=[any_space] * 5,
        out_specs=(any_space, vmem),
        scratch_shapes=[
            pltpu.VMEM((16, cells + 2 * PAD), f32),
            pltpu.VMEM((16, cells), f32),
            pltpu.VMEM((16, cells), f32),
            pltpu.VMEM((8, cells), f32),
            pltpu.VMEM((192, cells), f32),
            pltpu.VMEM(kb_energy.shape, f32),
            pltpu.VMEM(proj_count.shape, jnp.int32),
            pltpu.VMEM((16, cells), f32),
            pltpu.VMEM((16, cells), f32),
            pltpu.VMEM((16 * nb, width), f32),
            pltpu.VMEM((16 * nb, width), f32),
            pltpu.VMEM((16 * nb, width), f32),
            pltpu.VMEM((8, 8, CHUNK), f32),
            pltpu.VMEM((64, LANES), f32),
            pltpu.VMEM((48, LANES), f32),
            pltpu.VMEM((48, LANES), f32),
            pltpu.VMEM((16, LANES), f32),
            pltpu.VMEM((16, LANES), f32),
            pltpu.VMEM((16, LANES), f32),
            pltpu.VMEM((nb, 16, LANES), f32),
            pltpu.VMEM((nb, 8, LANES), f32),
            pltpu.VMEM((nx, 2, 8, LANES), f32),
            pltpu.VMEM((2, 8, LANES), f32),
            pltpu.VMEM((ny * 2, 8, LANES), f32),
            pltpu.VMEM((8, LANES), f32),
            pltpu.VMEM((nz * 2, 8, LANES), f32),
            dma((8,)),
            dma((48,)),
            dma((2,)),
            dma((2,)),
            dma((4,)),
            dma((4,)),
            dma((nb,)),
            dma((nb,)),
            dma((nb,)),
            dma((nb,)),
            dma((4,)),
            dma((32,)),
            dma((2,)),
            dma((2,)),
            dma,
            dma((nb,)),
            dma((4,)),
            dma((nx,)),
            dma((nx,)),
            dma((ny * 2,)),
            dma((ny * 2,)),
            dma((nz * 2,)),
            dma((nz * 2,)),
        ],
        compiler_params=pltpu.CompilerParams(
            collective_id=0, has_side_effects=True, vmem_limit_bytes=60 * 2**20
        ),
        cost_estimate=pl.CostEstimate(
            flops=80_000_000, bytes_accessed=6_000_000, transcendentals=0
        ),
    )(
        orbitals,
        potential,
        projectors.reshape(3 * 2 * kinds, layers, cells),
        kb_energy,
        proj_count,
    )
    return pl.pallas_call(
        finish,
        out_shape=(
            jax.ShapeDtypeStruct(orbitals.shape, f32),
            jax.ShapeDtypeStruct((groups, groups * nb), f32),
            jax.ShapeDtypeStruct((groups, groups * nb), f32),
        ),
        in_specs=[any_space, any_space],
        out_specs=(any_space, any_space, any_space),
        scratch_shapes=[
            pltpu.VMEM(orbitals.shape, f32),
            pltpu.VMEM((8, LANES), f32),
            pltpu.VMEM((groups, groups * nb), f32),
            pltpu.VMEM((groups, groups * nb), f32),
            dma((11,)),
        ],
        compiler_params=pltpu.CompilerParams(vmem_limit_bytes=60 * 2**20),
        cost_estimate=pl.CostEstimate(flops=0, bytes_accessed=900_000, transcendentals=0),
    )(full, sums)


def solution(mesh):
    ny = 4 if mesh.shape["grid"] == 64 else 1
    dims = (mesh.shape["band"] // 2, ny, mesh.shape["grid"] // (2 * ny))
    in_specs = (
        P("band", "grid", None),
        P("grid", None),
        P(None, None, None, "grid", None),
        P("grid", None, None),
        P("grid", None),
    )
    out_specs = (P("band", "grid", None), P("band", None), P("band", None))
    return jax.shard_map(
        functools.partial(shards, dims),
        mesh=mesh,
        in_specs=in_specs,
        out_specs=out_specs,
        check_vma=False,
    )
```

```python
import functools

import jax
import jax.numpy as jnp
from jax import lax
from jax.experimental import pallas as pl
from jax.experimental.pallas import tpu as pltpu
from jax.sharding import PartitionSpec as P

NY = 80
STENCIL = (-205.0 / 72.0, 8.0 / 5.0, -1.0 / 5.0, 8.0 / 315.0, -1.0 / 560.0)
MESH = pl.DeviceIdType.MESH
LANES = 128
PAD = 384
CHUNK = 640
WIDE = 1280


def iota(rows, cols):
    return (
        lax.broadcasted_iota(jnp.int32, (rows, cols), 0),
        lax.broadcasted_iota(jnp.int32, (rows, cols), 1),
    )


def ones_where(condition):
    return jnp.where(condition, 1.0, 0.0).astype(jnp.float32)


def dot(a, b, dims):
    return lax.dot_general(
        a,
        b,
        (dims, ((), ())),
        precision=lax.Precision.HIGHEST,
        preferred_element_type=jnp.float32,
    )


NN = ((1,), (0,))
NT = ((1,), (1,))
TN = ((0,), (0,))


def z_matrix():
    row, col = iota(16, 48)
    same = ((row >> 2) & 3) == ((col >> 2) & 3)
    diff = (col >> 4) * 4 + (col & 3) - 4 - (row & 3)
    dist = jnp.abs(diff)
    value = jnp.zeros((16, 48), jnp.float32)
    for k in range(1, 5):
        value = jnp.where(dist == k, -0.5 * STENCIL[k], value)
    return jnp.where(same, value, 0.0)


def kernel(
    dims,
    psi_in,
    pot_in,
    table_in,
    energy_in,
    count_in,
    h_out,
    sums_out,
    psi,
    before,
    after,
    pot,
    table,
    energy,
    count,
    h,
    full,
    got_psi,
    got_h,
    got_next,
    ycoef,
    part,
    low1,
    high1,
    low2,
    high2,
    owner,
    owners,
    terms,
    x_terms,
    x_sum,
    y_terms,
    y_sum,
    z_terms,
    in_sem,
    table_sem,
    halo_send,
    halo_recv,
    part_send,
    part_recv,
    psi_send,
    psi_recv,
    h_send,
    h_recv,
    extra_send,
    extra_recv,
    next_send,
    next_recv,
    owner_send,
    owner_recv,
    out_sem,
    x_send,
    x_recv,
    y_send,
    y_recv,
    z_send,
    z_recv,
):
    nx, ny, nz = dims
    nb, ng = nx * 2, ny * nz * 2
    cells = pot_in.shape[1]
    per = (cells // LANES) // nb
    share = per * LANES
    me_g = lax.axis_index("grid")
    me_b = lax.axis_index("band")
    my_x, my_h = me_b // 2, me_b % 2
    my_c, my_z, my_y = me_g % 2, (me_g // 2) % nz, me_g // (2 * nz)

    def extra_owner(i, core):
        return ((i * (nx // 2) + core * max(nx // 4, 1)) % nx) * 2 + i

    extras = [(per * nb + i, extra_owner(i, my_c)) for i in range(cells // LANES - per * nb)]
    far_x = sorted(range(nx), key=lambda dx: -min(dx, nx - dx))
    far_z = sorted(range(nz), key=lambda dz: -min(dz, nz - dz))
    band_offsets = [(dx, dh) for dh in (1, 0) for dx in far_x if (dx, dh) != (0, 0)]
    x_offsets = [dx for dx in far_x if dx]
    y_offsets = [(dh, dy) for dh in (1, 0) for dy in range(ny) if (dh, dy) != (0, 0)]
    z_offsets = [(dz, dc) for dz in far_z for dc in (1, 0) if (dz, dc) != (0, 0)]
    root = me_g % nb

    def band_peer(dx, dh):
        return ((my_x + dx) % nx) * 2 + (my_h + dh) % 2

    def y_peer(dh, dy):
        peer_g = (((my_y + dy) % ny) * nz + my_z) * 2 + my_c
        return peer_g, my_x * 2 + (my_h + dh) % 2

    def z_peer(dz, dc):
        return (my_y * nz + (my_z + dz) % nz) * 2 + (my_c + dc) % 2, me_b

    def grid_peer(step):
        return (me_g + step + ng) % ng

    loads = [
        pltpu.make_async_copy(
            psi_in.at[b], psi.at[pl.ds(4 * b, 4), pl.ds(PAD, cells)], in_sem.at[b]
        )
        for b in range(4)
    ]
    for copy in loads:
        copy.start()

    barrier = pltpu.get_barrier_semaphore()
    peers = 0
    for dx, dh in band_offsets:
        pl.semaphore_signal(
            barrier, inc=1, device_id=(me_g, band_peer(dx, dh)), device_id_type=MESH
        )
        peers += 1
    for step in (1, -1, 2, -2):
        pl.semaphore_signal(
            barrier, inc=1, device_id=(grid_peer(step), me_b), device_id_type=MESH
        )
        peers += 1
    for peer in [y_peer(dh, dy) for dh, dy in y_offsets] + [
        z_peer(dz, dc) for dz, dc in z_offsets
    ]:
        pl.semaphore_signal(barrier, inc=1, device_id=peer, device_id_type=MESH)
        peers += 1

    other_x = (my_x + max(nx // 4, 1) * (1 - 2 * my_c) + nx) % nx
    pl.semaphore_signal(
        barrier,
        inc=1,
        device_id=(grid_peer(1), other_x * 2 + my_h),
        device_id_type=MESH,
    )
    peers += 1

    pot_loads = [
        pltpu.make_async_copy(pot_in, pot.at[pl.ds(4 * b, 4), :], in_sem.at[4 + b])
        for b in range(2)
    ]
    small_loads = pot_loads + [
        pltpu.make_async_copy(energy_in, energy, in_sem.at[6]),
        pltpu.make_async_copy(count_in, count, in_sem.at[7]),
    ]
    for copy in small_loads:
        copy.start()

    def table_copy(i):
        return pltpu.make_async_copy(
            table_in.at[i], table.at[pl.ds(pl.multiple_of(4 * i, 4), 4), :], table_sem.at[i]
        )

    @pl.loop(0, 48)
    def _(i):
        table_copy(i).start()

    psi[:, 0:PAD] = jnp.zeros((16, PAD), jnp.float32)
    psi[:, PAD + cells : PAD + cells + PAD] = jnp.zeros((16, PAD), jnp.float32)

    @pl.when((me_b != extras[0][1]) & (me_b != extras[1][1]))
    def _():
        got_psi[:, share : share + LANES] = jnp.zeros((16 * nb, LANES), jnp.float32)
        got_h[:, share : share + LANES] = jnp.zeros((16 * nb, LANES), jnp.float32)
        got_next[:, share : share + LANES] = jnp.zeros((16 * nb, LANES), jnp.float32)

    @pl.when(me_b != root)
    def _():
        owners[...] = jnp.zeros(owners.shape, jnp.float32)


    _, lane = iota(8, CHUNK)
    turn = jnp.zeros((8, CHUNK), jnp.int32)
    for m in range(1, CHUNK // NY):
        turn = turn + jnp.where(lane >= m * NY, 1, 0)
    column = lane - turn * NY
    for k in range(1, 5):
        ycoef[k - 1] = jnp.where(column + k < NY, -0.5 * STENCIL[k], 0.0)
        ycoef[3 + k] = jnp.where(column >= k, -0.5 * STENCIL[k], 0.0)

    for copy in loads:
        copy.wait()
    pl.semaphore_wait(barrier, peers)

    my_rows = pl.ds(pl.multiple_of(me_b * 16, 16), 16)

    def spread(source, base, target, send, recv, which):
        copies = []
        for i, (dx, dh) in enumerate(band_offsets):
            peer = band_peer(dx, dh)
            start = pl.multiple_of(base + peer * share, LANES)
            copy = pltpu.make_async_remote_copy(
                src_ref=source.at[:, pl.ds(start, share)],
                dst_ref=target.at[my_rows, pl.ds(0, share)],
                send_sem=send.at[i],
                recv_sem=recv.at[i],
                device_id=(me_g, peer),
                device_id_type=MESH,
            )
            copy.start()
            copies.append(copy)
        for i, (tile, owner) in enumerate(extras):

            @pl.when(me_b != owner)
            def _(i=i, tile=tile, owner=owner):
                extra_copy(source, base, target, which, i, tile, owner, me_b).start()

        return copies

    def extra_copy(source, base, target, which, i, tile, owner, sem):
        return pltpu.make_async_remote_copy(
            src_ref=source.at[:, pl.ds(base + tile * LANES, LANES)],
            dst_ref=target.at[my_rows, pl.ds(share, LANES)],
            send_sem=extra_send.at[which * 2 + i],
            recv_sem=extra_recv.at[which * 16 + sem],
            device_id=(me_g, owner),
            device_id_type=MESH,
        )

    def keep_own(source, base, target):
        start = pl.multiple_of(base + me_b * share, LANES)
        target[my_rows, 0:share] = source[:, pl.ds(start, share)]
        for tile, owner in extras:

            @pl.when(me_b == owner)
            def _(tile=tile):
                target[my_rows, share : share + LANES] = source[
                    :, base + tile * LANES : base + (tile + 1) * LANES
                ]

    def await_spread(copies, source, base, target, which):
        for copy in copies:
            copy.wait_recv()
        for i, (tile, owner) in enumerate(extras):

            @pl.when(me_b == owner)
            def _(i=i, tile=tile, owner=owner):
                for other in range(nb):

                    @pl.when(other != owner)
                    def _(other=other):
                        extra_copy(
                            source, base, target, which, i, tile, owner, other
                        ).wait_recv()

    def await_sent(copies, source, base, target, which):
        for copy in copies:
            copy.wait_send()
        for i, (tile, owner) in enumerate(extras):

            @pl.when(me_b != owner)
            def _(i=i, tile=tile, owner=owner):
                extra_copy(source, base, target, which, i, tile, owner, me_b).wait_send()

    psi_copies = spread(psi, PAD, got_psi, psi_send, psi_recv, 0)

    for copy in small_loads:
        copy.wait()

    @pl.loop(0, 48)
    def _(i):
        table_copy(i).wait()

    def partial_step(i, total):
        start = pl.multiple_of(i * WIDE, LANES)
        return total + dot(
            table[:, pl.ds(start, WIDE)], psi[:, pl.ds(start + PAD, WIDE)], NT
        )

    raw = lax.fori_loop(0, cells // WIDE, partial_step, jnp.zeros((192, 16), jnp.float32))
    row, col = iota(192, 16)
    raw = jnp.where((row & 3) == (col & 3), raw, 0.0)
    row, col = iota(64, 192)
    source_row = jnp.where(row < 32, row, jnp.where(row < 48, -1, row - 16))
    gather = ones_where(source_row == (col >> 2))
    row, col = iota(16, LANES)
    widen = ones_where((row >> 2) == (col >> 2))
    sums = dot(dot(gather, raw, NN), widen, NN)
    part[...] = sums
    row, col = iota(16, 8)
    kinds = jnp.concatenate(
        [jnp.broadcast_to(energy[0, a : a + 1, :], (8, 8)) for a in range(2)], axis=0
    )
    active = jnp.concatenate(
        [jnp.broadcast_to(count[0:1, a : a + 1], (8, 8)) for a in range(2)], axis=0
    )
    chosen = jnp.where((col == (row & 7)) & (col < active), kinds, 0.0)
    weight = jnp.broadcast_to(jnp.sum(chosen, axis=1, keepdims=True), (16, LANES))
    part[32:48, :] = weight

    part_copies = []
    for i, (step, first, count, target) in enumerate(
        ((1, 16, 48, low1), (-1, 0, 48, high1), (2, 48, 16, low2), (-2, 0, 16, high2))
    ):
        copy = pltpu.make_async_remote_copy(
            src_ref=part.at[pl.ds(first, count), :],
            dst_ref=target,
            send_sem=part_send.at[i],
            recv_sem=part_recv.at[i],
            device_id=(grid_peer(step), me_b),
            device_id_type=MESH,
        )
        copy.start()
        part_copies.append(copy)

    @pl.loop(0, cells // CHUNK)
    def _(i):
        start = pl.multiple_of(i * CHUNK, LANES)
        wide = psi[:, pl.ds(start, CHUNK + 2 * PAD)]

        def shifted(offset):
            return wide[:, PAD + offset : PAD + offset + CHUNK]

        here = pot[:, pl.ds(start, CHUNK)] + (-1.5 * STENCIL[0])
        total = jnp.concatenate([here, here], axis=0) * shifted(0)
        for k in range(1, 5):
            total = total + (-0.5 * STENCIL[k]) * (shifted(NY * k) + shifted(-NY * k))
            up, down = ycoef[k - 1], ycoef[3 + k]
            total = total + jnp.concatenate([up, up], axis=0) * shifted(k)
            total = total + jnp.concatenate([down, down], axis=0) * shifted(-k)
        h[:, pl.ds(start, CHUNK)] = total

    h_copies = spread(h, 0, got_h, h_send, h_recv, 1)
    keep_own(h, 0, got_h)

    keep_own(psi, PAD, got_psi)

    for copy in part_copies:
        copy.wait_recv()
    total = part[16:32, :] + high1[0:16, :] + low1[32:48, :]
    coef = jnp.concatenate(
        [
            low1[16:32, :] * (low1[0:16, :] + part[0:16, :] + low2[...]),
            weight * total,
            high1[32:48, :] * (high1[16:32, :] + high2[...] + part[48:64, :]),
        ],
        axis=0,
    )

    row, col = iota(LANES, LANES)
    place = ones_where((row < 16) & ((row & 3) == 0) & (col == me_b * 4 + (row >> 2)))
    owner[...] = dot(total, place, NN)

    def owner_copy(sem):
        return pltpu.make_async_remote_copy(
            src_ref=owner,
            dst_ref=owners.at[me_b],
            send_sem=owner_send,
            recv_sem=owner_recv.at[sem],
            device_id=(me_g, root),
            device_id_type=MESH,
        )

    @pl.when(me_b != root)
    def _():
        owner_copy(me_b).start()

    @pl.when(me_b == root)
    def _():
        owners[me_b] = owner[...]

    await_spread(psi_copies, psi, PAD, got_psi, 0)

    def next_copy(first, width, sem, target):
        return pltpu.make_async_remote_copy(
            src_ref=got_psi.at[:, pl.ds(first, width)],
            dst_ref=got_next.at[:, pl.ds(first, width)],
            send_sem=next_send.at[sem],
            recv_sem=next_recv.at[sem],
            device_id=(grid_peer(-1), target),
            device_id_type=MESH,
        )

    def each_extra(act):
        for _, owner in extras:

            @pl.when(me_b == owner)
            def _():
                act(next_copy(share, LANES, 1, other_x * 2 + my_h))

    next_copy(0, share, 0, me_b).start()
    each_extra(lambda copy: copy.start())

    row, col = iota(48, 192)
    repeat = ones_where(row == (col >> 2))
    spread_coef = dot(coef, repeat, TN)[0:16, :]
    row, col = iota(16, 192)
    spread_coef = jnp.where((row & 3) == (col & 3), spread_coef, 0.0)

    rows = 16 * nb
    row, col = iota(8 * nb, rows)
    band_of = (row >> 3) * 4 + (row & 3)
    pick_corr = ones_where(((row & 4) == 0) & (band_of == (col >> 2)))
    pick_gram = ones_where(((row & 4) == 4) & (band_of == (col >> 2)))
    row, col = iota(8 * nb, LANES)
    band_of = (row >> 3) * 4 + (row & 3)
    pick_nonlocal = ones_where(((row & 4) == 4) & (band_of == col))
    row, col = iota(rows, LANES)
    narrow = ones_where((row >> 2) == col)
    row, col = iota(rows, rows)
    same_plane = (row & 3) == (col & 3)
    apart = jnp.abs((row & 3) - (col & 3))
    above = (col & 3) + 4 - (row & 3)

    def coupled(distance):
        value = jnp.zeros((rows, rows), jnp.float32)
        for k in range(1, 5):
            value = jnp.where(distance == k, -0.5 * STENCIL[k], value)
        return value

    bands = got_psi[...]
    pairs = dot(bands, bands, NT)
    corr = jnp.where(same_plane, pairs, 0.0)
    early = dot(dot(pick_corr, corr, NN), narrow, NN)
    across_gram = coupled(apart) * pairs
    await_spread(h_copies, h, 0, got_h, 1)
    gram = jnp.where(same_plane, dot(got_h[...], bands, NT), 0.0) + across_gram
    early = early + dot(dot(pick_gram, gram, NN), narrow, NN)
    halo = []
    for i, (step, target) in enumerate(((1, before), (-1, after))):
        copy = pltpu.make_async_remote_copy(
            src_ref=psi.at[:, pl.ds(PAD, cells)],
            dst_ref=target,
            send_sem=halo_send.at[i],
            recv_sem=halo_recv.at[i],
            device_id=(grid_peer(step), me_b),
            device_id_type=MESH,
        )
        copy.start()
        halo.append(copy)

    next_copy(0, share, 0, me_b).wait_recv()
    each_extra(lambda copy: copy.wait_recv())

    following = got_next[...]
    crossing = dot(coupled(above) * dot(bands, following, NT), narrow, NN)
    crossing = dot(narrow, crossing, TN)
    @pl.when(me_b == root)
    def _():
        for other in range(nb):

            @pl.when(other != me_b)
            def _(other=other):
                owner_copy(other).wait_recv()

    projections = jnp.sum(owners[...], axis=0)
    nonlocal_gram = dot(projections * weight, projections, TN)

    blocks = early + dot(pick_nonlocal, nonlocal_gram + crossing, NN)
    blocks = blocks + dot(pick_nonlocal, crossing, NT)
    terms[...] = blocks.reshape(nb, 8, LANES)

    def exchange(source_of, target, slot, peers_, send, recv):
        copies = []
        for i, peer in enumerate(peers_):
            copy = pltpu.make_async_remote_copy(
                src_ref=source_of(i),
                dst_ref=target.at[slot],
                send_sem=send.at[i],
                recv_sem=recv.at[i],
                device_id=peer,
                device_id_type=MESH,
            )
            copy.start()
            copies.append(copy)
        return copies

    x_copies = exchange(
        lambda i: terms.at[pl.ds(((my_x + x_offsets[i]) % nx) * 2, 2)],
        x_terms,
        my_x,
        [(me_g, band_peer(dx, 0)) for dx in x_offsets],
        x_send,
        x_recv,
    )
    x_terms[my_x] = terms[pl.ds(my_x * 2, 2)]
    for copy in x_copies:
        copy.wait_recv()
    x_sum[...] = jnp.sum(x_terms[...], axis=0)

    slot = my_h * ny + my_y
    y_copies = exchange(
        lambda i: x_sum.at[(my_h + y_offsets[i][0]) % 2],
        y_terms,
        slot,
        [y_peer(dh, dy) for dh, dy in y_offsets],
        y_send,
        y_recv,
    )
    y_terms[slot] = x_sum[my_h]

    for copy in y_copies:
        copy.wait_recv()
    y_sum[...] = jnp.sum(y_terms[...], axis=0)

    slot = my_z * 2 + my_c
    z_copies = exchange(
        lambda i: y_sum,
        z_terms,
        slot,
        [z_peer(dz, dc) for dz, dc in z_offsets],
        z_send,
        z_recv,
    )
    z_terms[slot] = y_sum[...]

    for copy in halo:
        copy.wait_recv()
    left = jnp.concatenate([spread_coef, z_matrix()], axis=1)

    @pl.loop(0, cells // WIDE)
    def _(i):
        start = pl.multiple_of(i * WIDE, LANES)
        here = pl.ds(start, WIDE)
        right = jnp.concatenate(
            [table[:, here], before[:, here], psi[:, pl.ds(start + PAD, WIDE)], after[:, here]],
            axis=0,
        )
        full[:, here] = h[:, here] + dot(left, right, NN)

    stores = [
        pltpu.make_async_copy(full.at[pl.ds(4 * b, 4), :], h_out.at[b], out_sem.at[b])
        for b in range(4)
    ]
    for copy in stores:
        copy.start()

    for copy in z_copies:
        copy.wait_recv()
    sums_out[...] = jnp.sum(z_terms[...], axis=0) * (1.0 / (4 * cells * ng))

    for copy in halo + part_copies + x_copies + y_copies + z_copies:
        copy.wait_send()
    await_sent(psi_copies, psi, PAD, got_psi, 0)
    await_sent(h_copies, h, 0, got_h, 1)

    next_copy(0, share, 0, me_b).wait_send()
    each_extra(lambda copy: copy.wait_send())

    @pl.when(me_b != root)
    def _():
        owner_copy(me_b).wait_send()

    for copy in stores:
        copy.wait()


def finish(h_in, sums_in, h_out, corr_out, gram_out, held, sums, corr, gram, sem):
    ins = [pltpu.make_async_copy(h_in.at[b], held.at[b], sem.at[b]) for b in range(4)]
    outs = [pltpu.make_async_copy(held.at[b], h_out.at[b], sem.at[4 + b]) for b in range(4)]
    sums_copy = pltpu.make_async_copy(sums_in, sums, sem.at[8])
    outs.append(pltpu.make_async_copy(corr, corr_out, sem.at[9]))
    outs.append(pltpu.make_async_copy(gram, gram_out, sem.at[10]))
    sums_copy.start()
    for copy in ins:
        copy.start()
    width = corr_out.shape[1]
    sums_copy.wait()
    corr[...] = sums[0:4, 0:width]
    gram[...] = sums[4:8, 0:width]
    for copy in ins:
        copy.wait()
    for copy in outs:
        copy.start()
    for copy in outs:
        copy.wait()


def shards(dims, orbitals, potential, projectors, kb_energy, proj_count):
    groups, layers, cells = orbitals.shape
    nx, ny, nz = dims
    nb = nx * 2
    kinds = projectors.shape[2]
    width = ((cells // LANES) // nb + 1) * LANES
    f32 = jnp.float32
    any_space = pl.BlockSpec(memory_space=pl.ANY)
    vmem = pl.BlockSpec(memory_space=pltpu.VMEM)
    dma = pltpu.SemaphoreType.DMA
    full, sums = pl.pallas_call(
        functools.partial(kernel, dims),
        out_shape=(
            jax.ShapeDtypeStruct(orbitals.shape, f32),
            jax.ShapeDtypeStruct((8, LANES), f32),
        ),
        in_specs=[any_space] * 5,
        out_specs=(any_space, vmem),
        scratch_shapes=[
            pltpu.VMEM((16, cells + 2 * PAD), f32),
            pltpu.VMEM((16, cells), f32),
            pltpu.VMEM((16, cells), f32),
            pltpu.VMEM((8, cells), f32),
            pltpu.VMEM((192, cells), f32),
            pltpu.VMEM(kb_energy.shape, f32),
            pltpu.VMEM(proj_count.shape, jnp.int32),
            pltpu.VMEM((16, cells), f32),
            pltpu.VMEM((16, cells), f32),
            pltpu.VMEM((16 * nb, width), f32),
            pltpu.VMEM((16 * nb, width), f32),
            pltpu.VMEM((16 * nb, width), f32),
            pltpu.VMEM((8, 8, CHUNK), f32),
            pltpu.VMEM((64, LANES), f32),
            pltpu.VMEM((48, LANES), f32),
            pltpu.VMEM((48, LANES), f32),
            pltpu.VMEM((16, LANES), f32),
            pltpu.VMEM((16, LANES), f32),
            pltpu.VMEM((16, LANES), f32),
            pltpu.VMEM((nb, 16, LANES), f32),
            pltpu.VMEM((nb, 8, LANES), f32),
            pltpu.VMEM((nx, 2, 8, LANES), f32),
            pltpu.VMEM((2, 8, LANES), f32),
            pltpu.VMEM((ny * 2, 8, LANES), f32),
            pltpu.VMEM((8, LANES), f32),
            pltpu.VMEM((nz * 2, 8, LANES), f32),
            dma((8,)),
            dma((48,)),
            dma((2,)),
            dma((2,)),
            dma((4,)),
            dma((4,)),
            dma((nb,)),
            dma((nb,)),
            dma((nb,)),
            dma((nb,)),
            dma((4,)),
            dma((32,)),
            dma((2,)),
            dma((2,)),
            dma,
            dma((nb,)),
            dma((4,)),
            dma((nx,)),
            dma((nx,)),
            dma((ny * 2,)),
            dma((ny * 2,)),
            dma((nz * 2,)),
            dma((nz * 2,)),
        ],
        compiler_params=pltpu.CompilerParams(
            collective_id=0, has_side_effects=True, vmem_limit_bytes=60 * 2**20
        ),
        cost_estimate=pl.CostEstimate(
            flops=80_000_000, bytes_accessed=6_000_000, transcendentals=0
        ),
    )(
        orbitals,
        potential,
        projectors.reshape(3 * 2 * kinds, layers, cells),
        kb_energy,
        proj_count,
    )
    return pl.pallas_call(
        finish,
        out_shape=(
            jax.ShapeDtypeStruct(orbitals.shape, f32),
            jax.ShapeDtypeStruct((groups, groups * nb), f32),
            jax.ShapeDtypeStruct((groups, groups * nb), f32),
        ),
        in_specs=[any_space, any_space],
        out_specs=(any_space, any_space, any_space),
        scratch_shapes=[
            pltpu.VMEM(orbitals.shape, f32),
            pltpu.VMEM((8, LANES), f32),
            pltpu.VMEM((groups, groups * nb), f32),
            pltpu.VMEM((groups, groups * nb), f32),
            dma((11,)),
        ],
        compiler_params=pltpu.CompilerParams(vmem_limit_bytes=60 * 2**20),
        cost_estimate=pl.CostEstimate(flops=0, bytes_accessed=900_000, transcendentals=0),
    )(full, sums)


def solution(mesh):
    ny = 4 if mesh.shape["grid"] == 64 else 1
    dims = (mesh.shape["band"] // 2, ny, mesh.shape["grid"] // (2 * ny))
    in_specs = (
        P("band", "grid", None),
        P("grid", None),
        P(None, None, None, "grid", None),
        P("grid", None, None),
        P("grid", None),
    )
    out_specs = (P("band", "grid", None), P("band", None), P("band", None))
    return jax.shard_map(
        functools.partial(shards, dims),
        mesh=mesh,
        in_specs=in_specs,
        out_specs=out_specs,
        check_vma=False,
    )
```

```python
import functools

import jax
import jax.numpy as jnp
from jax import lax
from jax.experimental import pallas as pl
from jax.experimental.pallas import tpu as pltpu
from jax.sharding import PartitionSpec as P

NY = 80
STENCIL = (-205.0 / 72.0, 8.0 / 5.0, -1.0 / 5.0, 8.0 / 315.0, -1.0 / 560.0)
MESH = pl.DeviceIdType.MESH
LANES = 128
PAD = 384
CHUNK = 640
WIDE = 1280


def iota(rows, cols):
    return (
        lax.broadcasted_iota(jnp.int32, (rows, cols), 0),
        lax.broadcasted_iota(jnp.int32, (rows, cols), 1),
    )


def ones_where(condition):
    return jnp.where(condition, 1.0, 0.0).astype(jnp.float32)


def dot(a, b, dims):
    return lax.dot_general(
        a,
        b,
        (dims, ((), ())),
        precision=lax.Precision.HIGHEST,
        preferred_element_type=jnp.float32,
    )


NN = ((1,), (0,))
NT = ((1,), (1,))
TN = ((0,), (0,))


def z_matrix():
    row, col = iota(16, 48)
    same = ((row >> 2) & 3) == ((col >> 2) & 3)
    diff = (col >> 4) * 4 + (col & 3) - 4 - (row & 3)
    dist = jnp.abs(diff)
    value = jnp.zeros((16, 48), jnp.float32)
    for k in range(1, 5):
        value = jnp.where(dist == k, -0.5 * STENCIL[k], value)
    return jnp.where(same, value, 0.0)


def kernel(
    dims,
    psi_in,
    pot_in,
    table_in,
    energy_in,
    count_in,
    h_out,
    sums_out,
    psi,
    before,
    after,
    pot,
    table,
    energy,
    count,
    h,
    full,
    got_psi,
    got_h,
    got_next,
    ycoef,
    part,
    low1,
    high1,
    low2,
    high2,
    owner,
    owners,
    terms,
    x_terms,
    x_sum,
    y_terms,
    y_sum,
    z_terms,
    in_sem,
    table_sem,
    halo_send,
    halo_recv,
    part_send,
    part_recv,
    psi_send,
    psi_recv,
    h_send,
    h_recv,
    extra_send,
    extra_recv,
    next_send,
    next_recv,
    owner_send,
    owner_recv,
    out_sem,
    x_send,
    x_recv,
    y_send,
    y_recv,
    z_send,
    z_recv,
):
    nx, ny, nz = dims
    nb, ng = nx * 2, ny * nz * 2
    cells = pot_in.shape[1]
    per = (cells // LANES) // nb
    share = per * LANES
    me_g = lax.axis_index("grid")
    me_b = lax.axis_index("band")
    my_x, my_h = me_b // 2, me_b % 2
    my_c, my_z, my_y = me_g % 2, (me_g // 2) % nz, me_g // (2 * nz)

    def extra_owner(i, core):
        return ((i * (nx // 2) + core * max(nx // 4, 1)) % nx) * 2 + i

    extras = [(per * nb + i, extra_owner(i, my_c)) for i in range(cells // LANES - per * nb)]
    far_x = sorted(range(nx), key=lambda dx: -min(dx, nx - dx))
    far_z = sorted(range(nz), key=lambda dz: -min(dz, nz - dz))
    band_offsets = [(dx, dh) for dh in (1, 0) for dx in far_x if (dx, dh) != (0, 0)]
    x_offsets = [dx for dx in far_x if dx]
    y_offsets = [(dh, dy) for dh in (1, 0) for dy in range(ny) if (dh, dy) != (0, 0)]
    z_offsets = [(dz, dc) for dz in far_z for dc in (1, 0) if (dz, dc) != (0, 0)]
    root = me_g % nb

    def band_peer(dx, dh):
        return ((my_x + dx) % nx) * 2 + (my_h + dh) % 2

    def y_peer(dh, dy):
        peer_g = (((my_y + dy) % ny) * nz + my_z) * 2 + my_c
        return peer_g, my_x * 2 + (my_h + dh) % 2

    def z_peer(dz, dc):
        return (my_y * nz + (my_z + dz) % nz) * 2 + (my_c + dc) % 2, me_b

    def grid_peer(step):
        return (me_g + step + ng) % ng

    loads = [
        pltpu.make_async_copy(
            psi_in.at[b], psi.at[pl.ds(4 * b, 4), pl.ds(PAD, cells)], in_sem.at[b]
        )
        for b in range(4)
    ]
    for copy in loads:
        copy.start()

    barrier = pltpu.get_barrier_semaphore()
    peers = 0
    for dx, dh in band_offsets:
        pl.semaphore_signal(
            barrier, inc=1, device_id=(me_g, band_peer(dx, dh)), device_id_type=MESH
        )
        peers += 1
    for step in (1, -1, 2, -2):
        pl.semaphore_signal(
            barrier, inc=1, device_id=(grid_peer(step), me_b), device_id_type=MESH
        )
        peers += 1
    for peer in [y_peer(dh, dy) for dh, dy in y_offsets] + [
        z_peer(dz, dc) for dz, dc in z_offsets
    ]:
        pl.semaphore_signal(barrier, inc=1, device_id=peer, device_id_type=MESH)
        peers += 1

    other_x = (my_x + max(nx // 4, 1) * (1 - 2 * my_c) + nx) % nx
    pl.semaphore_signal(
        barrier,
        inc=1,
        device_id=(grid_peer(1), other_x * 2 + my_h),
        device_id_type=MESH,
    )
    peers += 1

    pot_loads = [
        pltpu.make_async_copy(pot_in, pot.at[pl.ds(4 * b, 4), :], in_sem.at[4 + b])
        for b in range(2)
    ]
    small_loads = pot_loads + [
        pltpu.make_async_copy(energy_in, energy, in_sem.at[6]),
        pltpu.make_async_copy(count_in, count, in_sem.at[7]),
    ]
    for copy in small_loads:
        copy.start()

    def table_copy(i):
        return pltpu.make_async_copy(
            table_in.at[i], table.at[pl.ds(pl.multiple_of(4 * i, 4), 4), :], table_sem.at[i]
        )

    @pl.loop(0, 48)
    def _(i):
        table_copy(i).start()

    psi[:, 0:PAD] = jnp.zeros((16, PAD), jnp.float32)
    psi[:, PAD + cells : PAD + cells + PAD] = jnp.zeros((16, PAD), jnp.float32)

    @pl.when((me_b != extras[0][1]) & (me_b != extras[1][1]))
    def _():
        got_psi[:, share : share + LANES] = jnp.zeros((16 * nb, LANES), jnp.float32)
        got_h[:, share : share + LANES] = jnp.zeros((16 * nb, LANES), jnp.float32)
        got_next[:, share : share + LANES] = jnp.zeros((16 * nb, LANES), jnp.float32)

    @pl.when(me_b != root)
    def _():
        owners[...] = jnp.zeros(owners.shape, jnp.float32)


    _, lane = iota(8, CHUNK)
    turn = jnp.zeros((8, CHUNK), jnp.int32)
    for m in range(1, CHUNK // NY):
        turn = turn + jnp.where(lane >= m * NY, 1, 0)
    column = lane - turn * NY
    for k in range(1, 5):
        ycoef[k - 1] = jnp.where(column + k < NY, -0.5 * STENCIL[k], 0.0)
        ycoef[3 + k] = jnp.where(column >= k, -0.5 * STENCIL[k], 0.0)

    for copy in loads:
        copy.wait()
    pl.semaphore_wait(barrier, peers)

    my_rows = pl.ds(pl.multiple_of(me_b * 16, 16), 16)

    def spread(source, base, target, send, recv, which):
        copies = []
        for i, (dx, dh) in enumerate(band_offsets):
            peer = band_peer(dx, dh)
            start = pl.multiple_of(base + peer * share, LANES)
            copy = pltpu.make_async_remote_copy(
                src_ref=source.at[:, pl.ds(start, share)],
                dst_ref=target.at[my_rows, pl.ds(0, share)],
                send_sem=send.at[i],
                recv_sem=recv.at[i],
                device_id=(me_g, peer),
                device_id_type=MESH,
            )
            copy.start()
            copies.append(copy)
        for i, (tile, owner) in enumerate(extras):

            @pl.when(me_b != owner)
            def _(i=i, tile=tile, owner=owner):
                extra_copy(source, base, target, which, i, tile, owner, me_b).start()

        return copies

    def extra_copy(source, base, target, which, i, tile, owner, sem):
        return pltpu.make_async_remote_copy(
            src_ref=source.at[:, pl.ds(base + tile * LANES, LANES)],
            dst_ref=target.at[my_rows, pl.ds(share, LANES)],
            send_sem=extra_send.at[which * 2 + i],
            recv_sem=extra_recv.at[which * 16 + sem],
            device_id=(me_g, owner),
            device_id_type=MESH,
        )

    def keep_own(source, base, target):
        start = pl.multiple_of(base + me_b * share, LANES)
        target[my_rows, 0:share] = source[:, pl.ds(start, share)]
        for tile, owner in extras:

            @pl.when(me_b == owner)
            def _(tile=tile):
                target[my_rows, share : share + LANES] = source[
                    :, base + tile * LANES : base + (tile + 1) * LANES
                ]

    def await_spread(copies, source, base, target, which):
        for copy in copies:
            copy.wait_recv()
        for i, (tile, owner) in enumerate(extras):

            @pl.when(me_b == owner)
            def _(i=i, tile=tile, owner=owner):
                for other in range(nb):

                    @pl.when(other != owner)
                    def _(other=other):
                        extra_copy(
                            source, base, target, which, i, tile, owner, other
                        ).wait_recv()

    def await_sent(copies, source, base, target, which):
        for copy in copies:
            copy.wait_send()
        for i, (tile, owner) in enumerate(extras):

            @pl.when(me_b != owner)
            def _(i=i, tile=tile, owner=owner):
                extra_copy(source, base, target, which, i, tile, owner, me_b).wait_send()

    psi_copies = spread(psi, PAD, got_psi, psi_send, psi_recv, 0)

    for copy in small_loads:
        copy.wait()

    @pl.loop(0, 48)
    def _(i):
        table_copy(i).wait()

    def partial_step(i, total):
        start = pl.multiple_of(i * WIDE, LANES)
        return total + dot(
            table[:, pl.ds(start, WIDE)], psi[:, pl.ds(start + PAD, WIDE)], NT
        )

    raw = lax.fori_loop(0, cells // WIDE, partial_step, jnp.zeros((192, 16), jnp.float32))
    row, col = iota(192, 16)
    raw = jnp.where((row & 3) == (col & 3), raw, 0.0)
    row, col = iota(64, 192)
    source_row = jnp.where(row < 32, row, jnp.where(row < 48, -1, row - 16))
    gather = ones_where(source_row == (col >> 2))
    row, col = iota(16, LANES)
    widen = ones_where((row >> 2) == (col >> 2))
    sums = dot(dot(gather, raw, NN), widen, NN)
    part[...] = sums
    row, col = iota(16, 8)
    kinds = jnp.concatenate(
        [jnp.broadcast_to(energy[0, a : a + 1, :], (8, 8)) for a in range(2)], axis=0
    )
    active = jnp.concatenate(
        [jnp.broadcast_to(count[0:1, a : a + 1], (8, 8)) for a in range(2)], axis=0
    )
    chosen = jnp.where((col == (row & 7)) & (col < active), kinds, 0.0)
    weight = jnp.broadcast_to(jnp.sum(chosen, axis=1, keepdims=True), (16, LANES))
    part[32:48, :] = weight

    part_copies = []
    for i, (step, first, count, target) in enumerate(
        ((1, 16, 48, low1), (-1, 0, 48, high1), (2, 48, 16, low2), (-2, 0, 16, high2))
    ):
        copy = pltpu.make_async_remote_copy(
            src_ref=part.at[pl.ds(first, count), :],
            dst_ref=target,
            send_sem=part_send.at[i],
            recv_sem=part_recv.at[i],
            device_id=(grid_peer(step), me_b),
            device_id_type=MESH,
        )
        copy.start()
        part_copies.append(copy)

    @pl.loop(0, cells // CHUNK)
    def _(i):
        start = pl.multiple_of(i * CHUNK, LANES)
        wide = psi[:, pl.ds(start, CHUNK + 2 * PAD)]

        def shifted(offset):
            return wide[:, PAD + offset : PAD + offset + CHUNK]

        here = pot[:, pl.ds(start, CHUNK)] + (-1.5 * STENCIL[0])
        total = jnp.concatenate([here, here], axis=0) * shifted(0)
        for k in range(1, 5):
            total = total + (-0.5 * STENCIL[k]) * (shifted(NY * k) + shifted(-NY * k))
            up, down = ycoef[k - 1], ycoef[3 + k]
            total = total + jnp.concatenate([up, up], axis=0) * shifted(k)
            total = total + jnp.concatenate([down, down], axis=0) * shifted(-k)
        h[:, pl.ds(start, CHUNK)] = total

    h_copies = spread(h, 0, got_h, h_send, h_recv, 1)
    keep_own(h, 0, got_h)

    keep_own(psi, PAD, got_psi)

    await_spread(psi_copies, psi, PAD, got_psi, 0)

    def next_copy(first, width, sem, target):
        return pltpu.make_async_remote_copy(
            src_ref=got_psi.at[:, pl.ds(first, width)],
            dst_ref=got_next.at[:, pl.ds(first, width)],
            send_sem=next_send.at[sem],
            recv_sem=next_recv.at[sem],
            device_id=(grid_peer(-1), target),
            device_id_type=MESH,
        )

    def each_extra(act):
        for _, owner in extras:

            @pl.when(me_b == owner)
            def _():
                act(next_copy(share, LANES, 1, other_x * 2 + my_h))

    next_copy(0, share, 0, me_b).start()
    each_extra(lambda copy: copy.start())

    halo = []
    for i, (step, target) in enumerate(((1, before), (-1, after))):
        copy = pltpu.make_async_remote_copy(
            src_ref=psi.at[:, pl.ds(PAD, cells)],
            dst_ref=target,
            send_sem=halo_send.at[i],
            recv_sem=halo_recv.at[i],
            device_id=(grid_peer(step), me_b),
            device_id_type=MESH,
        )
        halo.append(copy)
    halo[0].start()

    for copy in part_copies:
        copy.wait_recv()
    total = part[16:32, :] + high1[0:16, :] + low1[32:48, :]
    coef = jnp.concatenate(
        [
            low1[16:32, :] * (low1[0:16, :] + part[0:16, :] + low2[...]),
            weight * total,
            high1[32:48, :] * (high1[16:32, :] + high2[...] + part[48:64, :]),
        ],
        axis=0,
    )

    row, col = iota(LANES, LANES)
    place = ones_where((row < 16) & ((row & 3) == 0) & (col == me_b * 4 + (row >> 2)))
    owner[...] = dot(total, place, NN)

    def owner_copy(sem):
        return pltpu.make_async_remote_copy(
            src_ref=owner,
            dst_ref=owners.at[me_b],
            send_sem=owner_send,
            recv_sem=owner_recv.at[sem],
            device_id=(me_g, root),
            device_id_type=MESH,
        )

    @pl.when(me_b != root)
    def _():
        owner_copy(me_b).start()

    @pl.when(me_b == root)
    def _():
        owners[me_b] = owner[...]

    row, col = iota(48, 192)
    repeat = ones_where(row == (col >> 2))
    spread_coef = dot(coef, repeat, TN)[0:16, :]
    row, col = iota(16, 192)
    spread_coef = jnp.where((row & 3) == (col & 3), spread_coef, 0.0)

    rows = 16 * nb
    row, col = iota(8 * nb, rows)
    band_of = (row >> 3) * 4 + (row & 3)
    pick_corr = ones_where(((row & 4) == 0) & (band_of == (col >> 2)))
    pick_gram = ones_where(((row & 4) == 4) & (band_of == (col >> 2)))
    row, col = iota(8 * nb, LANES)
    band_of = (row >> 3) * 4 + (row & 3)
    pick_nonlocal = ones_where(((row & 4) == 4) & (band_of == col))
    row, col = iota(rows, LANES)
    narrow = ones_where((row >> 2) == col)
    row, col = iota(rows, rows)
    same_plane = (row & 3) == (col & 3)
    apart = jnp.abs((row & 3) - (col & 3))
    above = (col & 3) + 4 - (row & 3)

    def coupled(distance):
        value = jnp.zeros((rows, rows), jnp.float32)
        for k in range(1, 5):
            value = jnp.where(distance == k, -0.5 * STENCIL[k], value)
        return value

    bands = got_psi[...]
    pairs = dot(bands, bands, NT)
    corr = jnp.where(same_plane, pairs, 0.0)
    early = dot(dot(pick_corr, corr, NN), narrow, NN)
    across_gram = coupled(apart) * pairs
    await_spread(h_copies, h, 0, got_h, 1)
    gram = jnp.where(same_plane, dot(got_h[...], bands, NT), 0.0) + across_gram
    early = early + dot(dot(pick_gram, gram, NN), narrow, NN)
    halo[1].start()
    next_copy(0, share, 0, me_b).wait_recv()
    each_extra(lambda copy: copy.wait_recv())

    following = got_next[...]
    crossing = dot(coupled(above) * dot(bands, following, NT), narrow, NN)
    crossing = dot(narrow, crossing, TN)
    @pl.when(me_b == root)
    def _():
        for other in range(nb):

            @pl.when(other != me_b)
            def _(other=other):
                owner_copy(other).wait_recv()

    projections = jnp.sum(owners[...], axis=0)
    nonlocal_gram = dot(projections * weight, projections, TN)

    blocks = early + dot(pick_nonlocal, nonlocal_gram + crossing, NN)
    blocks = blocks + dot(pick_nonlocal, crossing, NT)
    terms[...] = blocks.reshape(nb, 8, LANES)

    def exchange(source_of, target, slot, peers_, send, recv):
        copies = []
        for i, peer in enumerate(peers_):
            copy = pltpu.make_async_remote_copy(
                src_ref=source_of(i),
                dst_ref=target.at[slot],
                send_sem=send.at[i],
                recv_sem=recv.at[i],
                device_id=peer,
                device_id_type=MESH,
            )
            copy.start()
            copies.append(copy)
        return copies

    x_copies = exchange(
        lambda i: terms.at[pl.ds(((my_x + x_offsets[i]) % nx) * 2, 2)],
        x_terms,
        my_x,
        [(me_g, band_peer(dx, 0)) for dx in x_offsets],
        x_send,
        x_recv,
    )
    x_terms[my_x] = terms[pl.ds(my_x * 2, 2)]
    for copy in x_copies:
        copy.wait_recv()
    x_sum[...] = jnp.sum(x_terms[...], axis=0)

    slot = my_h * ny + my_y
    y_copies = exchange(
        lambda i: x_sum.at[(my_h + y_offsets[i][0]) % 2],
        y_terms,
        slot,
        [y_peer(dh, dy) for dh, dy in y_offsets],
        y_send,
        y_recv,
    )
    y_terms[slot] = x_sum[my_h]

    for copy in halo:
        copy.wait_recv()
    across = z_matrix()

    @pl.loop(0, cells // WIDE)
    def _(i):
        start = pl.multiple_of(i * WIDE, LANES)
        here = pl.ds(start, WIDE)
        planes = jnp.concatenate(
            [before[:, here], psi[:, pl.ds(start + PAD, WIDE)], after[:, here]], axis=0
        )
        full[:, here] = h[:, here] + dot(across, planes, NN)

    for copy in y_copies:
        copy.wait_recv()
    y_sum[...] = jnp.sum(y_terms[...], axis=0)

    slot = my_z * 2 + my_c
    z_copies = exchange(
        lambda i: y_sum,
        z_terms,
        slot,
        [z_peer(dz, dc) for dz, dc in z_offsets],
        z_send,
        z_recv,
    )
    z_terms[slot] = y_sum[...]

    @pl.loop(0, cells // WIDE)
    def _(i):
        start = pl.multiple_of(i * WIDE, LANES)
        here = pl.ds(start, WIDE)
        full[:, here] = full[:, here] + dot(spread_coef, table[:, here], NN)

    stores = [
        pltpu.make_async_copy(full.at[pl.ds(4 * b, 4), :], h_out.at[b], out_sem.at[b])
        for b in range(4)
    ]
    for copy in stores:
        copy.start()

    for copy in z_copies:
        copy.wait_recv()
    sums_out[...] = jnp.sum(z_terms[...], axis=0) * (1.0 / (4 * cells * ng))

    for copy in halo + part_copies + x_copies + y_copies + z_copies:
        copy.wait_send()
    await_sent(psi_copies, psi, PAD, got_psi, 0)
    await_sent(h_copies, h, 0, got_h, 1)

    next_copy(0, share, 0, me_b).wait_send()
    each_extra(lambda copy: copy.wait_send())

    @pl.when(me_b != root)
    def _():
        owner_copy(me_b).wait_send()

    for copy in stores:
        copy.wait()


def finish(h_in, sums_in, h_out, corr_out, gram_out, held, sums, corr, gram, sem):
    ins = [pltpu.make_async_copy(h_in.at[b], held.at[b], sem.at[b]) for b in range(4)]
    outs = [pltpu.make_async_copy(held.at[b], h_out.at[b], sem.at[4 + b]) for b in range(4)]
    sums_copy = pltpu.make_async_copy(sums_in, sums, sem.at[8])
    outs.append(pltpu.make_async_copy(corr, corr_out, sem.at[9]))
    outs.append(pltpu.make_async_copy(gram, gram_out, sem.at[10]))
    sums_copy.start()
    for copy in ins:
        copy.start()
    width = corr_out.shape[1]
    sums_copy.wait()
    corr[...] = sums[0:4, 0:width]
    gram[...] = sums[4:8, 0:width]
    for copy in ins:
        copy.wait()
    for copy in outs:
        copy.start()
    for copy in outs:
        copy.wait()


def shards(dims, orbitals, potential, projectors, kb_energy, proj_count):
    groups, layers, cells = orbitals.shape
    nx, ny, nz = dims
    nb = nx * 2
    kinds = projectors.shape[2]
    width = ((cells // LANES) // nb + 1) * LANES
    f32 = jnp.float32
    any_space = pl.BlockSpec(memory_space=pl.ANY)
    vmem = pl.BlockSpec(memory_space=pltpu.VMEM)
    dma = pltpu.SemaphoreType.DMA
    full, sums = pl.pallas_call(
        functools.partial(kernel, dims),
        out_shape=(
            jax.ShapeDtypeStruct(orbitals.shape, f32),
            jax.ShapeDtypeStruct((8, LANES), f32),
        ),
        in_specs=[any_space] * 5,
        out_specs=(any_space, vmem),
        scratch_shapes=[
            pltpu.VMEM((16, cells + 2 * PAD), f32),
            pltpu.VMEM((16, cells), f32),
            pltpu.VMEM((16, cells), f32),
            pltpu.VMEM((8, cells), f32),
            pltpu.VMEM((192, cells), f32),
            pltpu.VMEM(kb_energy.shape, f32),
            pltpu.VMEM(proj_count.shape, jnp.int32),
            pltpu.VMEM((16, cells), f32),
            pltpu.VMEM((16, cells), f32),
            pltpu.VMEM((16 * nb, width), f32),
            pltpu.VMEM((16 * nb, width), f32),
            pltpu.VMEM((16 * nb, width), f32),
            pltpu.VMEM((8, 8, CHUNK), f32),
            pltpu.VMEM((64, LANES), f32),
            pltpu.VMEM((48, LANES), f32),
            pltpu.VMEM((48, LANES), f32),
            pltpu.VMEM((16, LANES), f32),
            pltpu.VMEM((16, LANES), f32),
            pltpu.VMEM((16, LANES), f32),
            pltpu.VMEM((nb, 16, LANES), f32),
            pltpu.VMEM((nb, 8, LANES), f32),
            pltpu.VMEM((nx, 2, 8, LANES), f32),
            pltpu.VMEM((2, 8, LANES), f32),
            pltpu.VMEM((ny * 2, 8, LANES), f32),
            pltpu.VMEM((8, LANES), f32),
            pltpu.VMEM((nz * 2, 8, LANES), f32),
            dma((8,)),
            dma((48,)),
            dma((2,)),
            dma((2,)),
            dma((4,)),
            dma((4,)),
            dma((nb,)),
            dma((nb,)),
            dma((nb,)),
            dma((nb,)),
            dma((4,)),
            dma((32,)),
            dma((2,)),
            dma((2,)),
            dma,
            dma((nb,)),
            dma((4,)),
            dma((nx,)),
            dma((nx,)),
            dma((ny * 2,)),
            dma((ny * 2,)),
            dma((nz * 2,)),
            dma((nz * 2,)),
        ],
        compiler_params=pltpu.CompilerParams(
            collective_id=0, has_side_effects=True, vmem_limit_bytes=60 * 2**20
        ),
        cost_estimate=pl.CostEstimate(
            flops=80_000_000, bytes_accessed=6_000_000, transcendentals=0
        ),
    )(
        orbitals,
        potential,
        projectors.reshape(3 * 2 * kinds, layers, cells),
        kb_energy,
        proj_count,
    )
    return pl.pallas_call(
        finish,
        out_shape=(
            jax.ShapeDtypeStruct(orbitals.shape, f32),
            jax.ShapeDtypeStruct((groups, groups * nb), f32),
            jax.ShapeDtypeStruct((groups, groups * nb), f32),
        ),
        in_specs=[any_space, any_space],
        out_specs=(any_space, any_space, any_space),
        scratch_shapes=[
            pltpu.VMEM(orbitals.shape, f32),
            pltpu.VMEM((8, LANES), f32),
            pltpu.VMEM((groups, groups * nb), f32),
            pltpu.VMEM((groups, groups * nb), f32),
            dma((11,)),
        ],
        compiler_params=pltpu.CompilerParams(vmem_limit_bytes=60 * 2**20),
        cost_estimate=pl.CostEstimate(flops=0, bytes_accessed=900_000, transcendentals=0),
    )(full, sums)


def solution(mesh):
    ny = 4 if mesh.shape["grid"] == 64 else 1
    dims = (mesh.shape["band"] // 2, ny, mesh.shape["grid"] // (2 * ny))
    in_specs = (
        P("band", "grid", None),
        P("grid", None),
        P(None, None, None, "grid", None),
        P("grid", None, None),
        P("grid", None),
    )
    out_specs = (P("band", "grid", None), P("band", None), P("band", None))
    return jax.shard_map(
        functools.partial(shards, dims),
        mesh=mesh,
        in_specs=in_specs,
        out_specs=out_specs,
        check_vma=False,
    )
```
